32 devices in a mesh: dp: 8 (over y, x, core), fsdp: 4 (over z).
Axes of the slice: x: 2, y: 2, z: 4, core: 2. Of those that a mesh axis runs over, the one named last changes fastest.
Arguments:
- tokens: bfloat16 [4096, 2048], P(('dp', 'fsdp')), may hold values from -6 to 6
- counts: int32 [8, 4], replicated, may hold values from 64 to 128, as said below
- lengths: int32 [8, 3], replicated, may hold values from 1 to 510, as said below
- gain: bfloat16 [2048], P(('dp', 'fsdp')), may hold values from 0.5 to 1.5
- in_weight: bfloat16 [2048, 8192], P(('dp', 'fsdp')), may hold values from -0.125 to 0.125
- conv_weight: bfloat16 [4, 4096], P(None, ('dp', 'fsdp')), may hold values from -3 to 3
- conv_bias: bfloat16 [4096], P(('dp', 'fsdp')), may hold values from -3 to 3
- x_weight: bfloat16 [4096, 160], P(('dp', 'fsdp')), may hold values from -0.09375 to 0.09375
- dt_weight: bfloat16 [128, 4096], P(None, ('dp', 'fsdp')), may hold values from -0.5 to 0.5
- dt_bias: bfloat16 [4096], P(('dp', 'fsdp')), may hold values from -6.875 to -2.296875
- a_log: bfloat16 [4096, 16], P(('dp', 'fsdp')), may hold values from -4.59375 to 2.796875
- skip: bfloat16 [4096], P(('dp', 'fsdp')), may hold values from 0.5 to 1.5
- out_weight: bfloat16 [4096, 2048], P(('dp', 'fsdp')), may hold values from -0.09375 to 0.09375
- cotangent: bfloat16 [4096, 2048], P(('dp', 'fsdp')), may hold values from -6 to 6
Outputs:
- output: bfloat16 [4096, 2048], P(('dp', 'fsdp'))
- token_grad: float32 [4096, 2048], P(('dp', 'fsdp'))
- gain_grad: float32 [2048], P(('dp', 'fsdp'))
- in_weight_grad: float32 [2048, 8192], P(('dp', 'fsdp'))
- conv_weight_grad: float32 [4, 4096], P(None, ('dp', 'fsdp'))
- conv_bias_grad: float32 [4096], P(('dp', 'fsdp'))
- x_weight_grad: float32 [4096, 160], P(('dp', 'fsdp'))
- dt_weight_grad: float32 [128, 4096], P(None, ('dp', 'fsdp'))
- dt_bias_grad: float32 [4096], P(('dp', 'fsdp'))
- a_log_grad: float32 [4096, 16], P(('dp', 'fsdp'))
- skip_grad: float32 [4096], P(('dp', 'fsdp'))
- out_weight_grad: float32 [4096, 2048], P(('dp', 'fsdp'))
The draws below stay inside these ranges and needn't reach their ends.
Inputs may be any that keep to these rules, and one draw needn't show every extreme that they name: `counts`: valid slots of a device; in every group some device holds all 128. `lengths`: they sum to the group's valid tokens. The first document ends on the group's first device and the last begins on its last device, so the middle one runs from the first device to the last; the first and last hold at most a quarter of their device's valid tokens. In one group every slot is valid and the first and last documents have one token each.
All inputs are finite; a program needn't handle non-finite values.
Results may differ from the reference program's by a relative error of at most 0.0076.
Values may be sent and summed in bfloat16 or wider, within the bound.
No kernel may reach another device: no remote copies, remote signals or barrier semaphores. Data moves between devices by JAX's collectives and lax.ppermute only.
A program may use at most 320 MiB of HBM per device.

```python
import jax
import jax.numpy as jnp
from jax import lax

D = 2048
DI = 4096
N = 16
R = 128
KC = 4
TOK_DEV = 128
SPAN = 32
PROJ = 160
GROUP = 512
TOKENS = 4096
N_DP = 8
N_FSDP = 4


def layout(key):
    spread_key, filled_key, opening_key, closing_key, whole_key = jax.random.split(key, 5)
    halves = TOK_DEV // 2
    spread = jax.random.randint(spread_key, (N_DP, N_FSDP), 0, halves + 1)
    counts = TOK_DEV - spread * spread // halves
    filled = jax.random.randint(filled_key, (N_DP, 1), 0, N_FSDP)
    counts = jnp.where(jnp.arange(N_FSDP)[None, :] == filled, TOK_DEV, counts)
    whole_group = jax.random.randint(whole_key, (), 0, N_DP)
    chosen = jnp.arange(N_DP) == whole_group
    counts = jnp.where(chosen[:, None], TOK_DEV, counts).astype(jnp.int32)
    opening = jax.random.randint(opening_key, (N_DP,), 0, 1 << 20) % (counts[:, 0] // 4) + 1
    closing = jax.random.randint(closing_key, (N_DP,), 0, 1 << 20) % (counts[:, N_FSDP - 1] // 4) + 1
    opening = jnp.where(chosen, 1, opening)
    closing = jnp.where(chosen, 1, closing)
    overall = jnp.sum(counts, axis=1)
    lengths = jnp.stack([opening, overall - opening - closing, closing], axis=1).astype(jnp.int32)
    return (counts, lengths)


def draw_counts(key, part):
    return layout(key)[0]


def draw_lengths(key, part):
    return layout(key)[1]


def steps_of(key, shape, cuts, least, high):
    def one(dim, blocks):
        draws = jax.random.uniform(jax.random.fold_in(jax.random.fold_in(key, 6), dim), (blocks,), jnp.float32, least / len(cuts), high / len(cuts))
        return jnp.repeat(jnp.exp(draws), shape[dim] // blocks).reshape((-1,) + (1,) * (len(shape) - dim - 1))

    level = one(*cuts[0])
    for cut in cuts[1:]:
        level = level * one(*cut)
    return level


def bell_draw(rng, dims, width, limit, cuts=(), kind=jnp.bfloat16):
    drawn = width * jax.random.normal(rng, dims, jnp.float32)
    if cuts:
        drawn = drawn * steps_of(rng, dims, cuts, -0.22, 0.18)
    return jnp.clip(drawn, -limit, limit).astype(kind)


def setup_inputs(seed: int = 0) -> dict:
    keys = jax.random.split(jax.random.key(seed), 15)
    tokens = bell_draw(keys[0], (TOKENS, D), 1.0, 6.0, ((0, 32),))
    counts = draw_counts(jax.random.fold_in(keys[14], 71), 0)
    lengths = draw_lengths(jax.random.fold_in(keys[14], 71), 0)
    gain = jnp.clip(1.0 + 0.1 * jax.random.normal(keys[3], (D,), jnp.float32), 0.5, 1.5).astype(jnp.bfloat16)
    in_weight = bell_draw(keys[4], (D, 2 * DI), D ** -0.5, 0.125, ((0, 32),))
    conv_weight = bell_draw(keys[5], (KC, DI), KC ** -0.5, 3.0, ((1, 32),))
    conv_bias = bell_draw(keys[6], (DI,), 0.5, 3.0, ((0, 32),))
    x_weight = bell_draw(keys[7], (DI, PROJ), DI ** -0.5, 0.09375, ((0, 32),))
    dt_weight = bell_draw(keys[8], (R, DI), R ** -0.5, 0.5, ((1, 32),))
    dt_bias = jnp.clip(-6.875 + 4.578125 * jax.random.uniform(keys[9], (DI,), jnp.float32) ** steps_of(keys[9], (DI,), ((0, 32),), -0.2, 0.2), -6.875, -2.296875).astype(jnp.bfloat16)
    a_log = jnp.clip(-4.59375 + 7.390625 * jax.random.uniform(keys[10], (DI, N), jnp.float32) ** steps_of(keys[10], (DI, N), ((0, 32),), -0.2, 0.2), -4.59375, 2.796875).astype(jnp.bfloat16)
    skip = jnp.clip(0.5 + 1.0 * jax.random.uniform(keys[11], (DI,), jnp.float32) ** steps_of(keys[11], (DI,), ((0, 32),), -0.2, 0.2), 0.5, 1.5).astype(jnp.bfloat16)
    out_weight = bell_draw(keys[12], (DI, D), DI ** -0.5, 0.09375, ((0, 32),))
    cotangent = bell_draw(keys[13], (TOKENS, D), 1.0, 6.0, ((0, 32),))
    return {"tokens": tokens, "counts": counts, "lengths": lengths, "gain": gain, "in_weight": in_weight, "conv_weight": conv_weight, "conv_bias": conv_bias, "x_weight": x_weight, "dt_weight": dt_weight, "dt_bias": dt_bias, "a_log": a_log, "skip": skip, "out_weight": out_weight, "cotangent": cotangent}


EPS = 1e-05

@jax.custom_vjp
def low(v):
    return lax.optimization_barrier(v.astype(jnp.bfloat16)).astype(jnp.float32)

@jax.custom_vjp
def low_back(v):
    return v

def low_keep(v):
    return (low(v), None)

def low_pass(kept, grad):
    return (grad,)

def back_keep(v):
    return (v, None)

def back_low(kept, grad):
    return (low(grad),)
low.defvjp(low_keep, low_pass)
low_back.defvjp(back_keep, back_low)

def matmul(left, right):
    return jnp.dot(left, right, precision=lax.Precision.HIGHEST, preferred_element_type=jnp.float32)

def block_scan(state, pieces, decay_rates):

    def token_step(hidden, inputs):
        step_dt, step_u, step_b, step_c, step_keep, step_valid = inputs
        decay = step_keep * jnp.exp(step_dt[:, None] * decay_rates) + (1.0 - step_valid)
        hidden = decay * hidden + (step_valid * step_dt * step_u)[:, None] * step_b[None, :]
        return (hidden, lax.optimization_barrier(jnp.sum(hidden * step_c[None, :], axis=1)))
    return lax.scan(token_step, state, pieces)

def group_forward(tokens_group, weights, count_row, length_row):
    gain, in_weight, conv_weight, conv_bias, x_weight, dt_weight, dt_bias, a_log, skip, out_weight = weights
    slots = jnp.arange(GROUP, dtype=jnp.int32)
    device = slots // TOK_DEV
    within = slots % TOK_DEV
    offsets = jnp.cumsum(count_row) - count_row
    present = within < count_row[device]
    order = jnp.argsort(jnp.where(present, offsets[device] + within, GROUP + slots)).astype(jnp.int32)
    restore = jnp.argsort(order).astype(jnp.int32)
    overall = jnp.sum(count_row)
    second = length_row[0]
    third = length_row[0] + length_row[1]
    valid = (slots < overall).astype(jnp.float32)
    begin = jnp.where(slots >= third, third, jnp.where(slots >= second, second, 0))
    keep = valid * (slots != begin).astype(jnp.float32)
    packed = tokens_group[order]
    scale = lax.rsqrt(lax.optimization_barrier(jnp.mean(packed * packed, axis=1, keepdims=True)) + EPS)
    normed = low(packed * scale * gain)
    mixed = low_back(matmul(normed, in_weight))
    inner = mixed[:, :DI]
    gate = mixed[:, DI:]
    conv_out = conv_bias + conv_weight[KC - 1] * inner
    for lag_step in range(1, KC):
        moved = jnp.concatenate([jnp.zeros((lag_step, DI), jnp.float32), inner[:-lag_step]], axis=0)
        allowed = (slots - lag_step >= begin).astype(jnp.float32)
        conv_out = conv_out + conv_weight[KC - 1 - lag_step] * moved * allowed[:, None]
    activ = low(jax.nn.silu(conv_out))
    projected = low_back(matmul(activ, x_weight))
    rank_part = low(projected[:, :R])
    b_input = projected[:, R:R + N]
    c_output = projected[:, R + N:]
    step_dt = jax.nn.softplus(low_back(matmul(rank_part, dt_weight)) + dt_bias)
    decay_rates = -jnp.exp(a_log)
    blocks = GROUP // SPAN

    def shaped(value):
        return value.reshape((blocks, SPAN) + value.shape[1:])

    def one_block(state, pieces):
        return block_scan(state, pieces, decay_rates)
    _, scanned = lax.scan(jax.checkpoint(one_block), jnp.zeros((DI, N), jnp.float32), (shaped(step_dt), shaped(activ), shaped(b_input), shaped(c_output), shaped(keep), shaped(valid)))
    scan_out = scanned.reshape(GROUP, DI) + skip * activ
    gated = low(scan_out * jax.nn.silu(gate))
    result = packed + valid[:, None] * matmul(gated, out_weight)
    return result[restore]

def reference(tokens, counts, lengths, gain, in_weight, conv_weight, conv_bias, x_weight, dt_weight, dt_bias, a_log, skip, out_weight, cotangent):
    weights = tuple((value.astype(jnp.float32) for value in (gain, in_weight, conv_weight, conv_bias, x_weight, dt_weight, dt_bias, a_log, skip, out_weight)))
    inputs_all = tokens.astype(jnp.float32).reshape(N_DP, GROUP, D)
    cot_all = cotangent.astype(jnp.float32).reshape(N_DP, GROUP, D)
    start_sums = tuple((jnp.zeros_like(value) for value in weights))

    def one_group(running, inputs):
        group_tokens, group_cot, count_row, length_row = inputs

        def forward(tokens_value, weight_values):
            return group_forward(tokens_value, weight_values, count_row, length_row)
        result, pullback = jax.vjp(forward, group_tokens, weights)
        grad_tokens, grad_weights = pullback(group_cot)
        return (jax.tree.map(jnp.add, running, grad_weights), (result, grad_tokens))
    sums, (results, grad_tokens) = lax.scan(one_group, start_sums, (inputs_all, cot_all, counts, lengths))
    return (results.reshape(TOKENS, D).astype(jnp.bfloat16), grad_tokens.reshape(TOKENS, D), sums[0], sums[1], sums[2], sums[3], sums[4], sums[5], sums[6], sums[7], sums[8], sums[9])
```

```python
import functools

import jax
import jax.numpy as jnp
from jax import lax
from jax.experimental import pallas as pl
from jax.experimental.pallas import tpu as pltpu
from jax.sharding import PartitionSpec as P

BF, F32 = jnp.bfloat16, jnp.float32
LANES, SUB = 128, 8
LN2 = 0.6931471805599453
FAR = 1.0e5
EPS = 1e-5


def small_cost(flops):
    return pl.CostEstimate(flops=flops, bytes_accessed=1 << 16, transcendentals=0)


def scatter_lanes(ref, value, rows):
    for k in range(value.shape[1] // LANES):
        ref[pl.ds(k, rows, stride=SUB), :] = value[:, k * LANES : (k + 1) * LANES]


def gather_lanes(ref, width, rows):
    return jnp.concatenate(
        [ref[pl.ds(k, rows, stride=SUB), :] for k in range(width // LANES)], axis=1
    )


def softplus(v):
    return jnp.maximum(v, 0.0) + jnp.log1p(jnp.exp(-jnp.abs(v)))


def forward_kernel(bc, rank, dt_w, dt_b, act, valid, rate2, y_out, states, h_ref, dt_s, dtu_s, y_s):
    tb, width = act.shape
    n_state = rate2.shape[0] // SUB

    @pl.when(pl.program_id(0) == 0)
    def _():
        h_ref[...] = jnp.zeros_like(h_ref)
        if width < SUB * LANES:
            dt_s[...] = jnp.zeros_like(dt_s)
            dtu_s[...] = jnp.zeros_like(dtu_s)

    pre = jnp.dot(rank[...], dt_w[...], preferred_element_type=F32) + dt_b[...]
    dt = softplus(pre) * valid[...]
    scatter_lanes(dt_s, dt, tb)
    scatter_lanes(dtu_s, dt * act[...].astype(F32), tb)
    rates = [rate2[n * SUB : (n + 1) * SUB, :] for n in range(n_state)]
    first = [h_ref[n * SUB : (n + 1) * SUB, :] for n in range(n_state)]
    for n in range(n_state):
        states[0, n, 0:SUB, :] = first[n]

    def token(t, h):
        at = pl.multiple_of(t * SUB, SUB)
        dt_t = dt_s[pl.ds(at, SUB), :] + bc[t, 2 * n_state]
        dtu_t = dtu_s[pl.ds(at, SUB), :]
        new, parts = [], [None, None]
        for n in range(n_state):
            hn = jnp.exp2(dt_t * rates[n]) * h[n] + dtu_t * bc[t, n]
            states[0, n, pl.ds(at + SUB, SUB), :] = hn
            term = hn * bc[t, n_state + n]
            parts[n % 2] = term if parts[n % 2] is None else parts[n % 2] + term
            new.append(hn)
        y_s[pl.ds(at, SUB), :] = parts[0] + parts[1]
        return tuple(new)

    last = lax.fori_loop(0, tb, token, tuple(first), unroll=2)
    for n in range(n_state):
        h_ref[n * SUB : (n + 1) * SUB, :] = last[n]
    y_out[...] = gather_lanes(y_s, width, tb)


def scan_forward(bc, rank, dt_w, dt_b, act, valid, rate2, tb):
    slots, width = act.shape
    n_state = rate2.shape[0] // SUB
    nb = slots // tb
    whole = lambda i: (0, 0)
    row = lambda i: (i, 0)
    return pl.pallas_call(
        forward_kernel,
        grid=(nb,),
        in_specs=[
            pl.BlockSpec((tb, bc.shape[1]), row, memory_space=pltpu.SMEM),
            pl.BlockSpec((tb, rank.shape[1]), row),
            pl.BlockSpec(dt_w.shape, whole),
            pl.BlockSpec((1, width), whole),
            pl.BlockSpec((tb, width), row),
            pl.BlockSpec((tb, 1), row),
            pl.BlockSpec(rate2.shape, whole),
        ],
        out_specs=[
            pl.BlockSpec((tb, width), row),
            pl.BlockSpec((1, n_state, (tb + 1) * SUB, LANES), lambda i: (i, 0, 0, 0)),
        ],
        out_shape=[
            jax.ShapeDtypeStruct((slots, width), F32),
            jax.ShapeDtypeStruct((nb, n_state, (tb + 1) * SUB, LANES), F32),
        ],
        scratch_shapes=[pltpu.VMEM(rate2.shape, F32)] + [pltpu.VMEM((tb * SUB, LANES), F32)] * 3,
        compiler_params=pltpu.CompilerParams(vmem_limit_bytes=48 << 20),
        cost_estimate=small_cost(1 << 20),
        name="scan_forward",
    )(bc, rank, dt_w, dt_b, act, valid, rate2)


def backward_kernel(
    bc, rank, dt_w, dt_b, act, valid, rate2, skip, gs, states, fold,
    part_out, gu_out, dtw_out, vec_out, rate_out,
    g_ref, dt_s, dtu_s, gs_s, gdt_s, ab_s, lam_s,
):
    tb, width = act.shape
    n_state = rate2.shape[0] // SUB
    half = n_state // 2

    @pl.when(pl.program_id(0) == 0)
    def _():
        g_ref[...] = jnp.zeros_like(g_ref)
        rate_out[...] = jnp.zeros_like(rate_out)
        vec_out[...] = jnp.zeros_like(vec_out)
        dtw_out[...] = jnp.zeros_like(dtw_out)
        if width < SUB * LANES:
            for ref in (dt_s, dtu_s, gs_s):
                ref[...] = jnp.zeros_like(ref)

    u = act[...].astype(F32)
    ok = valid[...]
    pre = jnp.dot(rank[...], dt_w[...], preferred_element_type=F32) + dt_b[...]
    dt = softplus(pre) * ok
    gs_v = gs[...]
    scatter_lanes(dt_s, dt, tb)
    scatter_lanes(dtu_s, dt * u, tb)
    scatter_lanes(gs_s, gs_v, tb)

    for group in range(2):
        index = range(group * half, (group + 1) * half)
        rates = [rate2[n * SUB : (n + 1) * SUB, :] for n in index]

        def token(i, carry):
            g, acc = carry
            t = tb - 1 - i
            at = pl.multiple_of(t * SUB, SUB)
            dt_t = dt_s[pl.ds(at, SUB), :]
            dtd = dt_t + bc[t, 2 * n_state]
            gs_t = gs_s[pl.ds(at, SUB), :]
            new_g, new_acc = [], []
            gdt = ab = None
            for j, n in enumerate(index):
                lam = gs_t * bc[t, n_state + n] + g[j]
                lam_s[n, pl.ds(at, SUB), :] = lam
                back = jnp.exp2(dtd * rates[j]) * lam
                thr = back * states[0, n, pl.ds(at, SUB), :]
                gdt = thr * rates[j] if gdt is None else gdt + thr * rates[j]
                ab = lam * bc[t, n] if ab is None else ab + lam * bc[t, n]
                new_g.append(back)
                new_acc.append(acc[j] + thr * dt_t)
            if group == 0:
                gdt_s[pl.ds(at, SUB), :] = gdt
                ab_s[pl.ds(at, SUB), :] = ab
            else:
                gdt_s[pl.ds(at, SUB), :] += gdt
                ab_s[pl.ds(at, SUB), :] += ab
            return tuple(new_g), tuple(new_acc)

        start = (
            tuple(g_ref[n * SUB : (n + 1) * SUB, :] for n in index),
            tuple(rate_out[n * SUB : (n + 1) * SUB, :] for n in index),
        )
        g, acc = lax.fori_loop(0, tb, token, start, unroll=2)
        for j, n in enumerate(index):
            g_ref[n * SUB : (n + 1) * SUB, :] = g[j]
            rate_out[n * SUB : (n + 1) * SUB, :] = acc[j]

    ab = gather_lanes(ab_s, width, tb)
    gdt = gather_lanes(gdt_s, width, tb)
    gu_out[...] = gs_v * skip[...] + dt * ab
    grad_pre = ok * (gdt * LN2 + u * ab) * jax.nn.sigmoid(pre)
    vec_out[0:1, :] += jnp.sum(grad_pre, axis=0, keepdims=True)
    vec_out[1:2, :] += jnp.sum(gs_v * u, axis=0, keepdims=True)
    low = grad_pre.astype(BF)
    dtw_out[...] += lax.dot_general(rank[...], low, (((0,), (0,)), ((), ())), preferred_element_type=F32)
    rank_w = rank.shape[1]
    part_out[:, 0:rank_w] = lax.dot_general(low, dt_w[...], (((1,), (1,)), ((), ())), preferred_element_type=F32)

    lane = lax.broadcasted_iota(jnp.int32, (tb, LANES), 1)
    tail = jnp.zeros((tb, LANES), F32)
    dtu_v = dtu_s[...]
    gs_l = gs_s[...]
    for n in range(n_state):
        for at, value in ((n, lam_s[n] * dtu_v), (n_state + n, states[0, n, SUB:, :] * gs_l)):
            summed = jnp.dot(fold[...], value.astype(BF), preferred_element_type=F32)
            tail = jnp.where(lane == at, jnp.sum(summed, axis=1, keepdims=True), tail)
    part_out[:, rank_w:] = tail[:, 0 : 2 * n_state]


def scan_backward(bc, rank, dt_w, dt_b, act, valid, rate2, skip, gs, states, tb):
    slots, width = act.shape
    n_state = rate2.shape[0] // SUB
    nb = slots // tb
    whole = lambda i: (0, 0)
    row = lambda i: (nb - 1 - i, 0)
    rank_w = rank.shape[1]
    fold = (jnp.arange(tb * SUB)[None, :] // SUB == jnp.arange(tb)[:, None]).astype(BF)
    return pl.pallas_call(
        backward_kernel,
        grid=(nb,),
        in_specs=[
            pl.BlockSpec((tb, bc.shape[1]), row, memory_space=pltpu.SMEM),
            pl.BlockSpec((tb, rank_w), row),
            pl.BlockSpec(dt_w.shape, whole),
            pl.BlockSpec((1, width), whole),
            pl.BlockSpec((tb, width), row),
            pl.BlockSpec((tb, 1), row),
            pl.BlockSpec(rate2.shape, whole),
            pl.BlockSpec((1, width), whole),
            pl.BlockSpec((tb, width), row),
            pl.BlockSpec((1, n_state, (tb + 1) * SUB, LANES), lambda i: (nb - 1 - i, 0, 0, 0)),
            pl.BlockSpec(fold.shape, whole),
        ],
        out_specs=[
            pl.BlockSpec((tb, rank_w + 2 * n_state), row),
            pl.BlockSpec((tb, width), row),
            pl.BlockSpec(dt_w.shape, whole),
            pl.BlockSpec((2, width), whole),
            pl.BlockSpec(rate2.shape, whole),
        ],
        out_shape=[
            jax.ShapeDtypeStruct((slots, rank_w + 2 * n_state), F32),
            jax.ShapeDtypeStruct((slots, width), F32),
            jax.ShapeDtypeStruct(dt_w.shape, F32),
            jax.ShapeDtypeStruct((2, width), F32),
            jax.ShapeDtypeStruct(rate2.shape, F32),
        ],
        scratch_shapes=[pltpu.VMEM(rate2.shape, F32)]
        + [pltpu.VMEM((tb * SUB, LANES), F32)] * 5
        + [pltpu.VMEM((n_state, tb * SUB, LANES), F32)],
        compiler_params=pltpu.CompilerParams(vmem_limit_bytes=56 << 20),
        cost_estimate=small_cost(1 << 20),
        name="scan_backward",
    )(bc, rank, dt_w, dt_b, act, valid, rate2, skip, gs, states, fold)


def silu_grad(value, sig):
    return sig * (1.0 + value * (1.0 - sig))


def place_blocks(ref, own, other, index):
    chips, rows, _ = own.shape
    core = lax.rem(index, 2)
    for q in range(chips):
        ref[pl.ds(pl.multiple_of((2 * q + core) * rows, rows), rows), :] = own[q]
        ref[pl.ds(pl.multiple_of((2 * q + 1 - core) * rows, rows), rows), :] = other[q]


def read_row(ref, row, cols):
    base = pl.multiple_of(row // SUB * SUB, SUB)
    rows = ref[pl.ds(base, SUB), cols]
    mine = lax.broadcasted_iota(jnp.int32, rows.shape, 0) == row - base
    return jnp.sum(jnp.where(mine, rows, 0.0), axis=0, keepdims=True)


def add_row(ref, row, value):
    base = pl.multiple_of(row // SUB * SUB, SUB)
    rows = ref[pl.ds(base, SUB), :]
    mine = lax.broadcasted_iota(jnp.int32, rows.shape, 0) == row - base
    ref[pl.ds(base, SUB), :] = rows + jnp.where(mine, value, 0.0)


def split_kernel(n_dp, in_w, out):
    rows = in_w.shape[0]
    n_line, _, width = out.shape
    owned = width // n_dp
    for to in range(n_line):
        for half in range(2):
            for d in range(n_dp):
                at = ((half * n_dp + d) * n_line + to) * owned
                out[to, half * rows : (half + 1) * rows, d * owned : (d + 1) * owned] = in_w[:, at : at + owned]


def split_columns(in_w, n_dp, n_line):
    rows, both = in_w.shape
    width = both // (2 * n_line)
    if width // n_dp % LANES:
        blocks = in_w.reshape(rows, 2, n_dp, n_line, width // n_dp).transpose(3, 1, 0, 2, 4)
        return blocks.reshape(n_line, 2 * rows, width)
    vmem = pl.BlockSpec(memory_space=pltpu.VMEM)
    return pl.pallas_call(
        functools.partial(split_kernel, n_dp),
        in_specs=[vmem],
        out_specs=vmem,
        out_shape=jax.ShapeDtypeStruct((n_line, 2 * rows, width), in_w.dtype),
        cost_estimate=small_cost(1 << 10),
        name="split_columns",
    )(in_w)


def join_kernel(n_dp, inner, gate, in_w, gain, out, gain_out):
    n_line, rows, width = inner.shape
    owned = width // n_dp
    total = jnp.zeros((rows, LANES), F32)
    for half, parts in enumerate((inner, gate)):
        for line in range(n_line):
            for d in range(n_dp):
                at = ((half * n_dp + d) * n_line + line) * owned
                block = parts[line, :, d * owned : (d + 1) * owned].astype(F32)
                out[:, at : at + owned] = block
                term = block * in_w[:, at : at + owned].astype(F32)
                for low in range(0, owned, LANES):
                    total = total + term[:, low : low + LANES]
    gain_out[...] = jnp.sum(total, axis=1, keepdims=True) / gain[...]


def join_columns(inner, gate, in_w, gain, n_dp):
    rows, both = in_w.shape
    n_line, _, width = inner.shape
    if width // n_dp % LANES:
        blocks = jnp.stack([inner, gate]).astype(F32)
        full = blocks.reshape(2, n_line, rows, n_dp, -1).transpose(2, 0, 3, 1, 4).reshape(rows, both)
        return full, jnp.sum(full * in_w.astype(F32), axis=1) / gain.astype(F32)
    vmem = pl.BlockSpec(memory_space=pltpu.VMEM)
    full, gain_grad = pl.pallas_call(
        functools.partial(join_kernel, n_dp),
        in_specs=[vmem] * 4,
        out_specs=[vmem] * 2,
        out_shape=[jax.ShapeDtypeStruct((rows, both), F32), jax.ShapeDtypeStruct((rows, 1), F32)],
        cost_estimate=small_cost(1 << 10),
        name="join_columns",
    )(inner, gate, in_w, gain.astype(F32)[:, None])
    return full, gain_grad[:, 0]


def column_block(width, slots):
    return 256 if width % 256 == 0 and slots <= 1024 else LANES


def from_place(place, move, n_line, body):
    steps, sign = move
    if sign == 0:
        body(lax.rem(place - steps + n_line, n_line))
        return
    source = place - sign * steps

    @pl.when(jnp.logical_and(source >= 0, source < n_line))
    def _():
        body(source)


def split_cores(ref, kept, sent, index, n_dp):
    size = ref.shape[1] // n_dp
    core = lax.rem(index, 2)
    for q in range(kept.shape[1] // size):
        cols = slice(q * size, (q + 1) * size)
        kept[:, cols] = ref[:, pl.ds(pl.multiple_of((2 * q + core) * size, size), size)]
        sent[:, cols] = ref[:, pl.ds(pl.multiple_of((2 * q + 1 - core) * size, size), size)]


def project_kernel(n_line, n_dp, moves, info, *refs):
    toks, refs = refs[: len(moves)], refs[len(moves) :]
    own, other, gain, conv_w, conv_b, x_t, allowed, normed, kept, sent, inner, conv_out, activ, part32, w_nat, ext = refs
    held, model = toks[0].shape
    slots = held * n_line
    width = w_nat.shape[1]
    taps = conv_w.shape[0]
    rim = taps - 1
    step = 32
    for move, tok in zip(moves, toks):

        def normalise(source, tok=tok):
            base = source * held

            @pl.loop(0, held // step)
            def _(i):
                x = tok[pl.ds(pl.multiple_of(i * step, step), step), :].astype(F32)
                scale = lax.rsqrt(jnp.mean(x * x, axis=1, keepdims=True) + EPS)
                rows = pl.ds(pl.multiple_of(base + i * step, step), step)
                normed[rows, :] = (x * scale * gain[...]).astype(BF)

        from_place(info[1], move, n_line, normalise)

    split_cores(normed, kept, sent, info[0], n_dp)
    place_blocks(w_nat, own, other, info[0])
    cb = column_block(width, slots)

    @pl.loop(0, width // cb)
    def _(c):
        cols = pl.ds(pl.multiple_of(c * cb, cb), cb)
        inner[:, cols] = jnp.dot(normed[...], w_nat[:, cols], preferred_element_type=F32)
        for f in range(n_line):
            rows = slice(f * held, (f + 1) * held)
            ext[SUB : SUB + held, :] = inner[rows, cols]
            for k in range(1, rim + 1):
                if f == 0:
                    ext[SUB - k : SUB - k + 1, :] = jnp.zeros((1, cb), F32)
                else:
                    ext[SUB - k : SUB - k + 1, :] = read_row(inner, (f - 1) * held + info[1 + f] - k, cols)
            total = conv_b[:, cols]
            for lag in range(taps):
                tapped = ext[SUB - lag : SUB - lag + held, :]
                total = total + conv_w[rim - lag : rim - lag + 1, cols] * tapped * allowed[rows, lag : lag + 1]
            conv_out[rows, cols] = total
            activ[rows, cols] = (total * jax.nn.sigmoid(total)).astype(BF)

    part = lax.dot_general(activ[...], x_t[...], (((1,), (1,)), ((), ())), preferred_element_type=F32)
    part32[...] = part


def project(info, n_line, n_dp, moves, toks, own, other, gain, conv_w, conv_b, x_t, allowed):
    held, model = toks[0].shape
    slots = held * n_line
    width, proj = x_t.shape[1], x_t.shape[0]
    vmem = pl.BlockSpec(memory_space=pltpu.VMEM)
    shapes = [
        ((slots, model), BF), ((slots, model // 2), BF), ((slots, model // 2), BF),
        ((slots, width), F32), ((slots, width), F32), ((slots, width), BF),
        ((slots, proj), F32), ((model, width), BF),
    ]
    return pl.pallas_call(
        functools.partial(project_kernel, n_line, n_dp, moves),
        in_specs=[pl.BlockSpec(memory_space=pltpu.SMEM)] + [vmem] * (7 + len(toks)),
        out_specs=[vmem] * len(shapes),
        out_shape=[jax.ShapeDtypeStruct(s, t) for s, t in shapes],
        scratch_shapes=[pltpu.VMEM((SUB + slots // n_line, column_block(width, slots)), F32)],
        compiler_params=pltpu.CompilerParams(vmem_limit_bytes=56 << 20),
        cost_estimate=small_cost(1 << 20),
        name="project",
    )(info, *toks, own, other, gain, conv_w, conv_b, x_t, allowed)


def gate_kernel(n_line, n_dp, moves, info, *refs):
    cots, refs = refs[: len(moves)], refs[len(moves) :]
    own, other, o_nat, normed, y, act, skip, valid, gated, branch, gs, grad_gate, dout, w_nat, *halves = refs
    slots, width = y.shape
    held, model = cots[0].shape
    place_blocks(w_nat, own, other, info[0])
    for move, cot in zip(moves, cots):

        def mask(source, cot=cot):
            rows = pl.ds(pl.multiple_of(source * held, held), held)
            dout[rows, :] = (cot[...].astype(F32) * valid[rows, :]).astype(BF)

        from_place(info[1], move, n_line, mask)

    cb = column_block(width, slots)

    @pl.loop(0, width // cb)
    def _(c):
        cols = pl.ds(pl.multiple_of(c * cb, cb), cb)
        gate = jnp.dot(normed[...], w_nat[:, cols], preferred_element_type=F32)
        grad = lax.dot_general(dout[...], o_nat[cols, :], (((1,), (1,)), ((), ())), preferred_element_type=F32)
        sig = jax.nn.sigmoid(gate)
        scan_out = y[:, cols] + skip[:, cols] * act[:, cols].astype(F32)
        gated[:, cols] = (scan_out * gate * sig).astype(BF)
        gs[:, cols] = grad * gate * sig
        grad_gate[:, cols] = (grad * scan_out * silu_grad(gate, sig)).astype(BF)

    mb = column_block(model, slots)

    @pl.loop(0, model // mb)
    def _(c):
        cols = pl.ds(pl.multiple_of(c * mb, mb), mb)
        branch[:, cols] = jnp.dot(gated[...], o_nat[:, cols], preferred_element_type=F32).astype(BF)

    if halves:
        split_cores(gated, *halves, info[0], n_dp)


def gate_block(info, n_line, n_dp, moves, cots, own, other, out_w, normed, y, act, skip, valid):
    slots, width = y.shape
    model = normed.shape[1]
    vmem = pl.BlockSpec(memory_space=pltpu.VMEM)
    shapes = [
        ((slots, width), BF), ((slots, model), BF), ((slots, width), F32), ((slots, width), BF),
        ((slots, model), BF), ((model, width), BF),
    ]
    if width // n_dp % LANES == 0:
        shapes += [((slots, width // 2), BF)] * 2
    *outs, = pl.pallas_call(
        functools.partial(gate_kernel, n_line, n_dp, moves),
        in_specs=[pl.BlockSpec(memory_space=pltpu.SMEM)] + [vmem] * (8 + len(cots)),
        out_specs=[vmem] * len(shapes),
        out_shape=[jax.ShapeDtypeStruct(s, t) for s, t in shapes],
        compiler_params=pltpu.CompilerParams(vmem_limit_bytes=58 << 20),
        cost_estimate=small_cost(1 << 20),
        name="gate_block",
    )(info, *cots, own, other, out_w, normed, y, act, skip, valid)
    return outs[:6] + (outs[6:] or cores(outs[0], 1))


def conv_back_kernel(n_line, info, gp, gu, x_t, act, conv_out, inner, conv_w, allowed, gi_low, x_grad, vec, ext, gi, tail):
    slots, width = gu.shape
    held = slots // n_line
    taps = conv_w.shape[0]
    rim = taps - 1
    cb = column_block(width, slots)
    x_grad[...] = lax.dot_general(gp[...], act[...], (((0,), (0,)), ((), ())), preferred_element_type=F32)
    vec[...] = jnp.zeros_like(vec)
    for lag in range(taps):
        tail[lag, held : held + SUB, :] = jnp.zeros((SUB, cb), F32)

    @pl.loop(0, width // cb)
    def _(c):
        cols = pl.ds(pl.multiple_of(c * cb, cb), cb)
        for f in range(n_line - 1, -1, -1):
            rows = slice(f * held, (f + 1) * held)
            ext[SUB : SUB + held, :] = inner[rows, cols]
            for k in range(1, rim + 1):
                if f == 0:
                    ext[SUB - k : SUB - k + 1, :] = jnp.zeros((1, cb), F32)
                else:
                    ext[SUB - k : SUB - k + 1, :] = read_row(inner, (f - 1) * held + info[1 + f] - k, cols)
            grad = gu[rows, cols] + jnp.dot(gp[rows, :], x_t[:, cols], preferred_element_type=F32)
            co = conv_out[rows, cols]
            grad = grad * silu_grad(co, jax.nn.sigmoid(co))
            vec[taps : taps + 1, cols] += jnp.sum(grad, axis=0, keepdims=True)
            for lag in range(taps):
                weighted = grad * allowed[rows, lag : lag + 1]
                vec[rim - lag : rim - lag + 1, cols] += jnp.sum(
                    weighted * ext[SUB - lag : SUB - lag + held, :], axis=0, keepdims=True
                )
                tail[lag, 0:held, :] = weighted * conv_w[rim - lag : rim - lag + 1, cols]
            total = tail[0, 0:held, :]
            for lag in range(1, taps):
                total = total + tail[lag, lag : lag + held, :]
            gi[rows, :] = total
            if f + 1 < n_line:
                for k in range(1, rim + 1):
                    add_row(gi, f * held + info[2 + f] - k, gi[slots + k : slots + k + 1, :])
            for k in range(1, rim + 1):
                row = tail[k, 0:1, :]
                for lag in range(k + 1, taps):
                    row = row + tail[lag, lag - k : lag - k + 1, :]
                gi[slots + k : slots + k + 1, :] = row
        gi_low[:, cols] = gi[0:slots, :].astype(BF)


def conv_back(info, n_line, gp, gu, x_t, act, conv_out, inner, conv_w, allowed):
    slots, width = gu.shape
    held = slots // n_line
    taps = conv_w.shape[0]
    cb = column_block(width, slots)
    vmem = pl.BlockSpec(memory_space=pltpu.VMEM)
    shapes = [((slots, width), BF), (x_t.shape, F32), ((SUB, width), F32)]
    return pl.pallas_call(
        functools.partial(conv_back_kernel, n_line),
        in_specs=[pl.BlockSpec(memory_space=pltpu.SMEM)] + [vmem] * 8,
        out_specs=[vmem] * len(shapes),
        out_shape=[jax.ShapeDtypeStruct(s, t) for s, t in shapes],
        scratch_shapes=[
            pltpu.VMEM((SUB + held, cb), F32),
            pltpu.VMEM((slots + SUB, cb), F32),
            pltpu.VMEM((taps, held + SUB, cb), F32),
        ],
        compiler_params=pltpu.CompilerParams(vmem_limit_bytes=48 << 20),
        cost_estimate=small_cost(1 << 20),
        name="conv_back",
    )(info, gp, gu, x_t, act, conv_out, inner, conv_w, allowed)


def swap(value, axis, mask):
    count = lax.axis_size(axis)
    return lax.ppermute(value, axis, [(i, i ^ mask) for i in range(count)])


def shift(value, axis, steps):
    count = lax.axis_size(axis)
    return lax.ppermute(value, axis, [(i, (i + steps) % count) for i in range(count)])


def chips_of(axis):
    return [list(range(core, lax.axis_size(axis), 2)) for core in range(2)]


def to_line(blocks):
    return lax.all_to_all(blocks, "fsdp", 0, 0)


def to_chips(blocks):
    return lax.all_to_all(blocks, "dp", 0, 0, axis_index_groups=chips_of("dp"))


def repeated(value, count):
    return jnp.broadcast_to(value[None], (count,) + value.shape)


def in_order(parts, axis):
    count, me = lax.axis_size(axis), lax.axis_index(axis)
    up = jnp.stack([parts[-k % count] for k in range(count)] * 2)
    return lax.dynamic_slice_in_dim(up, lax.rem(count - me, count), count, 0)


def by_chip(parts):
    chip, count = lax.div(lax.axis_index("dp"), 2), len(parts)
    bits = count.bit_length() - 1
    cube = jnp.stack(parts).reshape((2,) * bits + parts[0].shape)
    for place in range(bits):
        mine = lax.rem(chip >> (bits - 1 - place), 2) == 1
        cube = jnp.where(mine, jnp.flip(cube, place), cube)
    return cube.reshape((count,) + parts[0].shape)


def by_device(own, other):
    core = lax.rem(lax.axis_index("dp"), 2) == 1
    both = jnp.where(core, jnp.stack([other, own], axis=1), jnp.stack([own, other], axis=1))
    return lax.optimization_barrier(both.reshape((-1,) + own.shape[1:]))


def total_line(value):
    reach = 1
    while reach < lax.axis_size("fsdp"):
        value = value + swap(value.astype(BF), "fsdp", reach).astype(F32)
        reach *= 2
    return value


def fence(*values):
    flat, shape = jax.tree.flatten(values)
    return jax.tree.unflatten(shape, lax.optimization_barrier(tuple(flat)))


def cores(value, axis):
    cut = value.shape[:axis] + (lax.axis_size("dp") // 2, 2, -1) + value.shape[axis + 1 :]
    cube = value.reshape(cut)
    core = lax.rem(lax.axis_index("dp"), 2)
    found = [lax.dynamic_index_in_dim(cube, at, axis + 1, keepdims=False) for at in (core, 1 - core)]
    flat = value.shape[:axis] + (value.shape[axis] // 2,) + value.shape[axis + 1 :]
    return [part.reshape(flat) for part in found]


def weight_grad(kept, sent, right):
    return contract_rows(kept, right), contract_rows(sent, right).astype(BF)


def add_core(kept, sent):
    total = kept + swap(sent, "dp", 1).astype(F32)
    return total.reshape((lax.axis_size("dp") // 2, -1) + kept.shape[1:])


def add_chips(blocks):
    return jnp.sum(to_chips(blocks.astype(BF)).astype(F32), axis=0)


def add_chips_near(blocks):
    count, chip = lax.axis_size("dp") // 2, lax.div(lax.axis_index("dp"), 2)
    total = lax.dynamic_index_in_dim(blocks, chip, 0, keepdims=False)
    for u in range(1, count):
        total = total + far(blocks, u).astype(F32)
    return total


def far(blocks, u):
    chip = lax.div(lax.axis_index("dp"), 2)
    block = lax.dynamic_index_in_dim(blocks, jnp.bitwise_xor(chip, u), 0, keepdims=False)
    return swap(block.astype(BF), "dp", 2 * u)


class Gather:
    def __init__(self, value):
        self.count = lax.axis_size("fsdp")
        self.hops = self.count <= 4
        self.found = {(0, 0): value}

    def hop(self, steps):
        if not self.hops:
            self.found[steps, 0] = shift(self.found[0, 0], "fsdp", steps)
            return
        for sign in (1, -1):
            last = self.found[(0, 0) if steps == 1 else (steps - 1, sign)]
            pairs = [(i, i + 1) for i in range(steps - 1, self.count - 1)]
            if sign < 0:
                pairs = [(self.count - 1 - i, self.count - 1 - j) for i, j in pairs]
            self.found[steps, sign] = lax.ppermute(last, "fsdp", pairs)

    def fenced(self, *others):
        self.found, *others = fence(self.found, *others)
        return others

    def moves(self):
        return tuple(sorted(self.found))

    def blocks(self):
        return [self.found[move] for move in sorted(self.found)]

def contract_rows(left, right):
    return lax.dot_general(left, right, (((0,), (0,)), ((), ())), preferred_element_type=F32)


def contract_cols(left, right):
    return lax.dot_general(left, right, (((1,), (1,)), ((), ())), preferred_element_type=F32)


def per_device(
    tokens, counts, lengths, gain, in_weight, conv_weight, conv_bias, x_weight,
    dt_weight, dt_bias, a_log, skip, out_weight, cotangent,
):
    n_dp, n_line = lax.axis_size("dp"), lax.axis_size("fsdp")
    group, place = lax.axis_index("dp"), lax.axis_index("fsdp")
    held_slots, model = tokens.shape
    slots = held_slots * n_line
    owned = skip.shape[0]
    width = owned * n_dp
    in_rows = in_weight.shape[0]
    taps, rank_w, n_state = conv_weight.shape[0], dt_weight.shape[0], a_log.shape[1]
    proj = x_weight.shape[1]
    tb = 64 if slots % 64 == 0 else slots

    count_row = lax.dynamic_index_in_dim(counts, group, 0, keepdims=False)
    length_row = lax.dynamic_index_in_dim(lengths, group, 0, keepdims=False)
    info = jnp.concatenate([jnp.stack([group, place]).astype(jnp.int32), count_row])
    offsets = jnp.cumsum(count_row) - count_row
    within = lax.broadcasted_iota(jnp.int32, (n_line, held_slots), 1)
    present = within < count_row[:, None]
    position = offsets[:, None] + within
    second, third = length_row[0], length_row[0] + length_row[1]
    begin = jnp.where(position >= third, third, jnp.where(position >= second, second, 0))
    marks = jnp.stack(
        [position - lag >= begin for lag in range(taps)] + [present, present & (position == begin)]
    ).astype(F32).reshape(taps + 2, slots).T
    allowed, valid, opens = marks[:, :taps], marks[:, taps : taps + 1], marks[:, taps + 1 :] * FAR

    own_tokens, own_cot = tokens, cotangent
    steps = range(1, n_line)
    chips = range(1, n_dp // 2)
    out_w = lax.all_gather(out_weight, "dp", tiled=True)

    parts = split_columns(in_weight, n_dp, n_line)
    parts, tokens, gain_in = fence(parts, tokens, gain)
    parts = to_line(parts)
    toks = Gather(tokens)
    toks.hop(1)
    gains = [gain_in] + [shift(gain_in, "fsdp", s) for s in steps]
    parts, gains = toks.fenced(parts, gains)

    line_gain = in_order(gains, "fsdp").reshape(-1, owned)
    rest = jnp.concatenate([conv_weight, conv_bias[None], dt_bias[None], skip[None], line_gain], axis=0)
    rest = jnp.pad(rest, ((0, -rest.shape[0] % 16), (0, 0)))
    small = jnp.concatenate([dt_weight, x_weight.T, a_log.T, rest], axis=0)
    inner_rep = repeated(parts[:, :in_rows].reshape(-1, width), n_dp // 2)
    inner_rep, small, gate_in = toks.fenced(inner_rep, small, parts[:, in_rows:].reshape(-1, width))
    inner_own = to_chips(inner_rep)
    toks.hop(2)
    near = [small] + [swap(small, "dp", 2 * u) for u in chips]
    near, gate_in, cotangent = toks.fenced(near, gate_in, cotangent)
    for s in steps[2:]:
        toks.hop(s)
    near = by_chip(near)
    near_other = swap(near, "dp", 1)
    inner_own, near, near_other = toks.fenced(inner_own, near, near_other)

    cots = Gather(cotangent)
    inner_own, near, near_other = cots.fenced(inner_own, near, near_other)
    inner_other = swap(inner_own, "dp", 1)
    cots.hop(1)
    gate_rep = repeated(gate_in, n_dp // 2)
    small = by_device(near, near_other)
    first = rank_w + proj + n_state
    at_gain = first + taps + 3
    full_gain = small[:, at_gain : at_gain + line_gain.shape[0]].reshape(1, model).astype(F32)
    small = lax.optimization_barrier(small.transpose(1, 0, 2).reshape(-1, width))
    cuts = [0]
    for size in (rank_w, proj, n_state, taps, 1, 1, 1):
        cuts.append(cuts[-1] + size)
    dt_w, x_t, a_t, conv_w, conv_b, dt_b, skip_w = [small[a:b] for a, b in zip(cuts[:-1], cuts[1:])]
    conv_w, conv_b, dt_b, skip_w = [v.astype(F32) for v in (conv_w, conv_b, dt_b, skip_w)]
    rates = -jnp.exp(a_t.astype(F32))
    chunks = width // LANES
    rate2 = jnp.pad(
        (rates * (1.0 / LN2)).reshape(n_state, chunks, LANES), ((0, 0), (0, SUB - chunks), (0, 0))
    ).reshape(n_state * SUB, LANES)

    gate_rep, inner_own, inner_other, full_gain, x_t, conv_w = cots.fenced(
        gate_rep, inner_own, inner_other, full_gain, x_t, conv_w
    )
    gate_own = to_chips(gate_rep)
    cots.hop(2)
    normed, normed_kept, normed_sent, inner, conv_out, activ, part, inner_nat = project(
        info, n_line, n_dp, toks.moves(), toks.blocks(), inner_own, inner_other, full_gain, conv_w, conv_b, x_t, allowed
    )
    part, = cots.fenced(part)

    projected = total_line(part)
    projected, gate_own = cots.fenced(projected, gate_own)

    gate_other = swap(gate_own, "dp", 1)
    for s in steps[2:]:
        cots.hop(s)
    rank_low = projected[:, :rank_w].astype(BF)
    bc = jnp.concatenate([projected[:, rank_w:], opens], axis=1)
    scanned, states = scan_forward(bc, rank_low, dt_w, dt_b, activ, valid, rate2, tb)
    scanned, gate_own, gate_other = cots.fenced(scanned, gate_own, gate_other)

    gated, branch, grad_scan, grad_gate, dout, gate_nat, gated_kept, gated_sent = gate_block(
        info, n_line, n_dp, cots.moves(), cots.blocks(), gate_own, gate_other, out_w, normed, scanned, activ, skip_w, valid
    )
    branch = branch.reshape(n_line, held_slots, model)

    def sent_to(blocks, s):
        return lax.dynamic_index_in_dim(blocks, lax.rem(place + s, n_line), 0, keepdims=False)

    branches = [sent_to(branch, s) for s in range(n_line)]
    branches, gated_kept, gated_sent, dout, grad_gate = fence(branches, gated_kept, gated_sent, dout, grad_gate)
    branches[1] = shift(branches[1], "fsdp", 1)
    gate_grad = weight_grad(normed_kept, normed_sent, grad_gate)
    gate_grad = add_core(*gate_grad).astype(BF)
    out_grad = weight_grad(gated_kept, gated_sent, dout)
    branches, out_grad, gate_grad, grad_scan = fence(branches, out_grad, gate_grad, grad_scan)

    gate_rows = add_chips(gate_grad).astype(BF)
    for s in steps[1:]:
        branches[s] = shift(branches[s], "fsdp", s)
    out_grad = add_core(*out_grad)
    part, grad_u, dt_w_grad, vectors, rate_sum = scan_backward(
        bc, rank_low, dt_w, dt_b, activ, valid, rate2, skip_w, grad_scan, states, tb
    )
    part, branches, out_grad, gate_rows = fence(part, branches, out_grad, gate_rows)

    out_far = {u: far(out_grad, u) for u in chips[:-1]}
    out_weight_grad = lax.dynamic_index_in_dim(out_grad, lax.div(group, 2), 0, keepdims=False)
    normed_gate = contract_cols(grad_gate, gate_nat)
    own_valid = lax.dynamic_slice_in_dim(valid, place * held_slots, held_slots, 0)
    own_f = own_tokens.astype(F32)
    output = (own_f + own_valid * sum(p.astype(F32) for p in branches)).astype(BF)
    grad_projected = total_line(part).astype(BF)
    grad_projected, out_far, output, normed_gate = fence(grad_projected, out_far, output, normed_gate)

    gate_got = to_line(gate_rows.reshape(n_line, in_rows, width))
    rate_sum = rate_sum.reshape(n_state, SUB, LANES)[:, :chunks].reshape(n_state, width)
    grad_inner, x_t_grad, conv_grads = conv_back(
        info, n_line, grad_projected, grad_u, x_t, activ, conv_out, inner, conv_w, allowed
    )
    inner_grad = weight_grad(normed_kept, normed_sent, grad_inner)
    grad_normed = (contract_cols(grad_inner, inner_nat) + normed_gate).astype(BF)
    grad_normed = grad_normed.reshape(n_line, held_slots, model)
    grads = [sent_to(grad_normed, s) for s in range(n_line)]
    inner_grad, grads, gate_got, x_t_grad, conv_grads = fence(inner_grad, grads, gate_got, x_t_grad, conv_grads)

    grads[1] = shift(grads[1], "fsdp", 1)
    inner_grad = add_core(*inner_grad).astype(BF)
    for u in chips[-1:]:
        out_far[u] = far(out_grad, u)
    small_grads = jnp.concatenate(
        [dt_w_grad, x_t_grad, rate_sum * rates, conv_grads[: taps + 1], vectors], axis=0
    )
    small_grads = jnp.pad(small_grads, ((0, -cuts[-1] % 32), (0, 0)))
    small_rows = small_grads.shape[0]
    small_kept, small_sent = cores(small_grads, 1)
    small_grads = (small_kept + swap(small_sent.astype(BF), "dp", 1).astype(F32)).reshape(small_rows, n_dp // 2, owned)
    small_grads = small_grads.transpose(1, 0, 2)
    inner_grad, grads, small_grads, out_far = fence(inner_grad, grads, small_grads, out_far)
    out_weight_grad = out_weight_grad + sum(out_far[u].astype(F32) for u in chips)

    inner_rows = add_chips(inner_grad).astype(BF)
    for s in steps[1:]:
        grads[s] = shift(grads[s], "fsdp", s)
    small_grads = add_chips_near(small_grads)
    inner_rows, grads, small_grads = fence(inner_rows, grads, small_grads)

    inner_got = to_line(inner_rows.reshape(n_line, in_rows, width))
    grad_normed = sum(p.astype(F32) for p in grads)
    own_scale = lax.rsqrt(jnp.mean(own_f * own_f, axis=1, keepdims=True) + EPS)
    unit = own_f * own_scale
    grad_unit = grad_normed * full_gain
    token_grad = own_cot.astype(F32) + own_scale * (
        grad_unit - unit * jnp.mean(grad_unit * unit, axis=1, keepdims=True)
    )
    dt_g, x_g, a_g, conv_g, conv_b_g, dt_b_g, skip_g = [
        small_grads[a:b] for a, b in zip(cuts[:-1], cuts[1:])
    ]
    in_weight_grad, gain_grad = join_columns(inner_got, gate_got, in_weight, gain, n_dp)
    return (
        output, token_grad, gain_grad, in_weight_grad, conv_g, conv_b_g[0], x_g.T, dt_g, dt_b_g[0], a_g.T,
        skip_g[0], out_weight_grad,
    )


def solution(mesh):
    both = ("dp", "fsdp")
    rows, cols, vec = P(both, None), P(None, both), P(both)
    return jax.shard_map(
        per_device,
        mesh=mesh,
        in_specs=(rows, P(), P(), vec, rows, cols, vec, rows, cols, vec, rows, vec, rows, rows),
        out_specs=(rows, rows, vec, rows, cols, vec, rows, cols, vec, rows, vec, rows),
        check_vma=False,
    )
```

```python
import functools

import jax
import jax.numpy as jnp
from jax import lax
from jax.experimental import pallas as pl
from jax.experimental.pallas import tpu as pltpu
from jax.sharding import PartitionSpec as P

BF, F32 = jnp.bfloat16, jnp.float32
LANES, SUB = 128, 8
LN2 = 0.6931471805599453
FAR = 1.0e5
EPS = 1e-5


def small_cost(flops):
    return pl.CostEstimate(flops=flops, bytes_accessed=1 << 16, transcendentals=0)


class Small:
    def __init__(self, rank, proj, state, taps):
        self.dt_w = slice(0, rank)
        self.x_t = slice(rank, rank + proj)
        self.a_t = slice(rank + proj, rank + proj + state)
        self.rest = slice(rank + proj + state, rank + proj + state + 16)
        self.taps, self.rows = taps, rank + proj + state + 16

    def fold(self, parts):
        rows = -(-self.rows // parts)
        return rows + -rows % 16

    def vector(self, ref, at):
        return ref[self.rest, :].astype(F32)[at : at + 1, :]


def scatter_lanes(ref, value, rows):
    for k in range(value.shape[1] // LANES):
        ref[pl.ds(k, rows, stride=SUB), :] = value[:, k * LANES : (k + 1) * LANES]


def gather_lanes(ref, width, rows):
    return jnp.concatenate(
        [ref[pl.ds(k, rows, stride=SUB), :] for k in range(width // LANES)], axis=1
    )


def softplus(v):
    return jnp.maximum(v, 0.0) + jnp.log1p(jnp.exp(-jnp.abs(v)))


def forward_kernel(at, bc, rank, small, act, valid, rate2, y_out, states, h_ref, dt_s, dtu_s, y_s):
    tb, width = act.shape
    n_state = rate2.shape[0] // SUB

    @pl.when(pl.program_id(0) == 0)
    def _():
        h_ref[...] = jnp.zeros_like(h_ref)
        if width < SUB * LANES:
            dt_s[...] = jnp.zeros_like(dt_s)
            dtu_s[...] = jnp.zeros_like(dtu_s)

    dt_b = at.vector(small, at.taps + 1)
    pre = jnp.dot(rank[...], small[at.dt_w, :], preferred_element_type=F32) + dt_b
    dt = softplus(pre) * valid[...]
    scatter_lanes(dt_s, dt, tb)
    scatter_lanes(dtu_s, dt * act[...].astype(F32), tb)
    rates = [rate2[n * SUB : (n + 1) * SUB, :] for n in range(n_state)]
    first = [h_ref[n * SUB : (n + 1) * SUB, :] for n in range(n_state)]
    for n in range(n_state):
        states[0, n, 0:SUB, :] = first[n]

    def token(t, h):
        at = pl.multiple_of(t * SUB, SUB)
        dt_t = dt_s[pl.ds(at, SUB), :] + bc[t, 2 * n_state]
        dtu_t = dtu_s[pl.ds(at, SUB), :]
        new, parts = [], [None, None]
        for n in range(n_state):
            hn = jnp.exp2(dt_t * rates[n]) * h[n] + dtu_t * bc[t, n]
            states[0, n, pl.ds(at + SUB, SUB), :] = hn
            term = hn * bc[t, n_state + n]
            parts[n % 2] = term if parts[n % 2] is None else parts[n % 2] + term
            new.append(hn)
        y_s[pl.ds(at, SUB), :] = parts[0] + parts[1]
        return tuple(new)

    last = lax.fori_loop(0, tb, token, tuple(first), unroll=8)
    for n in range(n_state):
        h_ref[n * SUB : (n + 1) * SUB, :] = last[n]
    y_out[...] = gather_lanes(y_s, width, tb)


def scan_forward(at, bc, rank, small, act, valid, rate2, tb):
    slots, width = act.shape
    n_state = rate2.shape[0] // SUB
    nb = slots // tb
    whole = lambda i: (0, 0)
    row = lambda i: (i, 0)
    return pl.pallas_call(
        functools.partial(forward_kernel, at),
        grid=(nb,),
        in_specs=[
            pl.BlockSpec((tb, bc.shape[1]), row, memory_space=pltpu.SMEM),
            pl.BlockSpec((tb, rank.shape[1]), row),
            pl.BlockSpec(small.shape, whole),
            pl.BlockSpec((tb, width), row),
            pl.BlockSpec((tb, 1), row),
            pl.BlockSpec(rate2.shape, whole),
        ],
        out_specs=[
            pl.BlockSpec((tb, width), row),
            pl.BlockSpec((1, n_state, (tb + 1) * SUB, LANES), lambda i: (i, 0, 0, 0)),
        ],
        out_shape=[
            jax.ShapeDtypeStruct((slots, width), F32),
            jax.ShapeDtypeStruct((nb, n_state, (tb + 1) * SUB, LANES), F32),
        ],
        scratch_shapes=[pltpu.VMEM(rate2.shape, F32)] + [pltpu.VMEM((tb * SUB, LANES), F32)] * 3,
        compiler_params=pltpu.CompilerParams(vmem_limit_bytes=48 << 20),
        cost_estimate=small_cost(1 << 20),
        name="scan_forward",
    )(bc, rank, small, act, valid, rate2)


def backward_kernel(
    at_small, bc, rank, small, act, valid, rate2, gs, states, fold,
    part_out, gu_out, dtw_out, vec_out, rate_out,
    g_ref, dt_s, dtu_s, gs_s, gdt_s, ab_s, lam_s,
):
    tb, width = act.shape
    n_state = rate2.shape[0] // SUB
    half = n_state // 2

    @pl.when(pl.program_id(0) == 0)
    def _():
        g_ref[...] = jnp.zeros_like(g_ref)
        rate_out[...] = jnp.zeros_like(rate_out)
        vec_out[...] = jnp.zeros_like(vec_out)
        dtw_out[...] = jnp.zeros_like(dtw_out)
        if width < SUB * LANES:
            for ref in (dt_s, dtu_s, gs_s):
                ref[...] = jnp.zeros_like(ref)

    u = act[...].astype(F32)
    ok = valid[...]
    dt_b, skip = at_small.vector(small, at_small.taps + 1), at_small.vector(small, at_small.taps + 2)
    pre = jnp.dot(rank[...], small[at_small.dt_w, :], preferred_element_type=F32) + dt_b
    dt = softplus(pre) * ok
    gs_v = gs[...]
    scatter_lanes(dt_s, dt, tb)
    scatter_lanes(dtu_s, dt * u, tb)
    scatter_lanes(gs_s, gs_v, tb)

    for group in range(2):
        index = range(group * half, (group + 1) * half)
        rates = [rate2[n * SUB : (n + 1) * SUB, :] for n in index]

        def token(i, carry):
            g, acc = carry
            t = tb - 1 - i
            at = pl.multiple_of(t * SUB, SUB)
            dt_t = dt_s[pl.ds(at, SUB), :]
            dtd = dt_t + bc[t, 2 * n_state]
            gs_t = gs_s[pl.ds(at, SUB), :]
            new_g, new_acc = [], []
            gdt = ab = None
            for j, n in enumerate(index):
                lam = gs_t * bc[t, n_state + n] + g[j]
                lam_s[n, pl.ds(at, SUB), :] = lam
                back = jnp.exp2(dtd * rates[j]) * lam
                thr = back * states[0, n, pl.ds(at, SUB), :]
                gdt = thr * rates[j] if gdt is None else gdt + thr * rates[j]
                ab = lam * bc[t, n] if ab is None else ab + lam * bc[t, n]
                new_g.append(back)
                new_acc.append(acc[j] + thr * dt_t)
            if group == 0:
                gdt_s[pl.ds(at, SUB), :] = gdt
                ab_s[pl.ds(at, SUB), :] = ab
            else:
                gdt_s[pl.ds(at, SUB), :] += gdt
                ab_s[pl.ds(at, SUB), :] += ab
            return tuple(new_g), tuple(new_acc)

        start = (
            tuple(g_ref[n * SUB : (n + 1) * SUB, :] for n in index),
            tuple(rate_out[n * SUB : (n + 1) * SUB, :] for n in index),
        )
        g, acc = lax.fori_loop(0, tb, token, start, unroll=8)
        for j, n in enumerate(index):
            g_ref[n * SUB : (n + 1) * SUB, :] = g[j]
            rate_out[n * SUB : (n + 1) * SUB, :] = acc[j]

    ab = gather_lanes(ab_s, width, tb)
    gdt = gather_lanes(gdt_s, width, tb)
    gu_out[...] = gs_v * skip + dt * ab
    grad_pre = ok * (gdt * LN2 + u * ab) * jax.nn.sigmoid(pre)
    vec_out[0:1, :] += jnp.sum(grad_pre, axis=0, keepdims=True)
    vec_out[1:2, :] += jnp.sum(gs_v * u, axis=0, keepdims=True)
    low = grad_pre.astype(BF)
    dtw_out[...] += lax.dot_general(rank[...], low, (((0,), (0,)), ((), ())), preferred_element_type=F32)
    rank_w = rank.shape[1]
    part_out[:, 0:rank_w] = lax.dot_general(low, small[at_small.dt_w, :], (((1,), (1,)), ((), ())), preferred_element_type=F32)

    lane = lax.broadcasted_iota(jnp.int32, (tb, LANES), 1)
    tail = jnp.zeros((tb, LANES), F32)
    dtu_v = dtu_s[...]
    gs_l = gs_s[...]
    for n in range(n_state):
        for at, value in ((n, lam_s[n] * dtu_v), (n_state + n, states[0, n, SUB:, :] * gs_l)):
            summed = jnp.dot(fold[...], value.astype(BF), preferred_element_type=F32)
            tail = jnp.where(lane == at, jnp.sum(summed, axis=1, keepdims=True), tail)
    part_out[:, rank_w:] = tail[:, 0 : 2 * n_state]


def scan_backward(at, bc, rank, small, act, valid, rate2, gs, states, tb):
    slots, width = act.shape
    n_state = rate2.shape[0] // SUB
    nb = slots // tb
    whole = lambda i: (0, 0)
    row = lambda i: (nb - 1 - i, 0)
    rank_w = rank.shape[1]
    fold = (jnp.arange(tb * SUB)[None, :] // SUB == jnp.arange(tb)[:, None]).astype(BF)
    return pl.pallas_call(
        functools.partial(backward_kernel, at),
        grid=(nb,),
        in_specs=[
            pl.BlockSpec((tb, bc.shape[1]), row, memory_space=pltpu.SMEM),
            pl.BlockSpec((tb, rank_w), row),
            pl.BlockSpec(small.shape, whole),
            pl.BlockSpec((tb, width), row),
            pl.BlockSpec((tb, 1), row),
            pl.BlockSpec(rate2.shape, whole),
            pl.BlockSpec((tb, width), row),
            pl.BlockSpec((1, n_state, (tb + 1) * SUB, LANES), lambda i: (nb - 1 - i, 0, 0, 0)),
            pl.BlockSpec(fold.shape, whole),
        ],
        out_specs=[
            pl.BlockSpec((tb, rank_w + 2 * n_state), row),
            pl.BlockSpec((tb, width), row),
            pl.BlockSpec((rank_w, width), whole),
            pl.BlockSpec((2, width), whole),
            pl.BlockSpec(rate2.shape, whole),
        ],
        out_shape=[
            jax.ShapeDtypeStruct((slots, rank_w + 2 * n_state), F32),
            jax.ShapeDtypeStruct((slots, width), F32),
            jax.ShapeDtypeStruct((rank_w, width), F32),
            jax.ShapeDtypeStruct((2, width), F32),
            jax.ShapeDtypeStruct(rate2.shape, F32),
        ],
        scratch_shapes=[pltpu.VMEM(rate2.shape, F32)]
        + [pltpu.VMEM((tb * SUB, LANES), F32)] * 5
        + [pltpu.VMEM((n_state, tb * SUB, LANES), F32)],
        compiler_params=pltpu.CompilerParams(vmem_limit_bytes=56 << 20),
        cost_estimate=small_cost(1 << 20),
        name="scan_backward",
    )(bc, rank, small, act, valid, rate2, gs, states, fold)


def silu_grad(value, sig):
    return sig * (1.0 + value * (1.0 - sig))


def place_blocks(ref, own, other, index):
    chips = own.shape[0]
    rows = ref.shape[0] // (2 * chips)
    core = lax.rem(index, 2)
    for q in range(chips):
        ref[pl.ds(pl.multiple_of((2 * q + core) * rows, rows), rows), :] = own[q, 0:rows, :]
        ref[pl.ds(pl.multiple_of((2 * q + 1 - core) * rows, rows), rows), :] = other[q, 0:rows, :]


def read_row(ref, row, cols):
    base = pl.multiple_of(row // SUB * SUB, SUB)
    rows = ref[pl.ds(base, SUB), cols]
    mine = lax.broadcasted_iota(jnp.int32, rows.shape, 0) == row - base
    return jnp.sum(jnp.where(mine, rows, 0.0), axis=0, keepdims=True)


def add_row(ref, row, value):
    base = pl.multiple_of(row // SUB * SUB, SUB)
    rows = ref[pl.ds(base, SUB), :]
    mine = lax.broadcasted_iota(jnp.int32, rows.shape, 0) == row - base
    ref[pl.ds(base, SUB), :] = rows + jnp.where(mine, value, 0.0)


def split_kernel(n_dp, in_w, gain, out):
    rows = in_w.shape[0]
    n_line, full, width = out.shape
    owned = width // n_dp
    top = jnp.broadcast_to(gain[...].astype(F32), (full - 2 * rows, rows)).astype(in_w.dtype)
    for to in range(n_line):
        for half in range(2):
            for d in range(n_dp):
                at = ((half * n_dp + d) * n_line + to) * owned
                out[to, half * rows : (half + 1) * rows, d * owned : (d + 1) * owned] = in_w[:, at : at + owned]
        out[to, 2 * rows :, :] = jnp.zeros((full - 2 * rows, width), in_w.dtype)
        out[to, 2 * rows :, 0:rows] = top


def split_columns(in_w, gain, n_dp, n_line):
    rows, both = in_w.shape
    width = both // (2 * n_line)
    if width // n_dp % LANES:
        blocks = in_w.reshape(rows, 2, n_dp, n_line, width // n_dp).transpose(3, 1, 0, 2, 4)
        top = jnp.broadcast_to(jnp.pad(gain, (0, width - rows)), (n_line, 16, width))
        return jnp.concatenate([blocks.reshape(n_line, 2 * rows, width), top], axis=1)
    vmem = pl.BlockSpec(memory_space=pltpu.VMEM)
    return pl.pallas_call(
        functools.partial(split_kernel, n_dp),
        in_specs=[vmem] * 2,
        out_specs=vmem,
        out_shape=jax.ShapeDtypeStruct((n_line, 2 * rows + 16, width), in_w.dtype),
        cost_estimate=small_cost(1 << 10),
        name="split_columns",
    )(in_w, gain[None])


def join_kernel(n_dp, inner, gate, in_w, gain, out, gain_out):
    n_line, rows, width = inner.shape
    owned = width // n_dp
    total = jnp.zeros((rows, LANES), F32)
    for half, got in enumerate((inner, gate)):
        for line in range(n_line):
            for d in range(n_dp):
                at = ((half * n_dp + d) * n_line + line) * owned
                block = got[line, :, d * owned : (d + 1) * owned].astype(F32)
                out[:, at : at + owned] = block
                term = block * in_w[:, at : at + owned].astype(F32)
                for low in range(0, owned, LANES):
                    total = total + term[:, low : low + LANES]
    ones = jnp.ones((SUB, LANES), F32)
    sums = lax.dot_general(
        ones, total, (((1,), (1,)), ((), ())), precision=lax.Precision.HIGHEST, preferred_element_type=F32
    )
    gain_out[...] = sums[0:1, :] / gain[...].astype(F32)


def join_columns(inner, gate, in_w, gain, n_dp):
    rows, both = in_w.shape
    n_line, _, width = inner.shape
    if width // n_dp % LANES:
        blocks = jnp.stack([inner, gate]).astype(F32).reshape(2, n_line, rows, n_dp, -1)
        full = blocks.transpose(2, 0, 3, 1, 4).reshape(rows, both)
        return full, jnp.sum(full * in_w.astype(F32), axis=1) / gain.astype(F32)
    vmem = pl.BlockSpec(memory_space=pltpu.VMEM)
    full, gain_grad = pl.pallas_call(
        functools.partial(join_kernel, n_dp),
        in_specs=[vmem] * 4,
        out_specs=[vmem] * 2,
        out_shape=[jax.ShapeDtypeStruct((rows, both), F32), jax.ShapeDtypeStruct((1, rows), F32)],
        cost_estimate=small_cost(1 << 10),
        name="join_columns",
    )(inner, gate, in_w, gain[None])
    return full, gain_grad[0]


def column_block(width, slots):
    return 256 if width % 256 == 0 and slots <= 1024 else LANES


def from_place(place, steps, n_line):
    return lax.rem(place - steps + n_line, n_line)


def outer(kept, sent, right, kept_out, sent_out):
    rows = min(256, kept.shape[1])

    @pl.loop(0, kept.shape[1] // rows)
    def _(r):
        at = pl.ds(pl.multiple_of(r * rows, rows), rows)
        for left, out in ((kept, kept_out), (sent, sent_out)):
            found = lax.dot_general(left[:, at], right[...], (((0,), (0,)), ((), ())), preferred_element_type=F32)
            out[at, :] = found.astype(out.dtype)


def outer_kernel(kept, sent, right, kept_out, sent_out):
    outer(kept, sent, right, kept_out, sent_out)


def outer_product(kept, sent, right):
    shape = (kept.shape[1], right.shape[1])
    vmem = pl.BlockSpec(memory_space=pltpu.VMEM)
    return pl.pallas_call(
        outer_kernel,
        in_specs=[vmem] * 3,
        out_specs=[vmem] * 2,
        out_shape=[jax.ShapeDtypeStruct(shape, BF)] * 2,
        compiler_params=pltpu.CompilerParams(vmem_limit_bytes=48 << 20),
        cost_estimate=small_cost(1 << 20),
        name="outer_product",
    )(kept, sent, right)


def to_shifts(source, outs, place):
    rows = outs[0].shape[0]
    for s, out in enumerate(outs):
        at = pl.multiple_of(lax.rem(place + s, len(outs)) * rows, rows)
        out[...] = source[pl.ds(at, rows), :]


def split_cores(ref, kept, sent, index, n_dp):
    size = ref.shape[1] // n_dp
    core = lax.rem(index, 2)
    for q in range(kept.shape[1] // size):
        cols = slice(q * size, (q + 1) * size)
        kept[:, cols] = ref[:, pl.ds(pl.multiple_of((2 * q + core) * size, size), size)]
        sent[:, cols] = ref[:, pl.ds(pl.multiple_of((2 * q + 1 - core) * size, size), size)]


def project_kernel(n_line, n_dp, at, info, *refs):
    toks, refs = refs[:n_line], refs[n_line:]
    own, other, small, allowed, gain, normed, kept, sent, inner, conv_out, activ, part32, w_nat, ext = refs
    held, model = toks[0].shape
    slots = held * n_line
    width = w_nat.shape[1]
    taps = at.taps
    rim = taps - 1
    rows_dp = model // n_dp
    core = lax.rem(info[0], 2)
    for q in range(n_dp // 2):
        for blocks, d in ((own, 2 * q + core), (other, 2 * q + 1 - core)):
            found = blocks[q, rows_dp:, 0:rows_dp].astype(F32)[0:1, :]
            gain[:, pl.ds(pl.multiple_of(d * rows_dp, rows_dp), rows_dp)] = found
    step = 32
    for s, tok in enumerate(toks):
        base = from_place(info[1], s, n_line) * held

        @pl.loop(0, held // step)
        def _(i):
            x = tok[pl.ds(pl.multiple_of(i * step, step), step), :].astype(F32)
            scale = lax.rsqrt(jnp.mean(x * x, axis=1, keepdims=True) + EPS)
            normed[pl.ds(pl.multiple_of(base + i * step, step), step), :] = (x * scale * gain[...]).astype(BF)

    split_cores(normed, kept, sent, info[0], n_dp)
    place_blocks(w_nat, own, other, info[0])
    cb = column_block(width, slots)

    @pl.loop(0, width // cb)
    def _(c):
        cols = pl.ds(pl.multiple_of(c * cb, cb), cb)
        inner[:, cols] = jnp.dot(normed[...], w_nat[:, cols], preferred_element_type=F32)
        vectors = small[at.rest, cols].astype(F32)
        for f in range(n_line):
            rows = slice(f * held, (f + 1) * held)
            ext[SUB : SUB + held, :] = inner[rows, cols]
            for k in range(1, rim + 1):
                if f == 0:
                    ext[SUB - k : SUB - k + 1, :] = jnp.zeros((1, cb), F32)
                else:
                    ext[SUB - k : SUB - k + 1, :] = read_row(inner, (f - 1) * held + info[1 + f] - k, cols)
            total = vectors[taps : taps + 1, :]
            for lag in range(taps):
                tapped = ext[SUB - lag : SUB - lag + held, :]
                total = total + vectors[rim - lag : rim - lag + 1, :] * tapped * allowed[rows, lag : lag + 1]
            conv_out[rows, cols] = total
            activ[rows, cols] = (total * jax.nn.sigmoid(total)).astype(BF)

    part32[...] = lax.dot_general(
        activ[...], small[at.x_t, :], (((1,), (1,)), ((), ())), preferred_element_type=F32
    )


def project(info, n_line, n_dp, toks, own, other, at, small, allowed):
    held, model = toks[0].shape
    slots = held * n_line
    width, proj = small.shape[1], at.x_t.stop - at.x_t.start
    vmem = pl.BlockSpec(memory_space=pltpu.VMEM)
    shapes = [
        ((1, model), F32), ((slots, model), BF), ((slots, model // 2), BF), ((slots, model // 2), BF),
        ((slots, width), F32), ((slots, width), F32), ((slots, width), BF), ((slots, proj), F32), ((model, width), BF),
    ]
    return pl.pallas_call(
        functools.partial(project_kernel, n_line, n_dp, at),
        in_specs=[pl.BlockSpec(memory_space=pltpu.SMEM)] + [vmem] * (4 + len(toks)),
        out_specs=[vmem] * len(shapes),
        out_shape=[jax.ShapeDtypeStruct(s, t) for s, t in shapes],
        scratch_shapes=[pltpu.VMEM((SUB + slots // n_line, column_block(width, slots)), F32)],
        compiler_params=pltpu.CompilerParams(vmem_limit_bytes=56 << 20),
        cost_estimate=small_cost(1 << 20),
        name="project",
    )(info, *toks, own, other, small, allowed)


def gate_kernel(n_line, n_dp, at, info, own, other, normed, y, act, small, *refs):
    out_own, out_other, refs = refs[: n_dp // 2], refs[n_dp // 2 : n_dp], refs[n_dp:]
    branches, refs = refs[:n_line], refs[n_line:]
    gate, gated, w_nat, o_nat, *halves, branch = refs
    slots, width = y.shape
    model = normed.shape[1]
    place_blocks(w_nat, own, other, info[0])
    rows = width // n_dp
    core, chip = lax.rem(info[0], 2), lax.div(info[0], 2)
    for u in range(n_dp // 2):
        first = 2 * jnp.bitwise_xor(chip, u)
        o_nat[pl.ds(pl.multiple_of((first + core) * rows, rows), rows), :] = out_own[u][0:rows, :]
        o_nat[pl.ds(pl.multiple_of((first + 1 - core) * rows, rows), rows), :] = out_other[u][0:rows, :]
    cb = column_block(width, slots)

    @pl.loop(0, width // cb)
    def _(c):
        cols = pl.ds(pl.multiple_of(c * cb, cb), cb)
        value = jnp.dot(normed[...], w_nat[:, cols], preferred_element_type=F32)
        gate[:, cols] = value
        skip = small[at.rest, cols].astype(F32)[at.taps + 2 : at.taps + 3, :]
        scan_out = y[:, cols] + skip * act[:, cols].astype(F32)
        gated[:, cols] = (scan_out * value * jax.nn.sigmoid(value)).astype(BF)

    mb = column_block(model, slots)

    @pl.loop(0, model // mb)
    def _(c):
        cols = pl.ds(pl.multiple_of(c * mb, mb), mb)
        branch[:, cols] = jnp.dot(gated[...], o_nat[:, cols], preferred_element_type=F32).astype(BF)

    to_shifts(branch, branches, info[1])
    if halves:
        split_cores(gated, *halves, info[0], n_dp)


def gate_block(info, n_line, n_dp, own, other, out_own, out_other, normed, y, act, at, small):
    slots, width = y.shape
    model = normed.shape[1]
    vmem = pl.BlockSpec(memory_space=pltpu.VMEM)
    shapes = [((slots // n_line, model), BF)] * n_line
    shapes += [((slots, width), F32), ((slots, width), BF), ((model, width), BF), ((width, model), BF)]
    if width // n_dp % LANES == 0:
        shapes += [((slots, width // 2), BF)] * 2
    outs = pl.pallas_call(
        functools.partial(gate_kernel, n_line, n_dp, at),
        in_specs=[pl.BlockSpec(memory_space=pltpu.SMEM)] + [vmem] * (6 + n_dp),
        out_specs=[vmem] * len(shapes),
        out_shape=[jax.ShapeDtypeStruct(s, t) for s, t in shapes],
        scratch_shapes=[pltpu.VMEM((slots, model), BF)],
        compiler_params=pltpu.CompilerParams(vmem_limit_bytes=58 << 20),
        cost_estimate=small_cost(1 << 20),
        name="gate_block",
    )(info, own, other, normed, y, act, small, *out_own, *out_other)
    branches, (gate, gated, w_nat, o_nat), halves = list(outs[:n_line]), outs[n_line : n_line + 4], outs[n_line + 4 :]
    return branches, gate, w_nat, o_nat, *(halves or cores(gated, 1))


def gate_back_kernel(n_line, at, info, *refs):
    cots, refs = refs[:n_line], refs[n_line:]
    o_nat, gate, y, act, small, valid, normed_k, normed_s, gs, grad_gate, dout, gate_k, gate_s = refs
    slots, width = y.shape
    held, model = cots[0].shape
    for s, cot in enumerate(cots):
        rows = pl.ds(pl.multiple_of(from_place(info[1], s, n_line) * held, held), held)
        dout[rows, :] = (cot[...].astype(F32) * valid[rows, :]).astype(BF)

    cb = column_block(width, slots)

    @pl.loop(0, width // cb)
    def _(c):
        cols = pl.ds(pl.multiple_of(c * cb, cb), cb)
        grad = lax.dot_general(dout[...], o_nat[cols, :], (((1,), (1,)), ((), ())), preferred_element_type=F32)
        value = gate[:, cols]
        sig = jax.nn.sigmoid(value)
        skip = small[at.rest, cols].astype(F32)[at.taps + 2 : at.taps + 3, :]
        scan_out = y[:, cols] + skip * act[:, cols].astype(F32)
        gs[:, cols] = grad * value * sig
        grad_gate[:, cols] = (grad * scan_out * silu_grad(value, sig)).astype(BF)

    outer(normed_k, normed_s, grad_gate, gate_k, gate_s)


def gate_back(info, n_line, cots, o_nat, gate, y, act, at, small, valid, normed_k, normed_s):
    slots, width = y.shape
    model = o_nat.shape[1]
    vmem = pl.BlockSpec(memory_space=pltpu.VMEM)
    shapes = [((slots, width), F32), ((slots, width), BF), ((slots, model), BF)]
    shapes += [((model // 2, width), BF)] * 2
    return pl.pallas_call(
        functools.partial(gate_back_kernel, n_line, at),
        in_specs=[pl.BlockSpec(memory_space=pltpu.SMEM)] + [vmem] * (8 + len(cots)),
        out_specs=[vmem] * len(shapes),
        out_shape=[jax.ShapeDtypeStruct(s, t) for s, t in shapes],
        compiler_params=pltpu.CompilerParams(vmem_limit_bytes=58 << 20),
        cost_estimate=small_cost(1 << 20),
        name="gate_back",
    )(info, *cots, o_nat, gate, y, act, small, valid, normed_k, normed_s)


def together(slots):
    return slots <= 1024


def conv_back_kernel(n_line, n_dp, at, info, gp, gu, small, act, conv_out, inner, allowed, dtw, rate_grad, scan_vec,
                     w_nat, normed_gate, *refs):
    halves, refs = (refs[:2], refs[2:]) if together(gu.shape[0]) else ((), refs)
    grads, refs = refs[:n_line], refs[n_line:]
    gi_low, kept, sent, *products, x_grad, vec, ext, gi, tail, grad_normed, column = refs
    slots, width = gu.shape
    held = slots // n_line
    taps = at.taps
    rim = taps - 1
    cb = column_block(width, slots)
    x_grad[...] = lax.dot_general(gp[...], act[...], (((0,), (0,)), ((), ())), preferred_element_type=F32)
    vec[...] = jnp.zeros_like(vec)
    for lag in range(taps):
        tail[lag, held : held + SUB, :] = jnp.zeros((SUB, cb), F32)

    @pl.loop(0, width // cb)
    def _(c):
        cols = pl.ds(pl.multiple_of(c * cb, cb), cb)
        vectors = small[at.rest, cols].astype(F32)
        for f in range(n_line - 1, -1, -1):
            rows = slice(f * held, (f + 1) * held)
            ext[SUB : SUB + held, :] = inner[rows, cols]
            for k in range(1, rim + 1):
                if f == 0:
                    ext[SUB - k : SUB - k + 1, :] = jnp.zeros((1, cb), F32)
                else:
                    ext[SUB - k : SUB - k + 1, :] = read_row(inner, (f - 1) * held + info[1 + f] - k, cols)
            grad = gu[rows, cols] + jnp.dot(gp[rows, :], small[at.x_t, cols], preferred_element_type=F32)
            co = conv_out[rows, cols]
            grad = grad * silu_grad(co, jax.nn.sigmoid(co))
            vec[taps : taps + 1, cols] += jnp.sum(grad, axis=0, keepdims=True)
            for lag in range(taps):
                weighted = grad * allowed[rows, lag : lag + 1]
                vec[rim - lag : rim - lag + 1, cols] += jnp.sum(
                    weighted * ext[SUB - lag : SUB - lag + held, :], axis=0, keepdims=True
                )
                tail[lag, 0:held, :] = weighted * vectors[rim - lag : rim - lag + 1, :]
            total = tail[0, 0:held, :]
            for lag in range(1, taps):
                total = total + tail[lag, lag : lag + held, :]
            gi[rows, :] = total
            if f + 1 < n_line:
                for k in range(1, rim + 1):
                    add_row(gi, f * held + info[2 + f] - k, gi[slots + k : slots + k + 1, :])
            for k in range(1, rim + 1):
                row = tail[k, 0:1, :]
                for lag in range(k + 1, taps):
                    row = row + tail[lag, lag - k : lag - k + 1, :]
                gi[slots + k : slots + k + 1, :] = row
        gi_low[:, cols] = gi[0:slots, :].astype(BF)

    model = w_nat.shape[0]
    mb = column_block(model, slots)

    @pl.loop(0, model // mb)
    def _(c):
        cols = pl.ds(pl.multiple_of(c * mb, mb), mb)
        found = lax.dot_general(gi_low[...], w_nat[cols, :], (((1,), (1,)), ((), ())), preferred_element_type=F32)
        grad_normed[:, cols] = (found + normed_gate[:, cols]).astype(BF)

    to_shifts(grad_normed, grads, info[1])
    if halves:
        outer(*halves, gi_low, *products)
    vec[taps + 1 : taps + 3, :] = scan_vec[...]
    owned = width // n_dp
    if kept.shape[0] == 1:
        kept[0, at.dt_w, :], kept[0, at.x_t, :], kept[0, at.a_t, :], kept[0, at.rest, :] = (
            dtw[...], x_grad[...], rate_grad[...], vec[...]
        )
        return
    core = lax.rem(info[0], 2)
    fold = kept.shape[1]
    for q in range(n_dp // 2):
        for ref, d in ((kept, 2 * q + core), (sent, 2 * q + 1 - core)):
            cols = pl.ds(pl.multiple_of(d * owned, owned), owned)
            for rows, source in ((at.dt_w, dtw), (at.x_t, x_grad), (at.a_t, rate_grad), (at.rest, vec)):
                column[rows, :] = source[:, cols]
            for b in range(width // owned):
                ref[q, :, b * owned : (b + 1) * owned] = column[b * fold : (b + 1) * fold, :].astype(ref.dtype)


def conv_back(info, n_line, n_dp, gp, gu, at, small, act, conv_out, inner, allowed, dtw, rate_grad, scan_vec, w_nat, normed_gate,
              normed_k, normed_s):
    slots, width = gu.shape
    held = slots // n_line
    cb = column_block(width, slots)
    owned = width // n_dp
    tiles = owned % LANES == 0
    vmem = pl.BlockSpec(memory_space=pltpu.VMEM)
    fold = at.fold(n_dp)
    shape = (n_dp // 2, fold, width) if tiles else (1, at.rows, width)
    model = w_nat.shape[0]
    halves = [normed_k, normed_s] if together(slots) else []
    outs = pl.pallas_call(
        functools.partial(conv_back_kernel, n_line, n_dp, at),
        in_specs=[pl.BlockSpec(memory_space=pltpu.SMEM)] + [vmem] * (12 + len(halves)),
        out_specs=[vmem] * (n_line + 3 + len(halves)),
        out_shape=[jax.ShapeDtypeStruct((held, model), BF)] * n_line
        + [
            jax.ShapeDtypeStruct((slots, width), BF),
            jax.ShapeDtypeStruct(shape, F32),
            jax.ShapeDtypeStruct(shape if tiles else (SUB, LANES), BF if tiles else F32),
        ]
        + [jax.ShapeDtypeStruct((model // 2, width), BF)] * len(halves),
        scratch_shapes=[
            pltpu.VMEM((at.x_t.stop - at.x_t.start, width), F32),
            pltpu.VMEM((16, width), F32),
            pltpu.VMEM((SUB + held, cb), F32),
            pltpu.VMEM((slots + SUB, cb), F32),
            pltpu.VMEM((at.taps, held + SUB, cb), F32),
            pltpu.VMEM((slots, model), BF),
            pltpu.VMEM((n_dp * fold, owned), F32),
        ],
        compiler_params=pltpu.CompilerParams(vmem_limit_bytes=58 << 20),
        cost_estimate=small_cost(1 << 20),
        name="conv_back",
    )(info, gp, gu, small, act, conv_out, inner, allowed, dtw, rate_grad, scan_vec, w_nat, normed_gate, *halves)
    grads, (gi_low, kept, sent, *products) = outs[:n_line], outs[n_line:]
    if not products:
        products = outer_product(normed_k, normed_s, gi_low)
    if not tiles:
        kept, sent = [
            part.reshape(at.rows, n_dp // 2, owned).transpose(1, 0, 2) for part in cores(kept[0], 1)
        ]
    return list(grads), *products, kept, sent.astype(BF)


def swap(value, axis, mask):
    count = lax.axis_size(axis)
    return lax.ppermute(value, axis, [(i, i ^ mask) for i in range(count)])


def shift(value, axis, steps):
    count = lax.axis_size(axis)
    return lax.ppermute(value, axis, [(i, (i + steps) % count) for i in range(count)])


def chips_of(axis):
    return [list(range(core, lax.axis_size(axis), 2)) for core in range(2)]


def to_line(blocks):
    return lax.all_to_all(blocks, "fsdp", 0, 0)


def to_chips(blocks):
    return lax.all_to_all(blocks, "dp", 0, 0, axis_index_groups=chips_of("dp"))


def repeated(value, count):
    return jnp.broadcast_to(value[None], (count,) + value.shape)


def in_order(parts, axis):
    count, me = lax.axis_size(axis), lax.axis_index(axis)
    up = jnp.stack([parts[-k % count] for k in range(count)] * 2)
    return lax.dynamic_slice_in_dim(up, lax.rem(count - me, count), count, 0)


def by_chip(parts):
    chip, count = lax.div(lax.axis_index("dp"), 2), len(parts)
    bits = count.bit_length() - 1
    cube = jnp.stack(parts).reshape((2,) * bits + parts[0].shape)
    for place in range(bits):
        mine = lax.rem(chip >> (bits - 1 - place), 2) == 1
        cube = jnp.where(mine, jnp.flip(cube, place), cube)
    return cube.reshape((count,) + parts[0].shape)


def by_device(own, other):
    core = lax.rem(lax.axis_index("dp"), 2) == 1
    both = jnp.where(core, jnp.stack([other, own], axis=1), jnp.stack([own, other], axis=1))
    return lax.optimization_barrier(both.reshape((-1,) + own.shape[1:]))


def total_line(value):
    reach = 1
    while reach < lax.axis_size("fsdp"):
        value = value + swap(value.astype(BF), "fsdp", reach).astype(F32)
        reach *= 2
    return value


def fence(*values):
    flat, shape = jax.tree.flatten(values)
    return jax.tree.unflatten(shape, lax.optimization_barrier(tuple(flat)))


def cores(value, axis):
    cut = value.shape[:axis] + (lax.axis_size("dp") // 2, 2, -1) + value.shape[axis + 1 :]
    cube = value.reshape(cut)
    core = lax.rem(lax.axis_index("dp"), 2)
    found = [lax.dynamic_index_in_dim(cube, at, axis + 1, keepdims=False) for at in (core, 1 - core)]
    flat = value.shape[:axis] + (value.shape[axis] // 2,) + value.shape[axis + 1 :]
    return [part.reshape(flat) for part in found]


def add_core_kernel(kept, got, *refs):
    *small, out = refs
    chips, rows, width = out.shape
    whole = kept.shape[0] // chips

    @pl.loop(0, chips)
    def _(q):
        at = pl.ds(pl.multiple_of(q * whole, whole), whole)
        out[q, 0:whole, :] = (kept[at, :].astype(F32) + got[at, :].astype(F32)).astype(BF)
        if small:
            out[q, whole:rows, :] = (small[0][q] + small[1][q].astype(F32)).astype(BF)


def add_core(kept, got, *small):
    chips = lax.axis_size("dp") // 2
    rows = kept.shape[0] // chips + (small[0].shape[1] if small else 0)
    vmem = pl.BlockSpec(memory_space=pltpu.VMEM)
    return pl.pallas_call(
        add_core_kernel,
        in_specs=[vmem] * (2 + len(small)),
        out_specs=vmem,
        out_shape=jax.ShapeDtypeStruct((chips, rows, kept.shape[1]), BF),
        compiler_params=pltpu.CompilerParams(vmem_limit_bytes=32 << 20),
        cost_estimate=small_cost(1 << 10),
        name="add_core",
    )(kept, got, *small)


def add_chips(blocks):
    return jnp.sum(to_chips(blocks.astype(BF)).astype(F32), axis=0)


def add_chips_near(blocks):
    count, chip = lax.axis_size("dp") // 2, lax.div(lax.axis_index("dp"), 2)
    total = lax.dynamic_index_in_dim(blocks, chip, 0, keepdims=False)
    for u in range(1, count):
        total = total + far(blocks, u).astype(F32)
    return total


def sent_far(blocks, u):
    chip = lax.div(lax.axis_index("dp"), 2)
    return lax.dynamic_index_in_dim(blocks, jnp.bitwise_xor(chip, u), 0, keepdims=False).astype(BF)


def far(blocks, u):
    return swap(sent_far(blocks, u), "dp", 2 * u)


def contract_cols(left, right):
    return lax.dot_general(left, right, (((1,), (1,)), ((), ())), preferred_element_type=F32)


def per_device(
    tokens, counts, lengths, gain, in_weight, conv_weight, conv_bias, x_weight,
    dt_weight, dt_bias, a_log, skip, out_weight, cotangent,
):
    n_dp, n_line = lax.axis_size("dp"), lax.axis_size("fsdp")
    group, place = lax.axis_index("dp"), lax.axis_index("fsdp")
    held_slots, model = tokens.shape
    slots = held_slots * n_line
    owned = skip.shape[0]
    width = owned * n_dp
    in_rows = in_weight.shape[0]
    taps, rank_w, n_state = conv_weight.shape[0], dt_weight.shape[0], a_log.shape[1]
    proj = x_weight.shape[1]
    tb = 64 if slots % 64 == 0 else slots

    count_row = lax.dynamic_index_in_dim(counts, group, 0, keepdims=False)
    length_row = lax.dynamic_index_in_dim(lengths, group, 0, keepdims=False)
    info = jnp.concatenate([jnp.stack([group, place]).astype(jnp.int32), count_row])
    offsets = jnp.cumsum(count_row) - count_row
    within = lax.broadcasted_iota(jnp.int32, (n_line, held_slots), 1)
    present = within < count_row[:, None]
    position = offsets[:, None] + within
    second, third = length_row[0], length_row[0] + length_row[1]
    begin = jnp.where(position >= third, third, jnp.where(position >= second, second, 0))
    marks = jnp.stack(
        [position - lag >= begin for lag in range(taps)] + [present, present & (position == begin)]
    ).astype(F32).reshape(taps + 2, slots).T
    allowed, valid, opens = marks[:, :taps], marks[:, taps : taps + 1], marks[:, taps + 1 :] * FAR

    own_tokens, own_cot = tokens, cotangent
    steps = range(1, n_line)
    chips = range(1, n_dp // 2)
    at = Small(rank_w, proj, n_state, taps)

    parts = split_columns(in_weight, gain, n_dp, n_line)
    rest = jnp.concatenate([conv_weight, conv_bias[None], dt_bias[None], skip[None]], axis=0)
    rest = jnp.pad(rest, ((0, 16 - rest.shape[0]), (0, 0)))
    small = jnp.concatenate([dt_weight, x_weight.T, a_log.T, rest], axis=0)
    small_rows = -(-at.rows * owned // model)
    small_rows += -small_rows % 16
    small = jnp.pad(small, ((0, small_rows * model // owned - at.rows), (0, 0))).reshape(small_rows, model)
    packed = jnp.concatenate([out_weight, small], axis=0)
    parts, tokens = fence(parts, tokens)
    parts = to_line(parts)
    toks = {0: tokens, 1: shift(tokens, "fsdp", 1)}
    near = [packed] + [swap(packed, "dp", 2 * u) for u in chips]
    parts, toks, near, info, allowed, valid, opens = fence(parts, toks, near, info, allowed, valid, opens)

    gain_rows = jnp.pad(parts[:, 2 * in_rows, :in_rows].reshape(1, -1), ((0, 15), (0, width - n_line * in_rows)))
    inner_block = jnp.concatenate([parts[:, :in_rows].reshape(-1, width), gain_rows], axis=0)
    gate_in = parts[:, in_rows : 2 * in_rows].reshape(-1, width)
    inner_rep, gate_in, toks = fence(repeated(inner_block, n_dp // 2), gate_in, toks)
    inner_own = to_chips(inner_rep)
    for s in steps[1:]:
        toks[s] = shift(toks[0], "fsdp", s)
    gate_rep = repeated(gate_in, n_dp // 2)
    small = by_chip([block[owned:].reshape(-1, owned)[: at.rows] for block in near])
    small_other = swap(small, "dp", 1)
    inner_own, toks, near, gate_rep, cotangent, small, small_other = fence(
        inner_own, toks, near, gate_rep, cotangent, small, small_other
    )

    inner_other = swap(inner_own, "dp", 1)
    small = by_device(small, small_other).transpose(1, 0, 2).reshape(-1, width)
    inner_own, inner_other, toks, cotangent, near, small = fence(inner_own, inner_other, toks, cotangent, near, small)
    rates = -jnp.exp(small[at.a_t].astype(F32))
    chunks = width // LANES
    rate2 = jnp.pad(
        (rates * (1.0 / LN2)).reshape(n_state, chunks, LANES), ((0, 0), (0, SUB - chunks), (0, 0))
    ).reshape(n_state * SUB, LANES)

    gate_own = to_chips(gate_rep)
    cots = {0: cotangent, 1: shift(cotangent, "fsdp", 1)}
    full_gain, normed, normed_kept, normed_sent, inner, conv_out, activ, part, inner_nat = project(
        info, n_line, n_dp, [toks[s] for s in range(n_line)], inner_own, inner_other, at, small, allowed
    )
    part, rate2, cots, near, gate_own = fence(part, rate2, cots, near, gate_own)

    projected = total_line(part)
    out_near, out_other = near, [swap(block, "dp", 1) for block in near]
    projected, cots, out_near, out_other = fence(projected, cots, out_near, out_other)

    gate_other = swap(gate_own, "dp", 1)
    for s in steps[1:]:
        cots[s] = shift(cots[0], "fsdp", s)
    rank_low = projected[:, :rank_w].astype(BF)
    bc = jnp.concatenate([projected[:, rank_w:], opens], axis=1)
    scanned, states = scan_forward(at, bc, rank_low, small, activ, valid, rate2, tb)
    scanned, gate_own, gate_other, cots[n_line - 1] = fence(scanned, gate_own, gate_other, cots[n_line - 1])

    branches, gate, gate_nat, out_nat, *gated = gate_block(
        info, n_line, n_dp, gate_own, gate_other, out_near, out_other, normed, scanned, activ, at, small
    )
    branches, gate, gated, gate_nat, out_nat, cots = fence(branches, gate, gated, gate_nat, out_nat, cots)

    branches[1] = shift(branches[1], "fsdp", 1)
    grad_scan, grad_gate, dout, gate_kept, gate_sent = gate_back(
        info, n_line, [cots[s] for s in range(n_line)], out_nat, gate, scanned, activ, at, small, valid,
        normed_kept, normed_sent,
    )
    branches, grad_scan, grad_gate, dout, gated, gate_kept, gate_sent = fence(
        branches, grad_scan, grad_gate, dout, gated, gate_kept, gate_sent
    )
    gate_grad = add_core(gate_kept, swap(gate_sent, "dp", 1))
    gate_grad, grad_scan, branches = fence(gate_grad, grad_scan, branches)

    gate_rows = add_chips(gate_grad).astype(BF)
    for s in steps[1:]:
        branches[s] = shift(branches[s], "fsdp", s)
    part, grad_u, dt_w_grad, vectors, rate_sum = scan_backward(
        at, bc, rank_low, small, activ, valid, rate2, grad_scan, states, tb
    )
    part, branches, gated, dout, grad_gate, rate_sum, gate_rows = fence(
        part, branches, gated, dout, grad_gate, rate_sum, gate_rows
    )

    out_kept, out_sent = outer_product(*gated, dout)
    reach = 1
    while reach < n_line:
        part = part + swap(part.astype(BF), "fsdp", reach).astype(F32)
        reach *= 2
        if reach == 2:
            part, out_kept, out_sent, grad_gate = fence(part, out_kept, out_sent, grad_gate)
            out_got = swap(out_sent, "dp", 1)
            normed_gate = contract_cols(grad_gate, gate_nat)
    rate_grad = rate_sum.reshape(n_state, SUB, LANES)[:, :chunks].reshape(n_state, width) * rates
    grad_projected, out_kept, out_got, normed_gate, rate_grad, gate_rows = fence(
        part.astype(BF), out_kept, out_got, normed_gate, rate_grad, gate_rows
    )

    gate_got = to_line(gate_rows.reshape(n_line, in_rows, width))
    out_grad = add_core(out_kept, out_got)
    grads, inner_kept, inner_sent, small_kept, small_sent = conv_back(
        info, n_line, n_dp, grad_projected, grad_u, at, small, activ, conv_out, inner, allowed,
        dt_w_grad, rate_grad, vectors, inner_nat, normed_gate, normed_kept, normed_sent,
    )
    out_far = {u: sent_far(out_grad, u) for u in chips}
    grads, gate_got, inner_kept, inner_sent, small_kept, small_sent, out_grad, out_far = fence(
        grads, gate_got, inner_kept, inner_sent, small_kept, small_sent, out_grad, out_far
    )

    folded = owned % LANES == 0
    grads[1] = shift(grads[1], "fsdp", 1)
    for u in chips[2:]:
        out_far[u] = swap(out_far[u], "dp", 2 * u)
    inner_got, small_got = swap(inner_sent, "dp", 1), swap(small_sent, "dp", 1)
    inner_grad = add_core(inner_kept, inner_got, *((small_kept, small_got) if folded else ()))
    inner_grad, grads, small_kept, small_got, out_grad, out_far, branches = fence(
        inner_grad, grads, small_kept, small_got, out_grad, out_far, branches
    )

    got = to_chips(inner_grad)
    inner_rows = jnp.sum(got[:, : n_line * in_rows].astype(F32), axis=0).astype(BF)
    small_sum = jnp.sum(got[:, n_line * in_rows :].astype(F32), axis=0)
    for s in steps[1:]:
        grads[s] = shift(grads[s], "fsdp", s)
    inner_rows, small_sum, grads, small_kept, small_got, out_grad, out_far, branches = fence(
        inner_rows, small_sum, grads, small_kept, small_got, out_grad, out_far, branches
    )

    inner_got = to_line(inner_rows.reshape(n_line, in_rows, width))
    for u in chips[:2]:
        out_far[u] = swap(out_far[u], "dp", 2 * u)
    grad_normed = sum(p.astype(F32) for p in grads)
    grad_normed, small_sum, small_kept, small_got, branches = fence(
        grad_normed, small_sum, small_kept, small_got, branches
    )
    out_weight_grad = lax.dynamic_index_in_dim(out_grad, lax.div(group, 2), 0, keepdims=False).astype(F32)
    out_weight_grad = out_weight_grad + sum(out_far[u].astype(F32) for u in chips)
    if folded:
        small_grads = small_sum.reshape(-1, n_dp, owned).transpose(1, 0, 2).reshape(-1, owned)
    else:
        small_grads = add_chips_near(small_kept + small_got.astype(F32))
    own_valid = lax.dynamic_slice_in_dim(valid, place * held_slots, held_slots, 0)
    own_f = own_tokens.astype(F32)
    output = (own_f + own_valid * sum(p.astype(F32) for p in branches)).astype(BF)
    own_scale = lax.rsqrt(jnp.mean(own_f * own_f, axis=1, keepdims=True) + EPS)
    unit = own_f * own_scale
    grad_unit = grad_normed * full_gain
    token_grad = own_cot.astype(F32) + own_scale * (
        grad_unit - unit * jnp.mean(grad_unit * unit, axis=1, keepdims=True)
    )
    dt_g, x_g, a_g = small_grads[at.dt_w], small_grads[at.x_t], small_grads[at.a_t]
    tail_g = small_grads[at.rest]
    conv_g, conv_b_g, dt_b_g, skip_g = tail_g[:taps], tail_g[taps : taps + 1], tail_g[taps + 1 : taps + 2], tail_g[taps + 2 : taps + 3]
    in_weight_grad, gain_grad = join_columns(inner_got, gate_got, in_weight, gain, n_dp)
    return (
        output, token_grad, gain_grad, in_weight_grad, conv_g, conv_b_g[0], x_g.T, dt_g, dt_b_g[0], a_g.T,
        skip_g[0], out_weight_grad,
    )


def solution(mesh):
    both = ("dp", "fsdp")
    rows, cols, vec = P(both, None), P(None, both), P(both)
    return jax.shard_map(
        per_device,
        mesh=mesh,
        in_specs=(rows, P(), P(), vec, rows, cols, vec, rows, cols, vec, rows, vec, rows, rows),
        out_specs=(rows, rows, vec, rows, cols, vec, rows, cols, vec, rows, vec, rows),
        check_vma=False,
    )
```

```python
import functools

import jax
import jax.numpy as jnp
from jax import lax
from jax.experimental import pallas as pl
from jax.experimental.pallas import tpu as pltpu
from jax.sharding import PartitionSpec as P

BF, F32 = jnp.bfloat16, jnp.float32
LANES, SUB = 128, 8
LN2 = 0.6931471805599453
FAR = 1.0e5
EPS = 1e-5


def small_cost(flops):
    return pl.CostEstimate(flops=flops, bytes_accessed=1 << 16, transcendentals=0)


class Small:
    def __init__(self, rank, proj, state, taps):
        self.dt_w = slice(0, rank)
        self.x_t = slice(rank, rank + proj)
        self.a_t = slice(rank + proj, rank + proj + state)
        self.rest = slice(rank + proj + state, rank + proj + state + 16)
        self.taps, self.rows = taps, rank + proj + state + 16

    def fold(self, parts):
        rows = -(-self.rows // parts)
        return rows + -rows % 16

    def vector(self, ref, at):
        return ref[self.rest, :].astype(F32)[at : at + 1, :]


def contract_cols(left, right):
    return lax.dot_general(left, right, (((1,), (1,)), ((), ())), preferred_element_type=F32)


def scatter_lanes(ref, value, rows):
    for k in range(value.shape[1] // LANES):
        ref[pl.ds(k, rows, stride=SUB), :] = value[:, k * LANES : (k + 1) * LANES]


def gather_lanes(ref, width, rows):
    return jnp.concatenate(
        [ref[pl.ds(k, rows, stride=SUB), :] for k in range(width // LANES)], axis=1
    )


def softplus(v):
    return jnp.maximum(v, 0.0) + jnp.log1p(jnp.exp(-jnp.abs(v)))


def forward_kernel(at, bc, rank, small, act, valid, rate2, y_out, states, h_ref, dt_s, dtu_s, y_s):
    tb, width = act.shape
    n_state = rate2.shape[0] // SUB

    @pl.when(pl.program_id(0) == 0)
    def _():
        h_ref[...] = jnp.zeros_like(h_ref)
        if width < SUB * LANES:
            dt_s[...] = jnp.zeros_like(dt_s)
            dtu_s[...] = jnp.zeros_like(dtu_s)

    dt_b = at.vector(small, at.taps + 1)
    pre = jnp.dot(rank[...], small[at.dt_w, :], preferred_element_type=F32) + dt_b
    dt = softplus(pre) * valid[...]
    scatter_lanes(dt_s, dt, tb)
    scatter_lanes(dtu_s, dt * act[...].astype(F32), tb)
    rates = [rate2[n * SUB : (n + 1) * SUB, :] for n in range(n_state)]
    first = [h_ref[n * SUB : (n + 1) * SUB, :] for n in range(n_state)]
    for n in range(n_state):
        states[0, n, 0:SUB, :] = first[n]

    def token(t, h):
        at = pl.multiple_of(t * SUB, SUB)
        dt_t = dt_s[pl.ds(at, SUB), :] + bc[t, 2 * n_state]
        dtu_t = dtu_s[pl.ds(at, SUB), :]
        new, parts = [], [None, None]
        for n in range(n_state):
            hn = jnp.exp2(dt_t * rates[n]) * h[n] + dtu_t * bc[t, n]
            states[0, n, pl.ds(at + SUB, SUB), :] = hn
            term = hn * bc[t, n_state + n]
            parts[n % 2] = term if parts[n % 2] is None else parts[n % 2] + term
            new.append(hn)
        y_s[pl.ds(at, SUB), :] = parts[0] + parts[1]
        return tuple(new)

    last = lax.fori_loop(0, tb, token, tuple(first), unroll=8)
    for n in range(n_state):
        h_ref[n * SUB : (n + 1) * SUB, :] = last[n]
    y_out[...] = gather_lanes(y_s, width, tb)


def scan_forward(at, bc, rank, small, act, valid, rate2, tb):
    slots, width = act.shape
    n_state = rate2.shape[0] // SUB
    nb = slots // tb
    whole = lambda i: (0, 0)
    row = lambda i: (i, 0)
    return pl.pallas_call(
        functools.partial(forward_kernel, at),
        grid=(nb,),
        in_specs=[
            pl.BlockSpec((tb, bc.shape[1]), row, memory_space=pltpu.SMEM),
            pl.BlockSpec((tb, rank.shape[1]), row),
            pl.BlockSpec(small.shape, whole),
            pl.BlockSpec((tb, width), row),
            pl.BlockSpec((tb, 1), row),
            pl.BlockSpec(rate2.shape, whole),
        ],
        out_specs=[
            pl.BlockSpec((tb, width), row),
            pl.BlockSpec((1, n_state, (tb + 1) * SUB, LANES), lambda i: (i, 0, 0, 0)),
        ],
        out_shape=[
            jax.ShapeDtypeStruct((slots, width), F32),
            jax.ShapeDtypeStruct((nb, n_state, (tb + 1) * SUB, LANES), F32),
        ],
        scratch_shapes=[pltpu.VMEM(rate2.shape, F32)] + [pltpu.VMEM((tb * SUB, LANES), F32)] * 3,
        compiler_params=pltpu.CompilerParams(vmem_limit_bytes=61 << 20),
        cost_estimate=small_cost(1 << 20),
        name="scan_forward",
    )(bc, rank, small, act, valid, rate2)


def backward_kernel(
    at_small, bc, rank, small, act, valid, rate2, gs, states,
    packed_out, gu_out, dtw_out, vec_out, rate_out,
    part_s, g_ref, dt_s, dtu_s, gs_s, gdt_s, ab_s, both_s, sums,
):
    tb, width = act.shape
    n_state = rate2.shape[0] // SUB
    part = 4

    @pl.when(pl.program_id(0) == 0)
    def _():
        g_ref[...] = jnp.zeros_like(g_ref)
        rate_out[...] = jnp.zeros_like(rate_out)
        vec_out[...] = jnp.zeros_like(vec_out)
        dtw_out[...] = jnp.zeros_like(dtw_out)
        if width < SUB * LANES:
            for ref in (dt_s, dtu_s, gs_s):
                ref[...] = jnp.zeros_like(ref)

    u = act[...].astype(F32)
    ok = valid[...]
    dt_b, skip = at_small.vector(small, at_small.taps + 1), at_small.vector(small, at_small.taps + 2)
    pre = jnp.dot(rank[...], small[at_small.dt_w, :], preferred_element_type=F32) + dt_b
    dt = softplus(pre) * ok
    gs_v = gs[...]
    scatter_lanes(dt_s, dt, tb)
    scatter_lanes(dtu_s, dt * u, tb)
    scatter_lanes(gs_s, gs_v, tb)

    row = lax.broadcasted_iota(jnp.int32, (SUB, 2 * LANES), 0)
    lane = lax.broadcasted_iota(jnp.int32, (SUB, 2 * LANES), 1)
    pick = (lane // LANES == row).astype(F32).astype(BF)
    run = SUB
    span = run * SUB

    def add_lanes(group, i):
        rows = pl.ds(pl.multiple_of(i * span, span), span)
        pairs = jnp.concatenate([both_s[group % 2, j, rows, :] for j in range(part)], axis=0)
        sums[group, pl.ds(pl.multiple_of(i * SUB, SUB), SUB), :] = contract_cols(pick, pairs)

    for group in range(n_state // part):
        index = range(group * part, (group + 1) * part)
        rates = [rate2[n * SUB : (n + 1) * SUB, :] for n in index]

        def token(t, carry, after):
            g, acc = carry
            at = pl.multiple_of(t * SUB, SUB)
            dt_t, dtu_t, gs_t = [ref[pl.ds(at, SUB), :] for ref in (dt_s, dtu_s, gs_s)]
            dtd = dt_t + bc[t, 2 * n_state]
            new_g, new_acc, before, sources, reads = [], [], [], [], []
            gdt = ab = None
            for j, n in enumerate(index):
                lam = gs_t * bc[t, n_state + n] + g[j]
                sources.append(lam * dtu_t)
                reads.append(after[j] * gs_t)
                back = jnp.exp2(dtd * rates[j]) * lam
                before.append(states[0, n, pl.ds(at, SUB), :])
                thr = back * before[j]
                gdt = thr * rates[j] if gdt is None else gdt + thr * rates[j]
                ab = lam * bc[t, n] if ab is None else ab + lam * bc[t, n]
                new_g.append(back)
                new_acc.append(acc[j] + thr * dt_t)
            if group == 0:
                gdt_s[pl.ds(at, SUB), :] = gdt
                ab_s[pl.ds(at, SUB), :] = ab
            else:
                gdt_s[pl.ds(at, SUB), :] += gdt
                ab_s[pl.ds(at, SUB), :] += ab
            return (tuple(new_g), tuple(new_acc)), before, sources, reads

        def some_tokens(i, carry):
            i = tb // run - 1 - i
            if group:
                add_lanes(group - 1, i)
            late = pl.multiple_of((i + 1) * span, SUB)
            after = [states[0, n, pl.ds(late, SUB), :] for n in index]
            for k in range(run - 1, 0, -2):
                t = i * run + k
                carry, after, sources1, reads1 = token(t, carry, after)
                carry, after, sources0, reads0 = token(t - 1, carry, after)
                rows = pl.ds(pl.multiple_of((t - 1) * SUB, 2 * SUB), 2 * SUB)
                for j in range(part):
                    both_s[group % 2, j, rows, 0:LANES] = jnp.concatenate([sources0[j], sources1[j]], axis=0).astype(BF)
                    both_s[group % 2, j, rows, LANES:] = jnp.concatenate([reads0[j], reads1[j]], axis=0).astype(BF)
            return carry

        start = (
            tuple(g_ref[n * SUB : (n + 1) * SUB, :] for n in index),
            tuple(rate_out[n * SUB : (n + 1) * SUB, :] for n in index),
        )
        g, acc = lax.fori_loop(0, tb // run, some_tokens, start, unroll=tb // run)
        for j, n in enumerate(index):
            g_ref[n * SUB : (n + 1) * SUB, :] = g[j]
            rate_out[n * SUB : (n + 1) * SUB, :] = acc[j]
    for i in range(tb // run):
        add_lanes(n_state // part - 1, i)

    ab = gather_lanes(ab_s, width, tb)
    gdt = gather_lanes(gdt_s, width, tb)
    gu_out[...] = (gs_v * skip + dt * ab).astype(BF)
    grad_pre = ok * (gdt * LN2 + u * ab) * jax.nn.sigmoid(pre)
    vec_out[0:1, :] += jnp.sum(grad_pre, axis=0, keepdims=True)
    vec_out[1:2, :] += jnp.sum(gs_v * u, axis=0, keepdims=True)
    low = grad_pre.astype(BF)
    dtw_out[...] += lax.dot_general(rank[...], low, (((0,), (0,)), ((), ())), preferred_element_type=F32)
    rank_w = rank.shape[1]
    rows = pl.ds(pl.multiple_of((pl.num_programs(0) - 1 - pl.program_id(0)) * tb, tb), tb)
    part_s[rows, 0:rank_w] = contract_cols(low, small[at_small.dt_w, :]).astype(BF)

    take_row = lax.broadcasted_iota(jnp.int32, (2 * tb, tb // run * SUB), 0)
    take_lane = lax.broadcasted_iota(jnp.int32, (2 * tb, tb // run * SUB), 1)
    take = (take_lane == take_row % tb // run * SUB + take_row // tb).astype(F32).astype(BF)
    keep_row = lax.broadcasted_iota(jnp.int32, (2 * tb, part * span), 0)
    keep_lane = lax.broadcasted_iota(jnp.int32, (2 * tb, part * span), 1)
    keep = keep_lane // SUB % run == keep_row % run
    from_lane = lax.broadcasted_iota(jnp.int32, (part * span, LANES), 0)
    to_lane = lax.broadcasted_iota(jnp.int32, (part * span, LANES), 1)
    tail = jnp.zeros((2 * tb, LANES), F32)
    for group in range(n_state // part):
        chosen = jnp.dot(take, sums[group].astype(BF), preferred_element_type=F32)
        chosen = jnp.where(keep, chosen, 0.0).astype(BF)
        fold = (to_lane == group * part + from_lane // span).astype(F32).astype(BF)
        tail = tail + jnp.dot(chosen, fold, preferred_element_type=F32)
    part_s[rows, rank_w : rank_w + n_state] = tail[0:tb, 0:n_state].astype(BF)
    part_s[rows, rank_w + n_state :] = tail[tb:, 0:n_state].astype(BF)

    @pl.when(pl.program_id(0) == pl.num_programs(0) - 1)
    def _():
        proj = part_s.shape[1]
        across = lax.broadcasted_iota(jnp.int32, (proj, proj), 0) == lax.broadcasted_iota(jnp.int32, (proj, proj), 1)
        one = across.astype(F32).astype(BF)
        for b in range(part_s.shape[0] // LANES):
            packed_out[b * proj : (b + 1) * proj, :] = contract_cols(
                one, part_s[b * LANES : (b + 1) * LANES, :]
            ).astype(BF)


def scan_backward(at, bc, rank, small, act, valid, rate2, gs, states, tb):
    slots, width = act.shape
    n_state = rate2.shape[0] // SUB
    nb = slots // tb
    whole = lambda i: (0, 0)
    row = lambda i: (nb - 1 - i, 0)
    rank_w = rank.shape[1]
    proj = rank_w + 2 * n_state
    return pl.pallas_call(
        functools.partial(backward_kernel, at),
        grid=(nb,),
        in_specs=[
            pl.BlockSpec((tb, bc.shape[1]), row, memory_space=pltpu.SMEM),
            pl.BlockSpec((tb, rank_w), row),
            pl.BlockSpec(small.shape, whole),
            pl.BlockSpec((tb, width), row),
            pl.BlockSpec((tb, 1), row),
            pl.BlockSpec(rate2.shape, whole),
            pl.BlockSpec((tb, width), row),
            pl.BlockSpec((1, n_state, (tb + 1) * SUB, LANES), lambda i: (nb - 1 - i, 0, 0, 0)),
        ],
        out_specs=[
            pl.BlockSpec((proj * slots // LANES, LANES), whole),
            pl.BlockSpec((tb, width), row),
            pl.BlockSpec((rank_w, width), whole),
            pl.BlockSpec((2, width), whole),
            pl.BlockSpec(rate2.shape, whole),
        ],
        out_shape=[
            jax.ShapeDtypeStruct((proj * slots // LANES, LANES), BF),
            jax.ShapeDtypeStruct((slots, width), BF),
            jax.ShapeDtypeStruct((rank_w, width), F32),
            jax.ShapeDtypeStruct((2, width), F32),
            jax.ShapeDtypeStruct(rate2.shape, F32),
        ],
        scratch_shapes=[pltpu.VMEM((slots, proj), BF), pltpu.VMEM(rate2.shape, F32)]
        + [pltpu.VMEM((tb * SUB, LANES), F32)] * 5
        + [pltpu.VMEM((2, 4, tb * SUB, 2 * LANES), BF), pltpu.VMEM((n_state // 4, tb, 4 * SUB * SUB), F32)],
        compiler_params=pltpu.CompilerParams(vmem_limit_bytes=61 << 20),
        cost_estimate=small_cost(1 << 20),
        name="scan_backward",
    )(bc, rank, small, act, valid, rate2, gs, states)


def silu_grad(value, sig):
    return sig * (1.0 + value * (1.0 - sig))


def place_blocks(ref, own, other, index):
    chips = own.shape[0]
    rows = ref.shape[0] // (2 * chips)
    core = lax.rem(index, 2)
    for q in range(chips):
        ref[pl.ds(pl.multiple_of((2 * q + core) * rows, rows), rows), :] = own[q, 0:rows, :]
        ref[pl.ds(pl.multiple_of((2 * q + 1 - core) * rows, rows), rows), :] = other[q, 0:rows, :]


def block_copies(ref, own, other, index, sems, first):
    chips = own.shape[0]
    rows = ref.shape[0] // (2 * chips)
    core = lax.rem(index, 2)
    found = []
    for q in range(chips):
        for blocks, d in ((own, 2 * q + core), (other, 2 * q + 1 - core)):
            at = pl.ds(pl.multiple_of(d * rows, rows), rows)
            found.append(
                pltpu.make_async_copy(blocks.at[q, pl.ds(0, rows)], ref.at[at], sems.at[first + len(found)])
            )
    return found


def read_row(ref, row, cols):
    tile = SUB if ref.dtype == F32 else 2 * SUB
    base = pl.multiple_of(row // tile * tile, tile)
    rows = ref[pl.ds(base, tile), cols].astype(F32)
    mine = lax.broadcasted_iota(jnp.int32, rows.shape, 0) == row - base
    return jnp.sum(jnp.where(mine, rows, 0.0), axis=0, keepdims=True)


def add_row(ref, row, value):
    base = pl.multiple_of(row // SUB * SUB, SUB)
    rows = ref[pl.ds(base, SUB), :]
    mine = lax.broadcasted_iota(jnp.int32, rows.shape, 0) == row - base
    ref[pl.ds(base, SUB), :] = rows + jnp.where(mine, value, 0.0)


def split_kernel(n_dp, in_w, gain, out):
    rows = in_w.shape[0]
    n_line, full, width = out.shape
    owned = width // n_dp
    top = jnp.broadcast_to(gain[...].astype(F32), (full - 2 * rows, rows)).astype(in_w.dtype)
    for to in range(n_line):
        for half in range(2):
            for d in range(n_dp):
                at = ((half * n_dp + d) * n_line + to) * owned
                out[to, half * rows : (half + 1) * rows, d * owned : (d + 1) * owned] = in_w[:, at : at + owned]
        out[to, 2 * rows :, :] = jnp.zeros((full - 2 * rows, width), in_w.dtype)
        out[to, 2 * rows :, 0:rows] = top


def split_columns(in_w, gain, n_dp, n_line):
    rows, both = in_w.shape
    width = both // (2 * n_line)
    if width // n_dp % LANES:
        blocks = in_w.reshape(rows, 2, n_dp, n_line, width // n_dp).transpose(3, 1, 0, 2, 4)
        top = jnp.broadcast_to(jnp.pad(gain, (0, width - rows)), (n_line, 16, width))
        return jnp.concatenate([blocks.reshape(n_line, 2 * rows, width), top], axis=1)
    vmem = pl.BlockSpec(memory_space=pltpu.VMEM)
    return pl.pallas_call(
        functools.partial(split_kernel, n_dp),
        in_specs=[vmem] * 2,
        out_specs=vmem,
        out_shape=jax.ShapeDtypeStruct((n_line, 2 * rows + 16, width), in_w.dtype),
        cost_estimate=small_cost(1 << 10),
        name="split_columns",
    )(in_w, gain[None])


def join_kernel(n_dp, inner, gate, in_w, gain, out, gain_out):
    n_line, rows, width = inner.shape
    owned = width // n_dp
    total = jnp.zeros((rows, LANES), F32)
    for half, got in enumerate((inner, gate)):
        for line in range(n_line):
            for d in range(n_dp):
                at = ((half * n_dp + d) * n_line + line) * owned
                block = got[line, :, d * owned : (d + 1) * owned].astype(F32)
                out[:, at : at + owned] = block
                term = block * in_w[:, at : at + owned].astype(F32)
                for low in range(0, owned, LANES):
                    total = total + term[:, low : low + LANES]
    ones = jnp.ones((SUB, LANES), F32)
    sums = lax.dot_general(
        ones, total, (((1,), (1,)), ((), ())), precision=lax.Precision.HIGHEST, preferred_element_type=F32
    )
    gain_out[...] = sums[0:1, :] / gain[...].astype(F32)


def join_columns(inner, gate, in_w, gain, n_dp):
    rows, both = in_w.shape
    n_line, _, width = inner.shape
    if width // n_dp % LANES:
        blocks = jnp.stack([inner, gate]).astype(F32).reshape(2, n_line, rows, n_dp, -1)
        full = blocks.transpose(2, 0, 3, 1, 4).reshape(rows, both)
        return full, jnp.sum(full * in_w.astype(F32), axis=1) / gain.astype(F32)
    vmem = pl.BlockSpec(memory_space=pltpu.VMEM)
    full, gain_grad = pl.pallas_call(
        functools.partial(join_kernel, n_dp),
        in_specs=[vmem] * 4,
        out_specs=[vmem] * 2,
        out_shape=[jax.ShapeDtypeStruct((rows, both), F32), jax.ShapeDtypeStruct((1, rows), F32)],
        cost_estimate=small_cost(1 << 10),
        name="join_columns",
    )(inner, gate, in_w, gain[None])
    return full, gain_grad[0]


def column_block(width, slots):
    return 256 if width % 256 == 0 and slots <= 1024 else LANES


def from_place(place, steps, n_line):
    return lax.rem(place - steps + n_line, n_line)


def outer(lefts, right, outs):
    rows = min(256, lefts[0].shape[1])

    @pl.loop(0, lefts[0].shape[1] // rows)
    def _(r):
        at = pl.ds(pl.multiple_of(r * rows, rows), rows)
        for left, out in zip(lefts, outs):
            found = lax.dot_general(left[:, at], right[...], (((0,), (0,)), ((), ())), preferred_element_type=F32)
            out[at, :] = found.astype(out.dtype)


def outer_kernel(kept, sent, right, kept_out, sent_out):
    outer((kept, sent), right, (kept_out, sent_out))


def outer_product(kept, sent, right):
    shape = (kept.shape[1], right.shape[1])
    vmem = pl.BlockSpec(memory_space=pltpu.VMEM)
    return pl.pallas_call(
        outer_kernel,
        in_specs=[vmem] * 3,
        out_specs=[vmem] * 2,
        out_shape=[jax.ShapeDtypeStruct(shape, BF)] * 2,
        compiler_params=pltpu.CompilerParams(vmem_limit_bytes=61 << 20),
        cost_estimate=small_cost(1 << 20),
        name="outer_product",
    )(kept, sent, right)


def to_shifts(source, outs, place):
    rows = outs[0].shape[0]
    for s, out in enumerate(outs):
        at = pl.multiple_of(lax.rem(place + s, len(outs)) * rows, rows)
        out[...] = source[pl.ds(at, rows), :]


def split_cores(ref, kept, sent, index, n_dp):
    size = ref.shape[1] // n_dp
    core = lax.rem(index, 2)
    for q in range(kept.shape[1] // size):
        cols = slice(q * size, (q + 1) * size)
        kept[:, cols] = ref[:, pl.ds(pl.multiple_of((2 * q + core) * size, size), size)]
        sent[:, cols] = ref[:, pl.ds(pl.multiple_of((2 * q + 1 - core) * size, size), size)]


def project_kernel(n_line, n_dp, at, info, *refs):
    toks, refs = refs[:n_line], refs[n_line:]
    own, other, small, allowed, gain, normed, kept, sent, inner, conv_out, activ, part, w_nat, inner_s, ext = refs
    held, model = toks[0].shape
    slots = held * n_line
    width = w_nat.shape[1]
    taps = at.taps
    rim = taps - 1
    rows_dp = model // n_dp
    core = lax.rem(info[0], 2)
    for q in range(n_dp // 2):
        for blocks, d in ((own, 2 * q + core), (other, 2 * q + 1 - core)):
            found = blocks[q, rows_dp:, 0:rows_dp].astype(F32)[0:1, :]
            gain[:, pl.ds(pl.multiple_of(d * rows_dp, rows_dp), rows_dp)] = found
    step = 32
    for s, tok in enumerate(toks):
        base = from_place(info[1], s, n_line) * held

        @pl.loop(0, held // step)
        def _(i):
            x = tok[pl.ds(pl.multiple_of(i * step, step), step), :].astype(F32)
            scale = lax.rsqrt(jnp.mean(x * x, axis=1, keepdims=True) + EPS)
            normed[pl.ds(pl.multiple_of(base + i * step, step), step), :] = (x * scale * gain[...]).astype(BF)

    split_cores(normed, kept, sent, info[0], n_dp)
    place_blocks(w_nat, own, other, info[0])
    cb = column_block(width, slots)

    @pl.loop(0, width // cb)
    def _(c):
        cols = pl.ds(pl.multiple_of(c * cb, cb), cb)
        inner_s[...] = jnp.dot(normed[...], w_nat[:, cols], preferred_element_type=F32)
        inner[:, cols] = inner_s[...].astype(BF)
        vectors = small[at.rest, cols].astype(F32)
        for f in range(n_line):
            rows = slice(f * held, (f + 1) * held)
            ext[SUB : SUB + held, :] = inner_s[rows, :]
            for k in range(1, rim + 1):
                if f == 0:
                    ext[SUB - k : SUB - k + 1, :] = jnp.zeros((1, cb), F32)
                else:
                    ext[SUB - k : SUB - k + 1, :] = read_row(inner_s, (f - 1) * held + info[1 + f] - k, slice(None))
            total = vectors[taps : taps + 1, :]
            for lag in range(taps):
                tapped = ext[SUB - lag : SUB - lag + held, :]
                total = total + vectors[rim - lag : rim - lag + 1, :] * tapped * allowed[rows, lag : lag + 1]
            conv_out[rows, cols] = total.astype(BF)
            activ[rows, cols] = (total * jax.nn.sigmoid(total)).astype(BF)

    proj = part.shape[0] * LANES // slots
    for b in range(slots // LANES):
        found = contract_cols(small[at.x_t, :], activ[b * LANES : (b + 1) * LANES, :])
        part[b * proj : (b + 1) * proj, :] = found.astype(BF)


def project(info, n_line, n_dp, toks, own, other, at, small, allowed):
    held, model = toks[0].shape
    slots = held * n_line
    width, proj = small.shape[1], at.x_t.stop - at.x_t.start
    vmem = pl.BlockSpec(memory_space=pltpu.VMEM)
    shapes = [
        ((1, model), F32), ((slots, model), BF), ((slots, model // 2), BF), ((slots, model // 2), BF),
        ((slots, width), BF), ((slots, width), BF), ((slots, width), BF), ((proj * slots // LANES, LANES), BF),
    ]
    return pl.pallas_call(
        functools.partial(project_kernel, n_line, n_dp, at),
        in_specs=[pl.BlockSpec(memory_space=pltpu.SMEM)] + [vmem] * (4 + len(toks)),
        out_specs=[vmem] * len(shapes),
        out_shape=[jax.ShapeDtypeStruct(s, t) for s, t in shapes],
        scratch_shapes=[
            pltpu.VMEM((model, width), BF),
            pltpu.VMEM((slots, column_block(width, slots)), F32),
            pltpu.VMEM((SUB + slots // n_line, column_block(width, slots)), F32),
        ],
        compiler_params=pltpu.CompilerParams(vmem_limit_bytes=61 << 20),
        cost_estimate=small_cost(1 << 20),
        name="project",
    )(info, *toks, own, other, small, allowed)


def gate_kernel(n_line, n_dp, at, info, own, other, normed, y, act, small, *refs):
    out_own, out_other, refs = refs[: n_dp // 2], refs[n_dp // 2 : n_dp], refs[n_dp:]
    branches, refs = refs[:n_line], refs[n_line:]
    gate, gated, o_nat, *halves, branch, w_nat = refs
    slots, width = y.shape
    model = normed.shape[1]
    place_blocks(w_nat, own, other, info[0])
    rows = width // n_dp
    core, chip = lax.rem(info[0], 2), lax.div(info[0], 2)
    for u in range(n_dp // 2):
        first = 2 * jnp.bitwise_xor(chip, u)
        o_nat[pl.ds(pl.multiple_of((first + core) * rows, rows), rows), :] = out_own[u][0:rows, :]
        o_nat[pl.ds(pl.multiple_of((first + 1 - core) * rows, rows), rows), :] = out_other[u][0:rows, :]
    cb = column_block(width, slots)

    @pl.loop(0, width // cb)
    def _(c):
        cols = pl.ds(pl.multiple_of(c * cb, cb), cb)
        value = jnp.dot(normed[...], w_nat[:, cols], preferred_element_type=F32)
        gate[:, cols] = value
        skip = small[at.rest, cols].astype(F32)[at.taps + 2 : at.taps + 3, :]
        scan_out = y[:, cols] + skip * act[:, cols].astype(F32)
        gated[:, cols] = (scan_out * value * jax.nn.sigmoid(value)).astype(BF)

    mb = column_block(model, slots)

    @pl.loop(0, model // mb)
    def _(c):
        cols = pl.ds(pl.multiple_of(c * mb, mb), mb)
        branch[:, cols] = jnp.dot(gated[...], o_nat[:, cols], preferred_element_type=F32).astype(BF)

    to_shifts(branch, branches, info[1])
    if halves:
        split_cores(gated, *halves, info[0], n_dp)


def gate_block(info, n_line, n_dp, own, other, out_own, out_other, normed, y, act, at, small):
    slots, width = y.shape
    model = normed.shape[1]
    vmem = pl.BlockSpec(memory_space=pltpu.VMEM)
    shapes = [((slots // n_line, model), BF)] * n_line
    shapes += [((slots, width), F32), ((slots, width), BF), ((width, model), BF)]
    if width // n_dp % LANES == 0:
        shapes += [((slots, width // 2), BF)] * 2
    outs = pl.pallas_call(
        functools.partial(gate_kernel, n_line, n_dp, at),
        in_specs=[pl.BlockSpec(memory_space=pltpu.SMEM)] + [vmem] * (6 + n_dp),
        out_specs=[vmem] * len(shapes),
        out_shape=[jax.ShapeDtypeStruct(s, t) for s, t in shapes],
        scratch_shapes=[pltpu.VMEM((slots, model), BF), pltpu.VMEM((model, width), BF)],
        compiler_params=pltpu.CompilerParams(vmem_limit_bytes=61 << 20),
        cost_estimate=small_cost(1 << 20),
        name="gate_block",
    )(info, own, other, normed, y, act, small, *out_own, *out_other)
    branches, (gate, gated, o_nat), halves = list(outs[:n_line]), outs[n_line : n_line + 3], outs[n_line + 3 :]
    return branches, gate, o_nat, *(halves or cores(gated, 1))


def gate_back_kernel(n_line, at, info, *refs):
    cots, refs = refs[:n_line], refs[n_line:]
    o_nat, gate, y, act, small, valid, normed, gs, grad_gate, dout, product = refs
    slots, width = y.shape
    held, model = cots[0].shape
    for s, cot in enumerate(cots):
        rows = pl.ds(pl.multiple_of(from_place(info[1], s, n_line) * held, held), held)
        dout[rows, :] = (cot[...].astype(F32) * valid[rows, :]).astype(BF)

    cb = column_block(width, slots)

    @pl.loop(0, width // cb)
    def _(c):
        cols = pl.ds(pl.multiple_of(c * cb, cb), cb)
        grad = lax.dot_general(dout[...], o_nat[cols, :], (((1,), (1,)), ((), ())), preferred_element_type=F32)
        value = gate[:, cols]
        sig = jax.nn.sigmoid(value)
        skip = small[at.rest, cols].astype(F32)[at.taps + 2 : at.taps + 3, :]
        scan_out = y[:, cols] + skip * act[:, cols].astype(F32)
        gs[:, cols] = grad * value * sig
        grad_gate[:, cols] = (grad * scan_out * silu_grad(value, sig)).astype(BF)

    outer((normed,), grad_gate, (product,))


def gate_back(info, n_line, cots, o_nat, gate, y, act, at, small, valid, normed):
    slots, width = y.shape
    model = o_nat.shape[1]
    vmem = pl.BlockSpec(memory_space=pltpu.VMEM)
    shapes = [((slots, width), F32), ((slots, width), BF), ((slots, model), BF)]
    shapes += [((model, width), BF)]
    return pl.pallas_call(
        functools.partial(gate_back_kernel, n_line, at),
        in_specs=[pl.BlockSpec(memory_space=pltpu.SMEM)] + [vmem] * (7 + len(cots)),
        out_specs=[vmem] * len(shapes),
        out_shape=[jax.ShapeDtypeStruct(s, t) for s, t in shapes],
        compiler_params=pltpu.CompilerParams(vmem_limit_bytes=61 << 20),
        cost_estimate=small_cost(1 << 20),
        name="gate_back",
    )(info, *cots, o_nat, gate, y, act, small, valid, normed)


def together(slots):
    return slots <= 1024


def conv_back_kernel(n_line, n_dp, at, info, gp_part, gp_got, gu, small, act, conv_out, inner, allowed, dtw, rate_grad, scan_vec,
                     grad_gate, *refs):
    slots, width = gu.shape
    inner_own, inner_other, gate_own, gate_other, *refs = refs
    halves_far, refs = (refs[:2], refs[2:]) if together(slots) else ((), refs)
    grads, refs = refs[:n_line], refs[n_line:]
    products_far, refs = (refs[:2], refs[2:]) if together(slots) else ((), refs)
    gi_low, refs = (None, refs) if together(slots) else (refs[0], refs[1:])
    kept, sent, x_grad, vec, ext, gi, tail, grad_normed, column, gp, arrived, left, w_nat, gate_nat, *refs = refs
    halves = ()
    copies = block_copies(w_nat, inner_own, inner_other, info[0], arrived, 0)
    copies += block_copies(gate_nat, gate_own, gate_other, info[0], arrived, n_dp)
    if together(slots):
        gi_low, *refs = refs
        halves, products = refs[:2], refs[2:]
        for i, (src, dst) in enumerate(zip(halves_far, halves)):
            copies.append(pltpu.make_async_copy(src, dst, arrived.at[2 * n_dp + i]))
    for copy in copies:
        copy.start()
    leaving = []

    def leave(src, dst):
        copy = pltpu.make_async_copy(src, dst, left.at[len(leaving)])
        copy.start()
        leaving.append(copy)

    gp[...] = (gp_part[...] + gp_got[...].astype(F32)).astype(BF)
    held = slots // n_line
    taps = at.taps
    rim = taps - 1
    cb = column_block(width, slots)
    proj = x_grad.shape[0]
    x_grad[...] = sum(
        jnp.dot(gp[b * proj : (b + 1) * proj, :], act[b * LANES : (b + 1) * LANES, :], preferred_element_type=F32)
        for b in range(slots // LANES)
    )
    vec[...] = jnp.zeros_like(vec)
    for lag in range(taps):
        tail[lag, held : held + SUB, :] = jnp.zeros((SUB, cb), F32)

    @pl.loop(0, width // cb)
    def _(c):
        cols = pl.ds(pl.multiple_of(c * cb, cb), cb)
        vectors = small[at.rest, cols].astype(F32)
        for f in range(n_line - 1, -1, -1):
            rows = slice(f * held, (f + 1) * held)
            ext[SUB : SUB + held, :] = inner[rows, cols].astype(F32)
            for k in range(1, rim + 1):
                if f == 0:
                    ext[SUB - k : SUB - k + 1, :] = jnp.zeros((1, cb), F32)
                else:
                    ext[SUB - k : SUB - k + 1, :] = read_row(inner, (f - 1) * held + info[1 + f] - k, cols)
            back = [
                lax.dot_general(
                    gp[b * proj : (b + 1) * proj, :], small[at.x_t, cols], (((0,), (0,)), ((), ())),
                    preferred_element_type=F32,
                )
                for b in range(f * held // LANES, (f + 1) * held // LANES)
            ]
            grad = gu[rows, cols].astype(F32) + jnp.concatenate(back, axis=0)
            co = conv_out[rows, cols].astype(F32)
            grad = grad * silu_grad(co, jax.nn.sigmoid(co))
            vec[taps : taps + 1, cols] += jnp.sum(grad, axis=0, keepdims=True)
            for lag in range(taps):
                weighted = grad * allowed[rows, lag : lag + 1]
                vec[rim - lag : rim - lag + 1, cols] += jnp.sum(
                    weighted * ext[SUB - lag : SUB - lag + held, :], axis=0, keepdims=True
                )
                tail[lag, 0:held, :] = weighted * vectors[rim - lag : rim - lag + 1, :]
            total = tail[0, 0:held, :]
            for lag in range(1, taps):
                total = total + tail[lag, lag : lag + held, :]
            gi[rows, :] = total
            if f + 1 < n_line:
                for k in range(1, rim + 1):
                    add_row(gi, f * held + info[2 + f] - k, gi[slots + k : slots + k + 1, :])
            for k in range(1, rim + 1):
                row = tail[k, 0:1, :]
                for lag in range(k + 1, taps):
                    row = row + tail[lag, lag - k : lag - k + 1, :]
                gi[slots + k : slots + k + 1, :] = row
        gi_low[:, cols] = gi[0:slots, :].astype(BF)

    for copy in copies:
        copy.wait()
    model = w_nat.shape[0]
    mb = column_block(model, slots)

    @pl.loop(0, model // mb)
    def _(c):
        cols = pl.ds(pl.multiple_of(c * mb, mb), mb)
        found = contract_cols(gi_low[...], w_nat[cols, :]) + contract_cols(grad_gate[...], gate_nat[cols, :])
        grad_normed[:, cols] = found.astype(BF)

    for s, grad in enumerate(grads):
        first = pl.multiple_of(lax.rem(info[1] + s, n_line) * held, held)
        leave(grad_normed.at[pl.ds(first, held)], grad)
    if halves:
        step = model // 2 // 4
        for r in range(4):
            rows = slice(r * step, (r + 1) * step)
            for half, product, out in zip(halves, products, products_far):
                product[rows, :] = lax.dot_general(
                    half[:, rows], gi_low[...], (((0,), (0,)), ((), ())), preferred_element_type=F32
                ).astype(BF)
                leave(product.at[pl.ds(r * step, step)], out.at[pl.ds(r * step, step)])
    vec[taps + 1 : taps + 3, :] = scan_vec[...]
    owned = width // n_dp
    if kept.shape[0] == 1:
        kept[0, at.dt_w, :], kept[0, at.x_t, :], kept[0, at.a_t, :], kept[0, at.rest, :] = (
            dtw[...], x_grad[...], rate_grad[...], vec[...]
        )
        for copy in leaving:
            copy.wait()
        return
    core = lax.rem(info[0], 2)
    fold = kept.shape[1]
    for q in range(n_dp // 2):
        for ref, d in ((kept, 2 * q + core), (sent, 2 * q + 1 - core)):
            cols = pl.ds(pl.multiple_of(d * owned, owned), owned)
            for rows, source in ((at.dt_w, dtw), (at.x_t, x_grad), (at.a_t, rate_grad), (at.rest, vec)):
                column[rows, :] = source[:, cols]
            for b in range(width // owned):
                ref[q, :, b * owned : (b + 1) * owned] = column[b * fold : (b + 1) * fold, :].astype(ref.dtype)
    for copy in leaving:
        copy.wait()


def conv_back(info, n_line, n_dp, gp_part, gp_got, gu, at, small, act, conv_out, inner, allowed, dtw, rate_grad, scan_vec, grad_gate,
              inner_blocks, gate_blocks, normed_k, normed_s):
    slots, width = gu.shape
    held, model = slots // n_line, 2 * normed_k.shape[1]
    cb = column_block(width, slots)
    owned = width // n_dp
    tiles, one = owned % LANES == 0, together(slots)
    vmem, away = pl.BlockSpec(memory_space=pltpu.VMEM), pl.BlockSpec(memory_space=pl.ANY)
    fold = at.fold(n_dp)
    shape = (n_dp // 2, fold, width) if tiles else (1, at.rows, width)
    later = [*inner_blocks, *gate_blocks] + ([normed_k, normed_s] if one else [])
    low, half = jax.ShapeDtypeStruct((slots, width), BF), jax.ShapeDtypeStruct((model // 2, width), BF)
    outs = pl.pallas_call(
        functools.partial(conv_back_kernel, n_line, n_dp, at),
        in_specs=[pl.BlockSpec(memory_space=pltpu.SMEM)] + [vmem] * 12 + [away] * len(later),
        out_specs=[away] * n_line + ([away] * 2 if one else [vmem]) + [vmem] * 2,
        out_shape=[jax.ShapeDtypeStruct((held, model), BF)] * n_line
        + ([half] * 2 if one else [low])
        + [
            jax.ShapeDtypeStruct(shape, F32),
            jax.ShapeDtypeStruct(shape if tiles else (SUB, LANES), BF if tiles else F32),
        ],
        scratch_shapes=[
            pltpu.VMEM((at.x_t.stop - at.x_t.start, width), F32),
            pltpu.VMEM((16, width), F32),
            pltpu.VMEM((SUB + held, cb), F32),
            pltpu.VMEM((slots + SUB, cb), F32),
            pltpu.VMEM((at.taps, held + SUB, cb), F32),
            pltpu.VMEM((slots, model), BF),
            pltpu.VMEM((n_dp * fold, owned), F32),
            pltpu.VMEM(gp_got.shape, BF),
            pltpu.SemaphoreType.DMA((2 * n_dp + 2,)),
            pltpu.SemaphoreType.DMA((n_line + 8,)),
        ]
        + [pltpu.VMEM((model, width), BF)] * 2
        + ([pltpu.VMEM((slots, width), BF)] + [pltpu.VMEM((slots, model // 2), BF)] * 2 if one else [])
        + ([pltpu.VMEM((model // 2, width), BF)] * 2 if one else []),
        compiler_params=pltpu.CompilerParams(vmem_limit_bytes=61 << 20),
        cost_estimate=small_cost(1 << 20),
        name="conv_back",
    )(info, gp_part, gp_got, gu, small, act, conv_out, inner, allowed, dtw, rate_grad, scan_vec, grad_gate, *later)
    grads, (*products, kept, sent) = outs[:n_line], outs[n_line:]
    if not one:
        products = outer_product(normed_k, normed_s, products[0])
    if not tiles:
        kept, sent = [
            part.reshape(at.rows, n_dp // 2, owned).transpose(1, 0, 2) for part in cores(kept[0], 1)
        ]
    return list(grads), *products, kept, sent.astype(BF)


def swap(value, axis, mask):
    count = lax.axis_size(axis)
    return lax.ppermute(value, axis, [(i, i ^ mask) for i in range(count)])


def shift(value, axis, steps):
    count = lax.axis_size(axis)
    return lax.ppermute(value, axis, [(i, (i + steps) % count) for i in range(count)])


def chips_of(axis):
    return [list(range(core, lax.axis_size(axis), 2)) for core in range(2)]


def to_line(blocks):
    return lax.all_to_all(blocks, "fsdp", 0, 0)


def to_chips(blocks):
    return lax.all_to_all(blocks, "dp", 0, 0, axis_index_groups=chips_of("dp"))


def repeated(value, count):
    return jnp.broadcast_to(value[None], (count,) + value.shape)


def in_order(parts, axis):
    count, me = lax.axis_size(axis), lax.axis_index(axis)
    up = jnp.stack([parts[-k % count] for k in range(count)] * 2)
    return lax.dynamic_slice_in_dim(up, lax.rem(count - me, count), count, 0)


def by_chip(parts):
    chip, count = lax.div(lax.axis_index("dp"), 2), len(parts)
    bits = count.bit_length() - 1
    cube = jnp.stack(parts).reshape((2,) * bits + parts[0].shape)
    for place in range(bits):
        mine = lax.rem(chip >> (bits - 1 - place), 2) == 1
        cube = jnp.where(mine, jnp.flip(cube, place), cube)
    return cube.reshape((count,) + parts[0].shape)


def by_device(own, other):
    core = lax.rem(lax.axis_index("dp"), 2) == 1
    both = jnp.where(core, jnp.stack([other, own], axis=1), jnp.stack([own, other], axis=1))
    return lax.optimization_barrier(both.reshape((-1,) + own.shape[1:]))


def last_line(value, reach):
    while True:
        got = swap(value.astype(BF), "fsdp", reach)
        reach *= 2
        if reach >= lax.axis_size("fsdp"):
            return value, got
        value = value + got.astype(F32)


def fence(*values):
    flat, shape = jax.tree.flatten(values)
    return jax.tree.unflatten(shape, lax.optimization_barrier(tuple(flat)))


def cores(value, axis):
    cut = value.shape[:axis] + (lax.axis_size("dp") // 2, 2, -1) + value.shape[axis + 1 :]
    cube = value.reshape(cut)
    core = lax.rem(lax.axis_index("dp"), 2)
    found = [lax.dynamic_index_in_dim(cube, at, axis + 1, keepdims=False) for at in (core, 1 - core)]
    flat = value.shape[:axis] + (value.shape[axis] // 2,) + value.shape[axis + 1 :]
    return [part.reshape(flat) for part in found]


def add_core_kernel(kept, got, *refs):
    *small, out = refs
    whole = kept.shape[0]
    out[0, 0:whole, :] = (kept[...].astype(F32) + got[...].astype(F32)).astype(BF)
    if small:
        out[0, whole:, :] = (small[0][0] + small[1][0].astype(F32)).astype(BF)


def add_core(kept, got, *small):
    chips, width = lax.axis_size("dp") // 2, kept.shape[1]
    whole = kept.shape[0] // chips
    more = small[0].shape[1] if small else 0
    return pl.pallas_call(
        add_core_kernel,
        grid=(chips,),
        in_specs=[pl.BlockSpec((whole, width), lambda q: (q, 0))] * 2
        + [pl.BlockSpec((1, more, width), lambda q: (q, 0, 0))] * len(small),
        out_specs=pl.BlockSpec((1, whole + more, width), lambda q: (q, 0, 0)),
        out_shape=jax.ShapeDtypeStruct((chips, whole + more, width), BF),
        compiler_params=pltpu.CompilerParams(vmem_limit_bytes=61 << 20),
        cost_estimate=small_cost(1 << 10),
        name="add_core",
    )(kept, got, *small)


def add_chips(blocks):
    return jnp.sum(to_chips(blocks.astype(BF)).astype(F32), axis=0)


def add_chips_near(blocks):
    count, chip = lax.axis_size("dp") // 2, lax.div(lax.axis_index("dp"), 2)
    total = lax.dynamic_index_in_dim(blocks, chip, 0, keepdims=False)
    for u in range(1, count):
        total = total + far(blocks, u).astype(F32)
    return total


def sent_far(kept, got, u):
    rows = kept.shape[0] // (lax.axis_size("dp") // 2)
    at = jnp.bitwise_xor(lax.div(lax.axis_index("dp"), 2), u) * rows
    return sum(lax.dynamic_slice_in_dim(part, at, rows, 0).astype(F32) for part in (kept, got)).astype(BF)


def far(blocks, u):
    block = lax.dynamic_index_in_dim(blocks, jnp.bitwise_xor(lax.div(lax.axis_index("dp"), 2), u), 0, keepdims=False)
    return swap(block.astype(BF), "dp", 2 * u)


def per_device(
    tokens, counts, lengths, gain, in_weight, conv_weight, conv_bias, x_weight,
    dt_weight, dt_bias, a_log, skip, out_weight, cotangent,
):
    n_dp, n_line = lax.axis_size("dp"), lax.axis_size("fsdp")
    group, place = lax.axis_index("dp"), lax.axis_index("fsdp")
    held_slots, model = tokens.shape
    slots = held_slots * n_line
    owned = skip.shape[0]
    width = owned * n_dp
    in_rows = in_weight.shape[0]
    taps, rank_w, n_state = conv_weight.shape[0], dt_weight.shape[0], a_log.shape[1]
    proj = x_weight.shape[1]
    tb = 64 if slots % 64 == 0 else slots

    count_row = lax.dynamic_index_in_dim(counts, group, 0, keepdims=False)
    length_row = lax.dynamic_index_in_dim(lengths, group, 0, keepdims=False)
    info = jnp.concatenate([jnp.stack([group, place]).astype(jnp.int32), count_row])
    offsets = jnp.cumsum(count_row) - count_row
    within = lax.broadcasted_iota(jnp.int32, (n_line, held_slots), 1)
    present = within < count_row[:, None]
    position = offsets[:, None] + within
    second, third = length_row[0], length_row[0] + length_row[1]
    begin = jnp.where(position >= third, third, jnp.where(position >= second, second, 0))
    marks = jnp.stack(
        [position - lag >= begin for lag in range(taps)] + [present, present & (position == begin)]
    ).astype(F32).reshape(taps + 2, slots).T
    allowed, valid, opens = marks[:, :taps], marks[:, taps : taps + 1], marks[:, taps + 1 :] * FAR

    own_tokens, own_cot = tokens, cotangent
    steps = range(1, n_line)
    chips = range(1, n_dp // 2)
    at = Small(rank_w, proj, n_state, taps)

    parts = split_columns(in_weight, gain, n_dp, n_line)
    rest = jnp.concatenate([conv_weight, conv_bias[None], dt_bias[None], skip[None]], axis=0)
    rest = jnp.pad(rest, ((0, 16 - rest.shape[0]), (0, 0)))
    small = jnp.concatenate([dt_weight, x_weight.T, a_log.T, rest], axis=0)
    small_rows = -(-at.rows * owned // model)
    small_rows += -small_rows % 16
    small = jnp.pad(small, ((0, small_rows * model // owned - at.rows), (0, 0))).reshape(small_rows, model)
    packed = jnp.concatenate([out_weight, small], axis=0)
    parts, tokens = fence(parts, tokens)
    parts = to_line(parts)
    toks = {0: tokens, 1: shift(tokens, "fsdp", 1)}
    near = [packed] + [swap(packed, "dp", 2 * u) for u in chips]
    parts, toks, near, info, allowed, valid, opens = fence(parts, toks, near, info, allowed, valid, opens)

    gain_rows = jnp.pad(parts[:, 2 * in_rows, :in_rows].reshape(1, -1), ((0, 15), (0, width - n_line * in_rows)))
    inner_block = jnp.concatenate([parts[:, :in_rows].reshape(-1, width), gain_rows], axis=0)
    gate_in = parts[:, in_rows : 2 * in_rows].reshape(-1, width)
    inner_rep, gate_in, toks = fence(repeated(inner_block, n_dp // 2), gate_in, toks)
    inner_own = to_chips(inner_rep)
    for s in steps[1:]:
        toks[s] = shift(toks[0], "fsdp", s)
    gate_rep = repeated(gate_in, n_dp // 2)
    small = by_chip([block[owned:].reshape(-1, owned)[: at.rows] for block in near])
    small_other = swap(small, "dp", 1)
    inner_own, toks, near, gate_rep, cotangent, small, small_other = fence(
        inner_own, toks, near, gate_rep, cotangent, small, small_other
    )

    inner_other = swap(inner_own, "dp", 1)
    small = by_device(small, small_other).transpose(1, 0, 2).reshape(-1, width)
    inner_own, inner_other, toks, cotangent, near, small = fence(inner_own, inner_other, toks, cotangent, near, small)
    rates = -jnp.exp(small[at.a_t].astype(F32))
    chunks = width // LANES
    rate2 = jnp.pad(
        (rates * (1.0 / LN2)).reshape(n_state, chunks, LANES), ((0, 0), (0, SUB - chunks), (0, 0))
    ).reshape(n_state * SUB, LANES)

    gate_own = to_chips(gate_rep)
    cots = {0: cotangent, 1: shift(cotangent, "fsdp", 1)}
    full_gain, normed, normed_kept, normed_sent, inner, conv_out, activ, low = project(
        info, n_line, n_dp, [toks[s] for s in range(n_line)], inner_own, inner_other, at, small, allowed
    )
    low, rate2, cots, near = fence(low, rate2, cots, near)

    part = low.astype(F32) + swap(low, "fsdp", 1).astype(F32)
    part, gate_own, near = fence(part, gate_own, near)
    part, got = last_line(part, 2)
    out_near, out_other = near, [swap(block, "dp", 1) for block in near]
    part, got, cots, out_near, out_other = fence(part, got, cots, out_near, out_other)
    projected = part + got.astype(F32)

    gate_other = swap(gate_own, "dp", 1)
    for s in steps[1:]:
        cots[s] = shift(cots[0], "fsdp", s)
    projected = projected.reshape(-1, proj, LANES).transpose(0, 2, 1).reshape(slots, proj)
    rank_low = projected[:, :rank_w].astype(BF)
    bc = jnp.concatenate([projected[:, rank_w:], opens], axis=1)
    scanned, states = scan_forward(at, bc, rank_low, small, activ, valid, rate2, tb)
    scanned, gate_own, gate_other, cots[n_line - 1] = fence(scanned, gate_own, gate_other, cots[n_line - 1])

    branches, gate, out_nat, *gated = gate_block(
        info, n_line, n_dp, gate_own, gate_other, out_near, out_other, normed, scanned, activ, at, small
    )
    branches, gate, gated, out_nat, cots = fence(branches, gate, gated, out_nat, cots)

    branches[1] = shift(branches[1], "fsdp", 1)
    grad_scan, grad_gate, dout, gate_grad = gate_back(
        info, n_line, [cots[s] for s in range(n_line)], out_nat, gate, scanned, activ, at, small, valid, normed
    )
    branches, grad_scan, grad_gate, dout, gated, gate_grad = fence(
        branches, grad_scan, grad_gate, dout, gated, gate_grad
    )

    gate_sums = lax.all_to_all(gate_grad.reshape(n_dp, -1, width), "dp", 0, 0)
    for s in steps[1:]:
        branches[s] = shift(branches[s], "fsdp", s)
    low, grad_u, dt_w_grad, vectors, rate_sum = scan_backward(
        at, bc, rank_low, small, activ, valid, rate2, grad_scan, states, tb
    )
    low, branches, gated, dout, grad_gate, rate_sum = fence(low, branches, gated, dout, grad_gate, rate_sum)

    out_kept, out_sent = outer_product(*gated, dout)
    part = low.astype(F32) + swap(low, "fsdp", 1).astype(F32)
    part, out_kept, out_sent, grad_gate = fence(part, out_kept, out_sent, grad_gate)
    out_got = swap(out_sent, "dp", 1)
    out_far = {u: sent_far(out_kept, out_got, u) for u in range(n_dp // 2)}
    gate_rows = jnp.sum(gate_sums.astype(F32), axis=0).astype(BF)
    rate_grad = rate_sum.reshape(n_state, SUB, LANES)[:, :chunks].reshape(n_state, width) * rates
    part, got = last_line(part, 2)
    part, got, out_far, rate_grad, gate_rows = fence(part, got, out_far, rate_grad, gate_rows)

    gate_got = to_line(gate_rows.reshape(n_line, in_rows, width))
    grads, inner_kept, inner_sent, small_kept, small_sent = conv_back(
        info, n_line, n_dp, part, got, grad_u, at, small, activ, conv_out, inner, allowed,
        dt_w_grad, rate_grad, vectors, grad_gate, (inner_own, inner_other), (gate_own, gate_other),
        normed_kept, normed_sent,
    )
    grads, gate_got, inner_kept, inner_sent, small_kept, small_sent, out_far, branches = fence(
        grads, gate_got, inner_kept, inner_sent, small_kept, small_sent, out_far, branches
    )

    folded = owned % LANES == 0
    grads[1] = shift(grads[1], "fsdp", 1)
    for u in chips[:2]:
        out_far[u] = swap(out_far[u], "dp", 2 * u)
    inner_got, small_got = swap(inner_sent, "dp", 1), swap(small_sent, "dp", 1)
    inner_grad = add_core(inner_kept, inner_got, *((small_kept, small_got) if folded else ()))
    inner_grad, grads, small_kept, small_got, out_far, branches = fence(
        inner_grad, grads, small_kept, small_got, out_far, branches
    )

    got = to_chips(inner_grad)
    inner_rows = jnp.sum(got[:, : n_line * in_rows].astype(F32), axis=0).astype(BF)
    small_sum = jnp.sum(got[:, n_line * in_rows :].astype(F32), axis=0)
    for s in steps[1:]:
        grads[s] = shift(grads[s], "fsdp", s)
    for u in chips[2:]:
        out_far[u] = swap(out_far[u], "dp", 2 * u)
    if folded:
        small_grads = small_sum.reshape(-1, n_dp, owned).transpose(1, 0, 2).reshape(-1, owned)
    else:
        small_grads = add_chips_near(small_kept + small_got.astype(F32))
    dt_g, x_g, a_g = small_grads[at.dt_w], small_grads[at.x_t], small_grads[at.a_t]
    tail_g = small_grads[at.rest]
    conv_g, conv_b_g, dt_b_g, skip_g = tail_g[:taps], tail_g[taps : taps + 1], tail_g[taps + 1 : taps + 2], tail_g[taps + 2 : taps + 3]
    small_out = [conv_g, conv_b_g[0], x_g.T, dt_g, dt_b_g[0], a_g.T, skip_g[0]]
    inner_rows, grads, out_far, branches, small_out = fence(inner_rows, grads, out_far, branches, small_out)

    inner_got = to_line(inner_rows.reshape(n_line, in_rows, width))
    grad_normed = sum(p.astype(F32) for p in grads)
    grad_normed, branches, out_far = fence(grad_normed, branches, out_far)
    out_weight_grad = sum(part.astype(F32) for part in out_far.values())
    own_valid = lax.dynamic_slice_in_dim(valid, place * held_slots, held_slots, 0)
    own_f = own_tokens.astype(F32)
    output = (own_f + own_valid * sum(p.astype(F32) for p in branches)).astype(BF)
    own_scale = lax.rsqrt(jnp.mean(own_f * own_f, axis=1, keepdims=True) + EPS)
    unit = own_f * own_scale
    grad_unit = grad_normed * full_gain
    token_grad = own_cot.astype(F32) + own_scale * (
        grad_unit - unit * jnp.mean(grad_unit * unit, axis=1, keepdims=True)
    )
    in_weight_grad, gain_grad = join_columns(inner_got, gate_got, in_weight, gain, n_dp)
    return output, token_grad, gain_grad, in_weight_grad, *small_out, out_weight_grad


def solution(mesh):
    both = ("dp", "fsdp")
    rows, cols, vec = P(both, None), P(None, both), P(both)
    return jax.shard_map(
        per_device,
        mesh=mesh,
        in_specs=(rows, P(), P(), vec, rows, cols, vec, rows, cols, vec, rows, vec, rows, rows),
        out_specs=(rows, rows, vec, rows, cols, vec, rows, cols, vec, rows, vec, rows),
        check_vma=False,
    )
```

```python
import functools

import jax
import jax.numpy as jnp
from jax import lax
from jax.experimental import pallas as pl
from jax.experimental.pallas import tpu as pltpu
from jax.sharding import PartitionSpec as P

BF, F32 = jnp.bfloat16, jnp.float32
LANES, SUB = 128, 8
LN2 = 0.6931471805599453
FAR = 1.0e5
EPS = 1e-5


def small_cost(flops):
    return pl.CostEstimate(flops=flops, bytes_accessed=1 << 16, transcendentals=0)


class Small:
    def __init__(self, rank, proj, state, taps):
        self.dt_w = slice(0, rank)
        self.x_t = slice(rank, rank + proj)
        self.a_t = slice(rank + proj, rank + proj + state)
        self.rest = slice(rank + proj + state, rank + proj + state + 16)
        self.taps, self.rows = taps, rank + proj + state + 16

    def fold(self, parts):
        rows = -(-self.rows // parts)
        return rows + -rows % 16

    def vector(self, ref, at):
        return ref[self.rest, :].astype(F32)[at : at + 1, :]


def contract_cols(left, right):
    return lax.dot_general(left, right, (((1,), (1,)), ((), ())), preferred_element_type=F32)


def scatter_lanes(ref, value, rows):
    for k in range(value.shape[1] // LANES):
        ref[pl.ds(k, rows, stride=SUB), :] = value[:, k * LANES : (k + 1) * LANES]


def gather_lanes(ref, width, rows):
    return jnp.concatenate(
        [ref[pl.ds(k, rows, stride=SUB), :] for k in range(width // LANES)], axis=1
    )


def softplus(v):
    return jnp.maximum(v, 0.0) + jnp.log1p(jnp.exp(-jnp.abs(v)))


def forward_kernel(at, bc, rank, small, act, valid, rate2, y_out, states, h_ref, dt_s, dtu_s, y_s):
    tb, width = act.shape
    n_state = rate2.shape[0] // SUB

    @pl.when(pl.program_id(0) == 0)
    def _():
        h_ref[...] = jnp.zeros_like(h_ref)
        if width < SUB * LANES:
            dt_s[...] = jnp.zeros_like(dt_s)
            dtu_s[...] = jnp.zeros_like(dtu_s)

    dt_b = at.vector(small, at.taps + 1)
    pre = jnp.dot(rank[...], small[at.dt_w, :], preferred_element_type=F32) + dt_b
    dt = softplus(pre) * valid[...]
    scatter_lanes(dt_s, dt, tb)
    scatter_lanes(dtu_s, dt * act[...].astype(F32), tb)
    rates = [rate2[n * SUB : (n + 1) * SUB, :] for n in range(n_state)]
    first = [h_ref[n * SUB : (n + 1) * SUB, :] for n in range(n_state)]
    for n in range(n_state):
        states[0, n, 0:SUB, :] = first[n]

    def token(t, h):
        at = pl.multiple_of(t * SUB, SUB)
        dt_t = dt_s[pl.ds(at, SUB), :] + bc[t, 2 * n_state]
        dtu_t = dtu_s[pl.ds(at, SUB), :]
        new, parts = [], [None, None]
        for n in range(n_state):
            hn = jnp.exp2(dt_t * rates[n]) * h[n] + dtu_t * bc[t, n]
            states[0, n, pl.ds(at + SUB, SUB), :] = hn
            term = hn * bc[t, n_state + n]
            parts[n % 2] = term if parts[n % 2] is None else parts[n % 2] + term
            new.append(hn)
        y_s[pl.ds(at, SUB), :] = parts[0] + parts[1]
        return tuple(new)

    last = lax.fori_loop(0, tb, token, tuple(first), unroll=8)
    for n in range(n_state):
        h_ref[n * SUB : (n + 1) * SUB, :] = last[n]
    y_out[...] = gather_lanes(y_s, width, tb)


def scan_forward(at, bc, rank, small, act, valid, rate2, tb):
    slots, width = act.shape
    n_state = rate2.shape[0] // SUB
    nb = slots // tb
    whole = lambda i: (0, 0)
    row = lambda i: (i, 0)
    return pl.pallas_call(
        functools.partial(forward_kernel, at),
        grid=(nb,),
        in_specs=[
            pl.BlockSpec((tb, bc.shape[1]), row, memory_space=pltpu.SMEM),
            pl.BlockSpec((tb, rank.shape[1]), row),
            pl.BlockSpec(small.shape, whole),
            pl.BlockSpec((tb, width), row),
            pl.BlockSpec((tb, 1), row),
            pl.BlockSpec(rate2.shape, whole),
        ],
        out_specs=[
            pl.BlockSpec((tb, width), row),
            pl.BlockSpec((1, n_state, (tb + 1) * SUB, LANES), lambda i: (i, 0, 0, 0)),
        ],
        out_shape=[
            jax.ShapeDtypeStruct((slots, width), F32),
            jax.ShapeDtypeStruct((nb, n_state, (tb + 1) * SUB, LANES), F32),
        ],
        scratch_shapes=[pltpu.VMEM(rate2.shape, F32)] + [pltpu.VMEM((tb * SUB, LANES), F32)] * 3,
        compiler_params=pltpu.CompilerParams(vmem_limit_bytes=61 << 20),
        cost_estimate=small_cost(1 << 20),
        name="scan_forward",
    )(bc, rank, small, act, valid, rate2)


def backward_kernel(
    at_small, bc, rank, small, act, valid, rate2, gs, states,
    packed_out, gu_out, dtw_out, vec_out, rate_grad,
    part_s, rate_out, g_ref, dt_s, dtu_s, gs_s, gdt_s, ab_s, both_s, sums,
):
    tb, width = act.shape
    n_state = rate2.shape[0] // SUB
    part = 4

    @pl.when(pl.program_id(0) == 0)
    def _():
        g_ref[...] = jnp.zeros_like(g_ref)
        rate_out[...] = jnp.zeros_like(rate_out)
        vec_out[...] = jnp.zeros_like(vec_out)
        dtw_out[...] = jnp.zeros_like(dtw_out)
        if width < SUB * LANES:
            for ref in (dt_s, dtu_s, gs_s):
                ref[...] = jnp.zeros_like(ref)

    u = act[...].astype(F32)
    ok = valid[...]
    dt_b, skip = at_small.vector(small, at_small.taps + 1), at_small.vector(small, at_small.taps + 2)
    pre = jnp.dot(rank[...], small[at_small.dt_w, :], preferred_element_type=F32) + dt_b
    dt = softplus(pre) * ok
    gs_v = gs[...]
    scatter_lanes(dt_s, dt, tb)
    scatter_lanes(dtu_s, dt * u, tb)
    scatter_lanes(gs_s, gs_v, tb)

    row = lax.broadcasted_iota(jnp.int32, (SUB, 2 * LANES), 0)
    lane = lax.broadcasted_iota(jnp.int32, (SUB, 2 * LANES), 1)
    pick = (lane // LANES == row).astype(F32).astype(BF)
    run = SUB
    span = run * SUB

    def add_lanes(group, i):
        rows = pl.ds(pl.multiple_of(i * span, span), span)
        pairs = jnp.concatenate([both_s[group % 2, j, rows, :] for j in range(part)], axis=0)
        sums[group, pl.ds(pl.multiple_of(i * SUB, SUB), SUB), :] = contract_cols(pick, pairs)

    for group in range(n_state // part):
        index = range(group * part, (group + 1) * part)
        rates = [rate2[n * SUB : (n + 1) * SUB, :] for n in index]

        def token(t, carry, after):
            g, acc = carry
            at = pl.multiple_of(t * SUB, SUB)
            dt_t, dtu_t, gs_t = [ref[pl.ds(at, SUB), :] for ref in (dt_s, dtu_s, gs_s)]
            dtd = dt_t + bc[t, 2 * n_state]
            new_g, new_acc, before, sources, reads = [], [], [], [], []
            gdt = ab = None
            for j, n in enumerate(index):
                lam = gs_t * bc[t, n_state + n] + g[j]
                sources.append(lam * dtu_t)
                reads.append(after[j] * gs_t)
                back = jnp.exp2(dtd * rates[j]) * lam
                before.append(states[0, n, pl.ds(at, SUB), :])
                thr = back * before[j]
                gdt = thr * rates[j] if gdt is None else gdt + thr * rates[j]
                ab = lam * bc[t, n] if ab is None else ab + lam * bc[t, n]
                new_g.append(back)
                new_acc.append(acc[j] + thr * dt_t)
            if group == 0:
                gdt_s[pl.ds(at, SUB), :] = gdt
                ab_s[pl.ds(at, SUB), :] = ab
            else:
                gdt_s[pl.ds(at, SUB), :] += gdt
                ab_s[pl.ds(at, SUB), :] += ab
            return (tuple(new_g), tuple(new_acc)), before, sources, reads

        def some_tokens(i, carry):
            i = tb // run - 1 - i
            if group:
                add_lanes(group - 1, i)
            late = pl.multiple_of((i + 1) * span, SUB)
            after = [states[0, n, pl.ds(late, SUB), :] for n in index]
            for k in range(run - 1, 0, -2):
                t = i * run + k
                carry, after, sources1, reads1 = token(t, carry, after)
                carry, after, sources0, reads0 = token(t - 1, carry, after)
                rows = pl.ds(pl.multiple_of((t - 1) * SUB, 2 * SUB), 2 * SUB)
                for j in range(part):
                    both_s[group % 2, j, rows, 0:LANES] = jnp.concatenate([sources0[j], sources1[j]], axis=0).astype(BF)
                    both_s[group % 2, j, rows, LANES:] = jnp.concatenate([reads0[j], reads1[j]], axis=0).astype(BF)
            return carry

        start = (
            tuple(g_ref[n * SUB : (n + 1) * SUB, :] for n in index),
            tuple(rate_out[n * SUB : (n + 1) * SUB, :] for n in index),
        )
        g, acc = lax.fori_loop(0, tb // run, some_tokens, start, unroll=tb // run)
        for j, n in enumerate(index):
            g_ref[n * SUB : (n + 1) * SUB, :] = g[j]
            rate_out[n * SUB : (n + 1) * SUB, :] = acc[j]
    for i in range(tb // run):
        add_lanes(n_state // part - 1, i)

    ab = gather_lanes(ab_s, width, tb)
    gdt = gather_lanes(gdt_s, width, tb)
    gu_out[...] = (gs_v * skip + dt * ab).astype(BF)
    grad_pre = ok * (gdt * LN2 + u * ab) * jax.nn.sigmoid(pre)
    vec_out[0:1, :] += jnp.sum(grad_pre, axis=0, keepdims=True)
    vec_out[1:2, :] += jnp.sum(gs_v * u, axis=0, keepdims=True)
    low = grad_pre.astype(BF)
    dtw_out[...] += lax.dot_general(rank[...], low, (((0,), (0,)), ((), ())), preferred_element_type=F32)
    rank_w = rank.shape[1]
    rows = pl.ds(pl.multiple_of((pl.num_programs(0) - 1 - pl.program_id(0)) * tb, tb), tb)
    part_s[rows, 0:rank_w] = contract_cols(low, small[at_small.dt_w, :]).astype(BF)

    take_row = lax.broadcasted_iota(jnp.int32, (2 * tb, tb // run * SUB), 0)
    take_lane = lax.broadcasted_iota(jnp.int32, (2 * tb, tb // run * SUB), 1)
    take = (take_lane == take_row % tb // run * SUB + take_row // tb).astype(F32).astype(BF)
    keep_row = lax.broadcasted_iota(jnp.int32, (2 * tb, part * span), 0)
    keep_lane = lax.broadcasted_iota(jnp.int32, (2 * tb, part * span), 1)
    keep = keep_lane // SUB % run == keep_row % run
    from_lane = lax.broadcasted_iota(jnp.int32, (part * span, LANES), 0)
    to_lane = lax.broadcasted_iota(jnp.int32, (part * span, LANES), 1)
    tail = jnp.zeros((2 * tb, LANES), F32)
    for group in range(n_state // part):
        chosen = jnp.dot(take, sums[group].astype(BF), preferred_element_type=F32)
        chosen = jnp.where(keep, chosen, 0.0).astype(BF)
        fold = (to_lane == group * part + from_lane // span).astype(F32).astype(BF)
        tail = tail + jnp.dot(chosen, fold, preferred_element_type=F32)
    part_s[rows, rank_w : rank_w + n_state] = tail[0:tb, 0:n_state].astype(BF)
    part_s[rows, rank_w + n_state :] = tail[tb:, 0:n_state].astype(BF)

    @pl.when(pl.program_id(0) == pl.num_programs(0) - 1)
    def _():
        proj = part_s.shape[1]
        across = lax.broadcasted_iota(jnp.int32, (proj, proj), 0) == lax.broadcasted_iota(jnp.int32, (proj, proj), 1)
        one = across.astype(F32).astype(BF)
        for b in range(part_s.shape[0] // LANES):
            packed_out[b * proj : (b + 1) * proj, :] = contract_cols(
                one, part_s[b * LANES : (b + 1) * LANES, :]
            ).astype(BF)
        for k in range(width // LANES):
            rows = pl.ds(k, n_state, stride=SUB)
            rate_grad[:, k * LANES : (k + 1) * LANES] = rate_out[rows, :] * rate2[rows, :] * LN2


def scan_backward(at, bc, rank, small, act, valid, rate2, gs, states, tb):
    slots, width = act.shape
    n_state = rate2.shape[0] // SUB
    nb = slots // tb
    whole = lambda i: (0, 0)
    row = lambda i: (nb - 1 - i, 0)
    rank_w = rank.shape[1]
    proj = rank_w + 2 * n_state
    return pl.pallas_call(
        functools.partial(backward_kernel, at),
        grid=(nb,),
        in_specs=[
            pl.BlockSpec((tb, bc.shape[1]), row, memory_space=pltpu.SMEM),
            pl.BlockSpec((tb, rank_w), row),
            pl.BlockSpec(small.shape, whole),
            pl.BlockSpec((tb, width), row),
            pl.BlockSpec((tb, 1), row),
            pl.BlockSpec(rate2.shape, whole),
            pl.BlockSpec((tb, width), row),
            pl.BlockSpec((1, n_state, (tb + 1) * SUB, LANES), lambda i: (nb - 1 - i, 0, 0, 0)),
        ],
        out_specs=[
            pl.BlockSpec((proj * slots // LANES, LANES), whole),
            pl.BlockSpec((tb, width), row),
            pl.BlockSpec((rank_w, width), whole),
            pl.BlockSpec((2, width), whole),
            pl.BlockSpec((n_state, width), whole),
        ],
        out_shape=[
            jax.ShapeDtypeStruct((proj * slots // LANES, LANES), BF),
            jax.ShapeDtypeStruct((slots, width), BF),
            jax.ShapeDtypeStruct((rank_w, width), F32),
            jax.ShapeDtypeStruct((2, width), F32),
            jax.ShapeDtypeStruct((n_state, width), F32),
        ],
        scratch_shapes=[pltpu.VMEM((slots, proj), BF)] + [pltpu.VMEM(rate2.shape, F32)] * 2
        + [pltpu.VMEM((tb * SUB, LANES), F32)] * 5
        + [pltpu.VMEM((2, 4, tb * SUB, 2 * LANES), BF), pltpu.VMEM((n_state // 4, tb, 4 * SUB * SUB), F32)],
        compiler_params=pltpu.CompilerParams(vmem_limit_bytes=61 << 20),
        cost_estimate=small_cost(1 << 20),
        name="scan_backward",
    )(bc, rank, small, act, valid, rate2, gs, states)


def silu_grad(value, sig):
    return sig * (1.0 + value * (1.0 - sig))


def place_blocks(ref, own, other, index):
    chips = own.shape[0]
    rows = ref.shape[0] // (2 * chips)
    core = lax.rem(index, 2)
    for q in range(chips):
        ref[pl.ds(pl.multiple_of((2 * q + core) * rows, rows), rows), :] = own[q, 0:rows, :]
        ref[pl.ds(pl.multiple_of((2 * q + 1 - core) * rows, rows), rows), :] = other[q, 0:rows, :]


def block_copies(ref, own, other, index, sems, first):
    chips = own.shape[0]
    rows = ref.shape[0] // (2 * chips)
    core = lax.rem(index, 2)
    found = []
    for q in range(chips):
        for blocks, d in ((own, 2 * q + core), (other, 2 * q + 1 - core)):
            at = pl.ds(pl.multiple_of(d * rows, rows), rows)
            found.append(
                pltpu.make_async_copy(blocks.at[q, pl.ds(0, rows)], ref.at[at], sems.at[first + len(found)])
            )
    return found


def read_row(ref, row, cols):
    tile = SUB if ref.dtype == F32 else 2 * SUB
    base = pl.multiple_of(row // tile * tile, tile)
    rows = ref[pl.ds(base, tile), cols].astype(F32)
    mine = lax.broadcasted_iota(jnp.int32, rows.shape, 0) == row - base
    return jnp.sum(jnp.where(mine, rows, 0.0), axis=0, keepdims=True)


def add_row(ref, row, value):
    base = pl.multiple_of(row // SUB * SUB, SUB)
    rows = ref[pl.ds(base, SUB), :]
    mine = lax.broadcasted_iota(jnp.int32, rows.shape, 0) == row - base
    ref[pl.ds(base, SUB), :] = rows + jnp.where(mine, value, 0.0)


def split_kernel(n_dp, in_w, gain, out):
    rows = in_w.shape[0]
    n_line, full, width = out.shape
    owned = width // n_dp
    top = jnp.broadcast_to(gain[...].astype(F32), (full - 2 * rows, rows)).astype(in_w.dtype)
    for to in range(n_line):
        for half in range(2):
            for d in range(n_dp):
                at = ((half * n_dp + d) * n_line + to) * owned
                out[to, half * rows : (half + 1) * rows, d * owned : (d + 1) * owned] = in_w[:, at : at + owned]
        out[to, 2 * rows :, :] = jnp.zeros((full - 2 * rows, width), in_w.dtype)
        out[to, 2 * rows :, 0:rows] = top


def split_columns(in_w, gain, n_dp, n_line):
    rows, both = in_w.shape
    width = both // (2 * n_line)
    if width // n_dp % LANES:
        blocks = in_w.reshape(rows, 2, n_dp, n_line, width // n_dp).transpose(3, 1, 0, 2, 4)
        top = jnp.broadcast_to(jnp.pad(gain, (0, width - rows)), (n_line, 16, width))
        return jnp.concatenate([blocks.reshape(n_line, 2 * rows, width), top], axis=1)
    vmem = pl.BlockSpec(memory_space=pltpu.VMEM)
    return pl.pallas_call(
        functools.partial(split_kernel, n_dp),
        in_specs=[vmem] * 2,
        out_specs=vmem,
        out_shape=jax.ShapeDtypeStruct((n_line, 2 * rows + 16, width), in_w.dtype),
        cost_estimate=small_cost(1 << 10),
        name="split_columns",
    )(in_w, gain[None])


def join_kernel(n_dp, place, *refs):
    *inner, gate, in_w, gain, out, gain_out = refs
    n_line, rows, width = gate.shape
    owned = width // n_dp
    total = jnp.zeros((rows, LANES), F32)
    for s in range(n_line):
        for half in range(2):
            line = from_place(place[0], s, n_line) if half == 0 else s
            for d in range(n_dp):
                cols = slice(d * owned, (d + 1) * owned)
                block = (inner[s][:, cols] if half == 0 else gate[s, :, cols]).astype(F32)
                at = ((half * n_dp + d) * n_line + line) * owned
                at = pl.ds(pl.multiple_of(at, owned), owned) if half == 0 else slice(at, at + owned)
                out[:, at] = block
                term = block * in_w[:, at].astype(F32)
                for low in range(0, owned, LANES):
                    total = total + term[:, low : low + LANES]
    ones = jnp.ones((SUB, LANES), F32)
    sums = lax.dot_general(
        ones, total, (((1,), (1,)), ((), ())), precision=lax.Precision.HIGHEST, preferred_element_type=F32
    )
    gain_out[...] = sums[0:1, :] / gain[...].astype(F32)


def join_columns(place, inner, gate, in_w, gain, n_dp):
    rows, both = in_w.shape
    n_line, _, width = gate.shape
    if width // n_dp % LANES:
        blocks = jnp.stack([in_order(inner, "fsdp"), gate]).astype(F32).reshape(2, n_line, rows, n_dp, -1)
        full = blocks.transpose(2, 0, 3, 1, 4).reshape(rows, both)
        return full, jnp.sum(full * in_w.astype(F32), axis=1) / gain.astype(F32)
    vmem = pl.BlockSpec(memory_space=pltpu.VMEM)
    full, gain_grad = pl.pallas_call(
        functools.partial(join_kernel, n_dp),
        in_specs=[pl.BlockSpec(memory_space=pltpu.SMEM)] + [vmem] * (n_line + 3),
        out_specs=[vmem] * 2,
        out_shape=[jax.ShapeDtypeStruct((rows, both), F32), jax.ShapeDtypeStruct((1, rows), F32)],
        cost_estimate=small_cost(1 << 10),
        name="join_columns",
    )(place[None], *inner, gate, in_w, gain[None])
    return full, gain_grad[0]


def column_block(width, slots):
    return 256 if width % 256 == 0 and slots <= 1024 else LANES


def from_place(place, steps, n_line):
    return lax.rem(place - steps + n_line, n_line)


def outer(lefts, right, outs):
    rows = min(256, lefts[0].shape[1])

    @pl.loop(0, lefts[0].shape[1] // rows)
    def _(r):
        at = pl.ds(pl.multiple_of(r * rows, rows), rows)
        for left, out in zip(lefts, outs):
            found = lax.dot_general(left[:, at], right[...], (((0,), (0,)), ((), ())), preferred_element_type=F32)
            out[at, :] = found.astype(out.dtype)


def outer_kernel(kept, sent, right, kept_out, sent_out):
    outer((kept, sent), right, (kept_out, sent_out))


def outer_product(kept, sent, right):
    shape = (kept.shape[1], right.shape[1])
    vmem = pl.BlockSpec(memory_space=pltpu.VMEM)
    return pl.pallas_call(
        outer_kernel,
        in_specs=[vmem] * 3,
        out_specs=[vmem] * 2,
        out_shape=[jax.ShapeDtypeStruct(shape, BF)] * 2,
        compiler_params=pltpu.CompilerParams(vmem_limit_bytes=61 << 20),
        cost_estimate=small_cost(1 << 20),
        name="outer_product",
    )(kept, sent, right)


def to_shifts(source, outs, place):
    rows = outs[0].shape[0]
    for s, out in enumerate(outs):
        at = pl.multiple_of(lax.rem(place + s, len(outs)) * rows, rows)
        out[...] = source[pl.ds(at, rows), :]


def split_cores(ref, kept, sent, index, n_dp):
    size = ref.shape[1] // n_dp
    core = lax.rem(index, 2)
    for q in range(kept.shape[1] // size):
        cols = slice(q * size, (q + 1) * size)
        kept[:, cols] = ref[:, pl.ds(pl.multiple_of((2 * q + core) * size, size), size)]
        sent[:, cols] = ref[:, pl.ds(pl.multiple_of((2 * q + 1 - core) * size, size), size)]


def project_kernel(n_line, n_dp, at, info, *refs):
    toks, refs = refs[:n_line], refs[n_line:]
    own, other, small, allowed, gain, normed, kept, sent, inner, conv_out, activ, part, w_nat, inner_s, ext = refs
    held, model = toks[0].shape
    slots = held * n_line
    width = w_nat.shape[1]
    taps = at.taps
    rim = taps - 1
    rows_dp = model // n_dp
    core = lax.rem(info[0], 2)
    for q in range(n_dp // 2):
        for blocks, d in ((own, 2 * q + core), (other, 2 * q + 1 - core)):
            found = blocks[q, rows_dp:, 0:rows_dp].astype(F32)[0:1, :]
            gain[:, pl.ds(pl.multiple_of(d * rows_dp, rows_dp), rows_dp)] = found
    step = 32
    for s, tok in enumerate(toks):
        base = from_place(info[1], s, n_line) * held

        @pl.loop(0, held // step)
        def _(i):
            x = tok[pl.ds(pl.multiple_of(i * step, step), step), :].astype(F32)
            scale = lax.rsqrt(jnp.mean(x * x, axis=1, keepdims=True) + EPS)
            normed[pl.ds(pl.multiple_of(base + i * step, step), step), :] = (x * scale * gain[...]).astype(BF)

    split_cores(normed, kept, sent, info[0], n_dp)
    place_blocks(w_nat, own, other, info[0])
    cb = column_block(width, slots)

    @pl.loop(0, width // cb)
    def _(c):
        cols = pl.ds(pl.multiple_of(c * cb, cb), cb)
        inner_s[...] = jnp.dot(normed[...], w_nat[:, cols], preferred_element_type=F32)
        inner[:, cols] = inner_s[...].astype(BF)
        vectors = small[at.rest, cols].astype(F32)
        for f in range(n_line):
            rows = slice(f * held, (f + 1) * held)
            ext[SUB : SUB + held, :] = inner_s[rows, :]
            for k in range(1, rim + 1):
                if f == 0:
                    ext[SUB - k : SUB - k + 1, :] = jnp.zeros((1, cb), F32)
                else:
                    ext[SUB - k : SUB - k + 1, :] = read_row(inner_s, (f - 1) * held + info[1 + f] - k, slice(None))
            total = vectors[taps : taps + 1, :]
            for lag in range(taps):
                tapped = ext[SUB - lag : SUB - lag + held, :]
                total = total + vectors[rim - lag : rim - lag + 1, :] * tapped * allowed[rows, lag : lag + 1]
            conv_out[rows, cols] = total.astype(BF)
            activ[rows, cols] = (total * jax.nn.sigmoid(total)).astype(BF)

    proj = part.shape[0] * LANES // slots
    for b in range(slots // LANES):
        found = contract_cols(small[at.x_t, :], activ[b * LANES : (b + 1) * LANES, :])
        part[b * proj : (b + 1) * proj, :] = found.astype(BF)


def project(info, n_line, n_dp, toks, own, other, at, small, allowed):
    held, model = toks[0].shape
    slots = held * n_line
    width, proj = small.shape[1], at.x_t.stop - at.x_t.start
    vmem = pl.BlockSpec(memory_space=pltpu.VMEM)
    shapes = [
        ((1, model), F32), ((slots, model), BF), ((slots, model // 2), BF), ((slots, model // 2), BF),
        ((slots, width), BF), ((slots, width), BF), ((slots, width), BF), ((proj * slots // LANES, LANES), BF),
    ]
    return pl.pallas_call(
        functools.partial(project_kernel, n_line, n_dp, at),
        in_specs=[pl.BlockSpec(memory_space=pltpu.SMEM)] + [vmem] * (4 + len(toks)),
        out_specs=[vmem] * len(shapes),
        out_shape=[jax.ShapeDtypeStruct(s, t) for s, t in shapes],
        scratch_shapes=[
            pltpu.VMEM((model, width), BF),
            pltpu.VMEM((slots, column_block(width, slots)), F32),
            pltpu.VMEM((SUB + slots // n_line, column_block(width, slots)), F32),
        ],
        compiler_params=pltpu.CompilerParams(vmem_limit_bytes=61 << 20),
        cost_estimate=small_cost(1 << 20),
        name="project",
    )(info, *toks, own, other, small, allowed)


def gate_kernel(n_line, n_dp, at, info, own, other, normed, y, act, small, *refs):
    out_own, out_other, refs = refs[: n_dp // 2], refs[n_dp // 2 : n_dp], refs[n_dp:]
    branches, refs = refs[:n_line], refs[n_line:]
    gate, gated, o_nat, *halves, branch, w_nat = refs
    slots, width = y.shape
    model = normed.shape[1]
    place_blocks(w_nat, own, other, info[0])
    rows = width // n_dp
    core, chip = lax.rem(info[0], 2), lax.div(info[0], 2)
    for u in range(n_dp // 2):
        first = 2 * jnp.bitwise_xor(chip, u)
        o_nat[pl.ds(pl.multiple_of((first + core) * rows, rows), rows), :] = out_own[u][0:rows, :]
        o_nat[pl.ds(pl.multiple_of((first + 1 - core) * rows, rows), rows), :] = out_other[u][0:rows, :]
    cb = column_block(width, slots)

    @pl.loop(0, width // cb)
    def _(c):
        cols = pl.ds(pl.multiple_of(c * cb, cb), cb)
        value = jnp.dot(normed[...], w_nat[:, cols], preferred_element_type=F32)
        gate[:, cols] = value
        skip = small[at.rest, cols].astype(F32)[at.taps + 2 : at.taps + 3, :]
        scan_out = y[:, cols] + skip * act[:, cols].astype(F32)
        gated[:, cols] = (scan_out * value * jax.nn.sigmoid(value)).astype(BF)

    mb = column_block(model, slots)

    @pl.loop(0, model // mb)
    def _(c):
        cols = pl.ds(pl.multiple_of(c * mb, mb), mb)
        branch[:, cols] = jnp.dot(gated[...], o_nat[:, cols], preferred_element_type=F32).astype(BF)

    to_shifts(branch, branches, info[1])
    if halves:
        split_cores(gated, *halves, info[0], n_dp)


def gate_block(info, n_line, n_dp, own, other, out_own, out_other, normed, y, act, at, small):
    slots, width = y.shape
    model = normed.shape[1]
    vmem = pl.BlockSpec(memory_space=pltpu.VMEM)
    shapes = [((slots // n_line, model), BF)] * n_line
    shapes += [((slots, width), F32), ((slots, width), BF), ((width, model), BF)]
    if width // n_dp % LANES == 0:
        shapes += [((slots, width // 2), BF)] * 2
    outs = pl.pallas_call(
        functools.partial(gate_kernel, n_line, n_dp, at),
        in_specs=[pl.BlockSpec(memory_space=pltpu.SMEM)] + [vmem] * (6 + n_dp),
        out_specs=[vmem] * len(shapes),
        out_shape=[jax.ShapeDtypeStruct(s, t) for s, t in shapes],
        scratch_shapes=[pltpu.VMEM((slots, model), BF), pltpu.VMEM((model, width), BF)],
        compiler_params=pltpu.CompilerParams(vmem_limit_bytes=61 << 20),
        cost_estimate=small_cost(1 << 20),
        name="gate_block",
    )(info, own, other, normed, y, act, small, *out_own, *out_other)
    branches, (gate, gated, o_nat), halves = list(outs[:n_line]), outs[n_line : n_line + 3], outs[n_line + 3 :]
    return branches, gate, o_nat, *(halves or cores(gated, 1))


def gate_back_kernel(n_line, at, info, *refs):
    cots, refs = refs[:n_line], refs[n_line:]
    o_nat, gate, y, act, small, valid, normed, gs, grad_gate, dout, product = refs
    slots, width = y.shape
    held, model = cots[0].shape
    for s, cot in enumerate(cots):
        rows = pl.ds(pl.multiple_of(from_place(info[1], s, n_line) * held, held), held)
        dout[rows, :] = (cot[...].astype(F32) * valid[rows, :]).astype(BF)

    cb = column_block(width, slots)

    @pl.loop(0, width // cb)
    def _(c):
        cols = pl.ds(pl.multiple_of(c * cb, cb), cb)
        grad = lax.dot_general(dout[...], o_nat[cols, :], (((1,), (1,)), ((), ())), preferred_element_type=F32)
        value = gate[:, cols]
        sig = jax.nn.sigmoid(value)
        skip = small[at.rest, cols].astype(F32)[at.taps + 2 : at.taps + 3, :]
        scan_out = y[:, cols] + skip * act[:, cols].astype(F32)
        gs[:, cols] = grad * value * sig
        grad_gate[:, cols] = (grad * scan_out * silu_grad(value, sig)).astype(BF)

    outer((normed,), grad_gate, (product,))


def gate_back(info, n_line, cots, o_nat, gate, y, act, at, small, valid, normed):
    slots, width = y.shape
    model = o_nat.shape[1]
    vmem = pl.BlockSpec(memory_space=pltpu.VMEM)
    shapes = [((slots, width), F32), ((slots, width), BF), ((slots, model), BF)]
    shapes += [((model, width), BF)]
    return pl.pallas_call(
        functools.partial(gate_back_kernel, n_line, at),
        in_specs=[pl.BlockSpec(memory_space=pltpu.SMEM)] + [vmem] * (7 + len(cots)),
        out_specs=[vmem] * len(shapes),
        out_shape=[jax.ShapeDtypeStruct(s, t) for s, t in shapes],
        compiler_params=pltpu.CompilerParams(vmem_limit_bytes=61 << 20),
        cost_estimate=small_cost(1 << 20),
        name="gate_back",
    )(info, *cots, o_nat, gate, y, act, small, valid, normed)


def together(slots):
    return slots <= 1024


def conv_back_kernel(n_line, n_dp, at, info, gp_part, gp_got, gu, small, act, conv_out, inner, allowed, dtw, rate_grad, scan_vec,
                     grad_gate, *refs):
    slots, width = gu.shape
    inner_own, inner_other, gate_own, gate_other, *refs = refs
    halves_far, refs = (refs[:2], refs[2:]) if together(slots) else ((), refs)
    normed_far, *refs = refs
    products_far, refs = (refs[:2], refs[2:]) if together(slots) else ((), refs)
    gi_low, refs = (None, refs) if together(slots) else (refs[0], refs[1:])
    kept, sent, x_grad, vec, ext, gi, tail, grad_normed, column, gp, arrived, left, w_nat, gate_nat, *refs = refs
    halves = ()
    copies = block_copies(w_nat, inner_own, inner_other, info[0], arrived, 0)
    copies += block_copies(gate_nat, gate_own, gate_other, info[0], arrived, n_dp)
    if together(slots):
        gi_low, *refs = refs
        halves, products = refs[:2], refs[2:]
        for i, (src, dst) in enumerate(zip(halves_far, halves)):
            copies.append(pltpu.make_async_copy(src, dst, arrived.at[2 * n_dp + i]))
    for copy in copies:
        copy.start()
    leaving = []

    def leave(src, dst):
        copy = pltpu.make_async_copy(src, dst, left.at[len(leaving)])
        copy.start()
        leaving.append(copy)

    gp[...] = (gp_part[...] + gp_got[...].astype(F32)).astype(BF)
    held = slots // n_line
    taps = at.taps
    rim = taps - 1
    cb = column_block(width, slots)
    proj = x_grad.shape[0]
    x_grad[...] = sum(
        jnp.dot(gp[b * proj : (b + 1) * proj, :], act[b * LANES : (b + 1) * LANES, :], preferred_element_type=F32)
        for b in range(slots // LANES)
    )
    vec[...] = jnp.zeros_like(vec)
    for lag in range(taps):
        tail[lag, held : held + SUB, :] = jnp.zeros((SUB, cb), F32)

    @pl.loop(0, width // cb)
    def _(c):
        cols = pl.ds(pl.multiple_of(c * cb, cb), cb)
        vectors = small[at.rest, cols].astype(F32)
        for f in range(n_line - 1, -1, -1):
            rows = slice(f * held, (f + 1) * held)
            ext[SUB : SUB + held, :] = inner[rows, cols].astype(F32)
            for k in range(1, rim + 1):
                if f == 0:
                    ext[SUB - k : SUB - k + 1, :] = jnp.zeros((1, cb), F32)
                else:
                    ext[SUB - k : SUB - k + 1, :] = read_row(inner, (f - 1) * held + info[1 + f] - k, cols)
            back = [
                lax.dot_general(
                    gp[b * proj : (b + 1) * proj, :], small[at.x_t, cols], (((0,), (0,)), ((), ())),
                    preferred_element_type=F32,
                )
                for b in range(f * held // LANES, (f + 1) * held // LANES)
            ]
            grad = gu[rows, cols].astype(F32) + jnp.concatenate(back, axis=0)
            co = conv_out[rows, cols].astype(F32)
            grad = grad * silu_grad(co, jax.nn.sigmoid(co))
            vec[taps : taps + 1, cols] += jnp.sum(grad, axis=0, keepdims=True)
            for lag in range(taps):
                weighted = grad * allowed[rows, lag : lag + 1]
                vec[rim - lag : rim - lag + 1, cols] += jnp.sum(
                    weighted * ext[SUB - lag : SUB - lag + held, :], axis=0, keepdims=True
                )
                tail[lag, 0:held, :] = weighted * vectors[rim - lag : rim - lag + 1, :]
            total = tail[0, 0:held, :]
            for lag in range(1, taps):
                total = total + tail[lag, lag : lag + held, :]
            gi[rows, :] = total
            if f + 1 < n_line:
                for k in range(1, rim + 1):
                    add_row(gi, f * held + info[2 + f] - k, gi[slots + k : slots + k + 1, :])
            for k in range(1, rim + 1):
                row = tail[k, 0:1, :]
                for lag in range(k + 1, taps):
                    row = row + tail[lag, lag - k : lag - k + 1, :]
                gi[slots + k : slots + k + 1, :] = row
        gi_low[:, cols] = gi[0:slots, :].astype(BF)

    for copy in copies:
        copy.wait()
    model = w_nat.shape[0]
    mb = column_block(model, slots)

    @pl.loop(0, model // mb)
    def _(c):
        cols = pl.ds(pl.multiple_of(c * mb, mb), mb)
        found = contract_cols(gi_low[...], w_nat[cols, :]) + contract_cols(grad_gate[...], gate_nat[cols, :])
        grad_normed[:, cols] = found.astype(BF)

    leave(grad_normed, normed_far)
    if halves:
        step = model // 2 // 4
        for r in range(4):
            rows = slice(r * step, (r + 1) * step)
            for half, product, out in zip(halves, products, products_far):
                product[rows, :] = lax.dot_general(
                    half[:, rows], gi_low[...], (((0,), (0,)), ((), ())), preferred_element_type=F32
                ).astype(BF)
                leave(product.at[pl.ds(r * step, step)], out.at[pl.ds(r * step, step)])
    vec[taps + 1 : taps + 3, :] = scan_vec[...]
    owned = width // n_dp
    if kept.shape[0] == 1:
        kept[0, at.dt_w, :], kept[0, at.x_t, :], kept[0, at.a_t, :], kept[0, at.rest, :] = (
            dtw[...], x_grad[...], rate_grad[...], vec[...]
        )
        for copy in leaving:
            copy.wait()
        return
    core = lax.rem(info[0], 2)
    fold = kept.shape[1]
    for q in range(n_dp // 2):
        for ref, d in ((kept, 2 * q + core), (sent, 2 * q + 1 - core)):
            cols = pl.ds(pl.multiple_of(d * owned, owned), owned)
            for rows, source in ((at.dt_w, dtw), (at.x_t, x_grad), (at.a_t, rate_grad), (at.rest, vec)):
                column[rows, :] = source[:, cols]
            for b in range(width // owned):
                ref[q, :, b * owned : (b + 1) * owned] = column[b * fold : (b + 1) * fold, :].astype(ref.dtype)
    for copy in leaving:
        copy.wait()


def conv_back(info, n_line, n_dp, gp_part, gp_got, gu, at, small, act, conv_out, inner, allowed, dtw, rate_grad, scan_vec, grad_gate,
              inner_blocks, gate_blocks, normed_k, normed_s):
    slots, width = gu.shape
    held, model = slots // n_line, 2 * normed_k.shape[1]
    cb = column_block(width, slots)
    owned = width // n_dp
    tiles, one = owned % LANES == 0, together(slots)
    vmem, away = pl.BlockSpec(memory_space=pltpu.VMEM), pl.BlockSpec(memory_space=pl.ANY)
    fold = at.fold(n_dp)
    shape = (n_dp // 2, fold, width) if tiles else (1, at.rows, width)
    later = [*inner_blocks, *gate_blocks] + ([normed_k, normed_s] if one else [])
    low, half = jax.ShapeDtypeStruct((slots, width), BF), jax.ShapeDtypeStruct((model // 2, width), BF)
    outs = pl.pallas_call(
        functools.partial(conv_back_kernel, n_line, n_dp, at),
        in_specs=[pl.BlockSpec(memory_space=pltpu.SMEM)] + [vmem] * 12 + [away] * len(later),
        out_specs=[away] + ([away] * 2 if one else [vmem]) + [vmem] * 2,
        out_shape=[jax.ShapeDtypeStruct((slots, model), BF)]
        + ([half] * 2 if one else [low])
        + [
            jax.ShapeDtypeStruct(shape, F32),
            jax.ShapeDtypeStruct(shape if tiles else (SUB, LANES), BF if tiles else F32),
        ],
        scratch_shapes=[
            pltpu.VMEM((at.x_t.stop - at.x_t.start, width), F32),
            pltpu.VMEM((16, width), F32),
            pltpu.VMEM((SUB + held, cb), F32),
            pltpu.VMEM((slots + SUB, cb), F32),
            pltpu.VMEM((at.taps, held + SUB, cb), F32),
            pltpu.VMEM((slots, model), BF),
            pltpu.VMEM((n_dp * fold, owned), F32),
            pltpu.VMEM(gp_got.shape, BF),
            pltpu.SemaphoreType.DMA((2 * n_dp + 2,)),
            pltpu.SemaphoreType.DMA((9,)),
        ]
        + [pltpu.VMEM((model, width), BF)] * 2
        + ([pltpu.VMEM((slots, width), BF)] + [pltpu.VMEM((slots, model // 2), BF)] * 2 if one else [])
        + ([pltpu.VMEM((model // 2, width), BF)] * 2 if one else []),
        compiler_params=pltpu.CompilerParams(vmem_limit_bytes=61 << 20),
        cost_estimate=small_cost(1 << 20),
        name="conv_back",
    )(info, gp_part, gp_got, gu, small, act, conv_out, inner, allowed, dtw, rate_grad, scan_vec, grad_gate, *later)
    grad_normed, *products, kept, sent = outs
    if not one:
        products = outer_product(normed_k, normed_s, products[0])
    if not tiles:
        kept, sent = [
            part.reshape(at.rows, n_dp // 2, owned).transpose(1, 0, 2) for part in cores(kept[0], 1)
        ]
    return grad_normed, *products, kept, sent.astype(BF)


def swap(value, axis, mask):
    count = lax.axis_size(axis)
    return lax.ppermute(value, axis, [(i, i ^ mask) for i in range(count)])


def shift(value, axis, steps):
    count = lax.axis_size(axis)
    return lax.ppermute(value, axis, [(i, (i + steps) % count) for i in range(count)])


def chips_of(axis):
    return [list(range(core, lax.axis_size(axis), 2)) for core in range(2)]


def to_line(blocks):
    return lax.all_to_all(blocks, "fsdp", 0, 0)


def to_chips(blocks):
    return lax.all_to_all(blocks, "dp", 0, 0, axis_index_groups=chips_of("dp"))


def repeated(value, count):
    return jnp.broadcast_to(value[None], (count,) + value.shape)


def in_order(parts, axis):
    count, me = lax.axis_size(axis), lax.axis_index(axis)
    up = jnp.stack([parts[-k % count] for k in range(count)] * 2)
    return lax.dynamic_slice_in_dim(up, lax.rem(count - me, count), count, 0)


def by_chip(parts):
    chip, count = lax.div(lax.axis_index("dp"), 2), len(parts)
    bits = count.bit_length() - 1
    cube = jnp.stack(parts).reshape((2,) * bits + parts[0].shape)
    for place in range(bits):
        mine = lax.rem(chip >> (bits - 1 - place), 2) == 1
        cube = jnp.where(mine, jnp.flip(cube, place), cube)
    return cube.reshape((count,) + parts[0].shape)


def by_device(own, other):
    core = lax.rem(lax.axis_index("dp"), 2) == 1
    both = jnp.where(core, jnp.stack([other, own], axis=1), jnp.stack([own, other], axis=1))
    return lax.optimization_barrier(both.reshape((-1,) + own.shape[1:]))


def last_line(value, reach):
    while True:
        got = swap(value.astype(BF), "fsdp", reach)
        reach *= 2
        if reach >= lax.axis_size("fsdp"):
            return value, got
        value = value + got.astype(F32)


def fence(*values):
    flat, shape = jax.tree.flatten(values)
    return jax.tree.unflatten(shape, lax.optimization_barrier(tuple(flat)))


def cores(value, axis):
    cut = value.shape[:axis] + (lax.axis_size("dp") // 2, 2, -1) + value.shape[axis + 1 :]
    cube = value.reshape(cut)
    core = lax.rem(lax.axis_index("dp"), 2)
    found = [lax.dynamic_index_in_dim(cube, at, axis + 1, keepdims=False) for at in (core, 1 - core)]
    flat = value.shape[:axis] + (value.shape[axis] // 2,) + value.shape[axis + 1 :]
    return [part.reshape(flat) for part in found]


def add_core_kernel(chip, kept, got, small_kept, small_got, *outs):
    rows = kept.shape[0] // len(outs)
    for u, out in enumerate(outs):
        q = jnp.bitwise_xor(chip[0], u)
        at = pl.ds(pl.multiple_of(q * rows, rows), rows)
        out[0:rows, :] = (kept[at, :].astype(F32) + got[at, :].astype(F32)).astype(BF)
        out[rows:, :] = (small_kept[q] + small_got[q].astype(F32)).astype(BF)


def add_core(kept, got, small_kept, small_got):
    chips, width = lax.axis_size("dp") // 2, kept.shape[1]
    rows = kept.shape[0] // chips + small_kept.shape[1]
    vmem = pl.BlockSpec(memory_space=pltpu.VMEM)
    return pl.pallas_call(
        add_core_kernel,
        in_specs=[pl.BlockSpec(memory_space=pltpu.SMEM)] + [vmem] * 4,
        out_specs=[vmem] * chips,
        out_shape=[jax.ShapeDtypeStruct((rows, width), BF)] * chips,
        compiler_params=pltpu.CompilerParams(vmem_limit_bytes=61 << 20),
        cost_estimate=small_cost(1 << 10),
        name="add_core",
    )(lax.div(lax.axis_index("dp"), 2)[None], kept, got, small_kept, small_got)


def add_chips_near(blocks):
    count, chip = lax.axis_size("dp") // 2, lax.div(lax.axis_index("dp"), 2)
    total = lax.dynamic_index_in_dim(blocks, chip, 0, keepdims=False)
    for u in range(1, count):
        total = total + far(blocks, u).astype(F32)
    return total


def sum_chips_kernel(count, place, *refs):
    blocks, (*outs, small) = refs[:count], refs[count:]
    rows = outs[0].shape[0]
    for s, out in enumerate(outs):
        at = pl.ds(pl.multiple_of(lax.rem(place[0] + s, len(outs)) * rows, rows), rows)
        out[...] = sum(block[at, :].astype(F32) for block in blocks).astype(BF)
    first = rows * len(outs)
    small[...] = sum(block[first:, :].astype(F32) for block in blocks)


def sum_chips(place, blocks, n_line, rows):
    full, width = blocks[0].shape
    vmem = pl.BlockSpec(memory_space=pltpu.VMEM)
    *parts, small = pl.pallas_call(
        functools.partial(sum_chips_kernel, len(blocks)),
        in_specs=[pl.BlockSpec(memory_space=pltpu.SMEM)] + [vmem] * len(blocks),
        out_specs=[vmem] * (n_line + 1),
        out_shape=[jax.ShapeDtypeStruct((rows, width), BF)] * n_line
        + [jax.ShapeDtypeStruct((full - n_line * rows, width), F32)],
        compiler_params=pltpu.CompilerParams(vmem_limit_bytes=61 << 20),
        cost_estimate=small_cost(1 << 10),
        name="sum_chips",
    )(place[None], *blocks)
    return parts, small


def sent_far(kept, got, u):
    rows = kept.shape[0] // (lax.axis_size("dp") // 2)
    at = jnp.bitwise_xor(lax.div(lax.axis_index("dp"), 2), u) * rows
    return sum(lax.dynamic_slice_in_dim(part, at, rows, 0).astype(F32) for part in (kept, got)).astype(BF)


def far(blocks, u):
    block = lax.dynamic_index_in_dim(blocks, jnp.bitwise_xor(lax.div(lax.axis_index("dp"), 2), u), 0, keepdims=False)
    return swap(block.astype(BF), "dp", 2 * u)


def halves_kernel(chip, kept, got, first, second, *held):
    rows, half = held[0].shape
    outs = {
        (0, 0): held[0], (2, 0): held[1], (0, 1): held[2], (1, 1): held[3],
        (1, 0): first.at[0:rows], (3, 0): first.at[rows : 2 * rows],
        (2, 1): second.at[0:rows], (3, 1): second.at[rows : 2 * rows],
    }
    for (u, side), out in outs.items():
        at = pl.ds(pl.multiple_of(jnp.bitwise_xor(chip[0], u) * rows, rows), rows)
        cols = slice(side * half, (side + 1) * half)
        out[...] = (kept[at, cols].astype(F32) + got[at, cols].astype(F32)).astype(BF)


def chip_sum(kept, got):
    chips, (rows, width) = lax.axis_size("dp") // 2, kept.shape
    if chips != 4 or rows // chips % LANES:
        return ChipSum([sent_far(kept, got, u) for u in range(chips)])
    rows, half = rows // chips, width // 2
    vmem = pl.BlockSpec(memory_space=pltpu.VMEM)
    first, second, *held = pl.pallas_call(
        halves_kernel,
        in_specs=[pl.BlockSpec(memory_space=pltpu.SMEM)] + [vmem] * 2,
        out_specs=[vmem] * 6,
        out_shape=[jax.ShapeDtypeStruct((2 * rows, half), BF)] * 2 + [jax.ShapeDtypeStruct((rows, half), BF)] * 4,
        compiler_params=pltpu.CompilerParams(vmem_limit_bytes=61 << 20),
        cost_estimate=small_cost(1 << 10),
        name="chip_halves",
    )(lax.div(lax.axis_index("dp"), 2)[None], kept, got)
    return ChipSum(held, [first, second])


class ChipSum:
    def __init__(self, held, sends=None):
        self.direct = sends is None
        self.held, self.sends, self.got = held, sends or held[1:], []

    def fenced(self, *others):
        (self.held, self.sends, self.got), *others = fence((self.held, self.sends, self.got), *others)
        return others

    def first(self):
        self.got = [swap(send, "dp", 2 * u) for u, send in enumerate(self.sends, 1)]
        self.sends = []

    def add(self):
        if self.direct:
            return
        rows = self.held[0].shape[0]
        own = [h.astype(F32) + got[:rows].astype(F32) for h, got in zip(self.held[::2], self.got)]
        self.sends = [(h.astype(F32) + got[rows:].astype(F32)).astype(BF) for h, got in zip(self.held[1::2], self.got)]
        self.held, self.got = own, []

    def second(self):
        if not self.direct:
            self.got = [swap(send, "dp", 2 * u) for u, send in zip((2, 1), self.sends)]

    def total(self):
        if self.direct:
            return sum(part.astype(F32) for part in (self.held[0], *self.got))
        return jnp.concatenate([h + got.astype(F32) for h, got in zip(self.held, self.got)], axis=1)


def per_device(
    tokens, counts, lengths, gain, in_weight, conv_weight, conv_bias, x_weight,
    dt_weight, dt_bias, a_log, skip, out_weight, cotangent,
):
    n_dp, n_line = lax.axis_size("dp"), lax.axis_size("fsdp")
    group, place = lax.axis_index("dp"), lax.axis_index("fsdp")
    held_slots, model = tokens.shape
    slots = held_slots * n_line
    owned = skip.shape[0]
    width = owned * n_dp
    in_rows = in_weight.shape[0]
    taps, rank_w, n_state = conv_weight.shape[0], dt_weight.shape[0], a_log.shape[1]
    proj = x_weight.shape[1]
    tb = 64 if slots % 64 == 0 else slots

    count_row = lax.dynamic_index_in_dim(counts, group, 0, keepdims=False)
    length_row = lax.dynamic_index_in_dim(lengths, group, 0, keepdims=False)
    info = jnp.concatenate([jnp.stack([group, place]).astype(jnp.int32), count_row])
    offsets = jnp.cumsum(count_row) - count_row
    within = lax.broadcasted_iota(jnp.int32, (n_line, held_slots), 1)
    present = within < count_row[:, None]
    position = offsets[:, None] + within
    second, third = length_row[0], length_row[0] + length_row[1]
    begin = jnp.where(position >= third, third, jnp.where(position >= second, second, 0))
    marks = jnp.stack(
        [position - lag >= begin for lag in range(taps)] + [present, present & (position == begin)]
    ).astype(F32).reshape(taps + 2, slots).T
    allowed, valid, opens = marks[:, :taps], marks[:, taps : taps + 1], marks[:, taps + 1 :] * FAR

    own_tokens, own_cot = tokens, cotangent
    steps = range(1, n_line)
    chips = range(1, n_dp // 2)
    at = Small(rank_w, proj, n_state, taps)

    parts = split_columns(in_weight, gain, n_dp, n_line)
    rest = jnp.concatenate([conv_weight, conv_bias[None], dt_bias[None], skip[None]], axis=0)
    rest = jnp.pad(rest, ((0, 16 - rest.shape[0]), (0, 0)))
    small = jnp.concatenate([dt_weight, x_weight.T, a_log.T, rest], axis=0)
    small_rows = -(-at.rows * owned // model)
    small_rows += -small_rows % 16
    small = jnp.pad(small, ((0, small_rows * model // owned - at.rows), (0, 0))).reshape(small_rows, model)
    packed = jnp.concatenate([out_weight, small], axis=0)
    parts, tokens = fence(parts, tokens)
    parts = to_line(parts)
    toks = {0: tokens, 1: shift(tokens, "fsdp", 1)}
    near = [packed] + [swap(packed, "dp", 2 * u) for u in chips]
    own_valid = lax.dynamic_slice_in_dim(valid, place * held_slots, held_slots, 0)
    parts, toks, near, info, allowed, valid, opens, own_valid = fence(
        parts, toks, near, info, allowed, valid, opens, own_valid
    )

    gain_rows = jnp.pad(parts[:, 2 * in_rows, :in_rows].reshape(1, -1), ((0, 15), (0, width - n_line * in_rows)))
    inner_block = jnp.concatenate([parts[:, :in_rows].reshape(-1, width), gain_rows], axis=0)
    gate_in = parts[:, in_rows : 2 * in_rows].reshape(-1, width)
    inner_rep, gate_in, toks = fence(repeated(inner_block, n_dp // 2), gate_in, toks)
    inner_own = to_chips(inner_rep)
    for s in steps[1:]:
        toks[s] = shift(toks[0], "fsdp", s)
    gate_rep = repeated(gate_in, n_dp // 2)
    small = by_chip([block[owned:].reshape(-1, owned)[: at.rows] for block in near])
    small_other = swap(small, "dp", 1)
    inner_own, toks, near, gate_rep, cotangent, small, small_other = fence(
        inner_own, toks, near, gate_rep, cotangent, small, small_other
    )

    inner_other = swap(inner_own, "dp", 1)
    small = by_device(small, small_other).transpose(1, 0, 2).reshape(-1, width)
    inner_own, inner_other, toks, cotangent, near, small = fence(inner_own, inner_other, toks, cotangent, near, small)
    rates = -jnp.exp(small[at.a_t].astype(F32))
    chunks = width // LANES
    rate2 = jnp.pad(
        (rates * (1.0 / LN2)).reshape(n_state, chunks, LANES), ((0, 0), (0, SUB - chunks), (0, 0))
    ).reshape(n_state * SUB, LANES)

    gate_own = to_chips(gate_rep)
    cots = {0: cotangent, 1: shift(cotangent, "fsdp", 1)}
    out_other = [swap(block, "dp", 1) for block in near[: len(near) // 2]]
    full_gain, normed, normed_kept, normed_sent, inner, conv_out, activ, low = project(
        info, n_line, n_dp, [toks[s] for s in range(n_line)], inner_own, inner_other, at, small, allowed
    )
    low, rate2, cots, near, out_other = fence(low, rate2, cots, near, out_other)

    part = low.astype(F32) + swap(low, "fsdp", 1).astype(F32)
    part, gate_own, near, out_other = fence(part, gate_own, near, out_other)
    part, got = last_line(part, 2)
    out_near, out_other = near, out_other + [swap(block, "dp", 1) for block in near[len(near) // 2 :]]
    part, got, cots, out_near, out_other = fence(part, got, cots, out_near, out_other)
    projected = part + got.astype(F32)

    gate_other = swap(gate_own, "dp", 1)
    for s in steps[1:]:
        cots[s] = shift(cots[0], "fsdp", s)
    projected = projected.reshape(-1, proj, LANES).transpose(0, 2, 1).reshape(slots, proj)
    rank_low = projected[:, :rank_w].astype(BF)
    bc = jnp.concatenate([projected[:, rank_w:], opens], axis=1)
    scanned, states = scan_forward(at, bc, rank_low, small, activ, valid, rate2, tb)
    scanned, gate_own, gate_other, cots[n_line - 1] = fence(scanned, gate_own, gate_other, cots[n_line - 1])

    branches, gate, out_nat, *gated = gate_block(
        info, n_line, n_dp, gate_own, gate_other, out_near, out_other, normed, scanned, activ, at, small
    )
    branches, gate, gated, out_nat, cots = fence(branches, gate, gated, out_nat, cots)

    branches[1] = shift(branches[1], "fsdp", 1)
    grad_scan, grad_gate, dout, gate_grad = gate_back(
        info, n_line, [cots[s] for s in range(n_line)], out_nat, gate, scanned, activ, at, small, valid, normed
    )
    branches, grad_scan, grad_gate, dout, gated, gate_grad = fence(
        branches, grad_scan, grad_gate, dout, gated, gate_grad
    )

    gate_sums = lax.all_to_all(gate_grad.reshape(n_dp, -1, width), "dp", 0, 0)
    for s in steps[1:]:
        branches[s] = shift(branches[s], "fsdp", s)
    low, grad_u, dt_w_grad, vectors, rate_grad = scan_backward(
        at, bc, rank_low, small, activ, valid, rate2, grad_scan, states, tb
    )
    low, branches, gated, dout, grad_gate = fence(low, branches, gated, dout, grad_gate)

    out_kept, out_sent = outer_product(*gated, dout)
    part = low.astype(F32) + swap(low, "fsdp", 1).astype(F32)
    part, out_kept, out_sent, grad_gate = fence(part, out_kept, out_sent, grad_gate)
    out_got = swap(out_sent, "dp", 1)
    gate_rows = jnp.sum(gate_sums.astype(F32), axis=0).astype(BF)
    out_kept, out_got, gate_rows = fence(out_kept, out_got, gate_rows)
    out_sum = chip_sum(out_kept, out_got)
    part, got = last_line(part, 2)
    part, got, out_sum.held, out_sum.sends, gate_rows = fence(part, got, out_sum.held, out_sum.sends, gate_rows)

    gate_got = to_line(gate_rows.reshape(n_line, in_rows, width))
    grad_normed, inner_kept, inner_sent, small_kept, small_sent = conv_back(
        info, n_line, n_dp, part, got, grad_u, at, small, activ, conv_out, inner, allowed,
        dt_w_grad, rate_grad, vectors, grad_gate, (inner_own, inner_other), (gate_own, gate_other),
        normed_kept, normed_sent,
    )
    grad_normed, gate_got, inner_kept, inner_sent, small_kept, small_sent, branches = out_sum.fenced(
        grad_normed, gate_got, inner_kept, inner_sent, small_kept, small_sent, branches
    )

    grad_normed = to_line(grad_normed.reshape(n_line, held_slots, model))
    folded = owned % LANES == 0
    out_sum.first()
    inner_got, small_got = swap(inner_sent, "dp", 1), swap(small_sent, "dp", 1)
    if folded:
        blocks = add_core(inner_kept, inner_got, small_kept, small_got)
    else:
        blocks = [sent_far(inner_kept, inner_got, u) for u in range(n_dp // 2)]
    blocks, small_kept, small_got, branches = out_sum.fenced(blocks, small_kept, small_got, branches)

    blocks = [swap(block, "dp", 2 * u) if u else block for u, block in enumerate(blocks)]
    out_sum.add()
    if folded:
        inner_sent, small_sum = sum_chips(place, blocks, n_line, in_rows)
    else:
        rows = sum(block.astype(F32) for block in blocks).astype(BF).reshape(n_line, in_rows, width)
        inner_sent = [
            lax.dynamic_index_in_dim(rows, lax.rem(place + s, n_line), 0, keepdims=False) for s in range(n_line)
        ]
        small_sum = add_chips_near(small_kept + small_got.astype(F32))
    inner_sent, small_sum, branches = out_sum.fenced(inner_sent, small_sum, branches)

    inner_got = [shift(block, "fsdp", s) if s else block for s, block in enumerate(inner_sent)]
    out_sum.second()
    grad_normed, small_sum = fence(grad_normed, small_sum)
    grad_normed = jnp.sum(grad_normed.astype(F32), axis=0)
    out_weight_grad = out_sum.total()
    small_grads = small_sum
    if folded:
        small_grads = small_sum.reshape(-1, n_dp, owned).transpose(1, 0, 2).reshape(-1, owned)
    dt_g, x_g, a_g = small_grads[at.dt_w], small_grads[at.x_t], small_grads[at.a_t]
    tail_g = small_grads[at.rest]
    conv_g, conv_b_g, dt_b_g, skip_g = tail_g[:taps], tail_g[taps], tail_g[taps + 1], tail_g[taps + 2]
    small_out = [conv_g, conv_b_g, x_g.T, dt_g, dt_b_g, a_g.T, skip_g]
    own_f = own_tokens.astype(F32)
    output = (own_f + own_valid * sum(p.astype(F32) for p in branches)).astype(BF)
    own_scale = lax.rsqrt(jnp.mean(own_f * own_f, axis=1, keepdims=True) + EPS)
    unit = own_f * own_scale
    grad_unit = grad_normed * full_gain
    token_grad = own_cot.astype(F32) + own_scale * (
        grad_unit - unit * jnp.mean(grad_unit * unit, axis=1, keepdims=True)
    )
    inner_got, token_grad, output, out_weight_grad, small_out = fence(
        inner_got, token_grad, output, out_weight_grad, small_out
    )
    in_weight_grad, gain_grad = join_columns(place, inner_got, gate_got, in_weight, gain, n_dp)
    return output, token_grad, gain_grad, in_weight_grad, *small_out, out_weight_grad


def solution(mesh):
    both = ("dp", "fsdp")
    rows, cols, vec = P(both, None), P(None, both), P(both)
    return jax.shard_map(
        per_device,
        mesh=mesh,
        in_specs=(rows, P(), P(), vec, rows, cols, vec, rows, cols, vec, rows, vec, rows, rows),
        out_specs=(rows, rows, vec, rows, cols, vec, rows, cols, vec, rows, vec, rows),
        check_vma=False,
    )
```

```python
import functools

import jax
import jax.numpy as jnp
from jax import lax
from jax.experimental import pallas as pl
from jax.experimental.pallas import tpu as pltpu
from jax.sharding import PartitionSpec as P

BF, F32 = jnp.bfloat16, jnp.float32
LANES, SUB = 128, 8
LN2 = 0.6931471805599453
FAR = 1.0e5
EPS = 1e-5


def small_cost(flops):
    return pl.CostEstimate(flops=flops, bytes_accessed=1 << 16, transcendentals=0)


class Small:
    def __init__(self, rank, proj, state, taps):
        self.dt_w = slice(0, rank)
        self.x_t = slice(rank, rank + proj)
        self.a_t = slice(rank + proj, rank + proj + state)
        self.rest = slice(rank + proj + state, rank + proj + state + 16)
        self.taps, self.rows = taps, rank + proj + state + 16

    def fold(self, parts):
        rows = -(-self.rows // parts)
        return rows + -rows % 16

    def vector(self, ref, at):
        return ref[self.rest, :].astype(F32)[at : at + 1, :]


def contract_cols(left, right):
    return lax.dot_general(left, right, (((1,), (1,)), ((), ())), preferred_element_type=F32)


def scatter_lanes(ref, value, rows):
    for k in range(value.shape[1] // LANES):
        ref[pl.ds(k, rows, stride=SUB), :] = value[:, k * LANES : (k + 1) * LANES]


def gather_lanes(ref, width, rows):
    return jnp.concatenate(
        [ref[pl.ds(k, rows, stride=SUB), :] for k in range(width // LANES)], axis=1
    )


def softplus(v):
    return jnp.maximum(v, 0.0) + jnp.log1p(jnp.exp(-jnp.abs(v)))


def forward_kernel(at, bc, rank, small, act, valid, rate2, y_out, states, h_ref, dt_s, dtu_s, y_s):
    tb, width = act.shape
    n_state = rate2.shape[0] // SUB

    @pl.when(pl.program_id(0) == 0)
    def _():
        h_ref[...] = jnp.zeros_like(h_ref)
        if width < SUB * LANES:
            dt_s[...] = jnp.zeros_like(dt_s)
            dtu_s[...] = jnp.zeros_like(dtu_s)

    dt_b = at.vector(small, at.taps + 1)
    pre = jnp.dot(rank[...], small[at.dt_w, :], preferred_element_type=F32) + dt_b
    dt = softplus(pre) * valid[...]
    scatter_lanes(dt_s, dt, tb)
    scatter_lanes(dtu_s, dt * act[...].astype(F32), tb)
    rates = [rate2[n * SUB : (n + 1) * SUB, :] for n in range(n_state)]
    first = [h_ref[n * SUB : (n + 1) * SUB, :] for n in range(n_state)]
    for n in range(n_state):
        states[0, n, 0:SUB, :] = first[n]

    def token(t, h):
        at = pl.multiple_of(t * SUB, SUB)
        dt_t = dt_s[pl.ds(at, SUB), :] + bc[t, 2 * n_state]
        dtu_t = dtu_s[pl.ds(at, SUB), :]
        new, parts = [], [None, None]
        for n in range(n_state):
            hn = jnp.exp2(dt_t * rates[n]) * h[n] + dtu_t * bc[t, n]
            states[0, n, pl.ds(at + SUB, SUB), :] = hn
            term = hn * bc[t, n_state + n]
            parts[n % 2] = term if parts[n % 2] is None else parts[n % 2] + term
            new.append(hn)
        y_s[pl.ds(at, SUB), :] = parts[0] + parts[1]
        return tuple(new)

    last = lax.fori_loop(0, tb, token, tuple(first), unroll=8)
    for n in range(n_state):
        h_ref[n * SUB : (n + 1) * SUB, :] = last[n]
    y_out[...] = gather_lanes(y_s, width, tb)


def scan_forward(at, bc, rank, small, act, valid, rate2, tb):
    slots, width = act.shape
    n_state = rate2.shape[0] // SUB
    nb = slots // tb
    whole = lambda i: (0, 0)
    row = lambda i: (i, 0)
    return pl.pallas_call(
        functools.partial(forward_kernel, at),
        grid=(nb,),
        in_specs=[
            pl.BlockSpec((tb, bc.shape[1]), row, memory_space=pltpu.SMEM),
            pl.BlockSpec((tb, rank.shape[1]), row),
            pl.BlockSpec(small.shape, whole),
            pl.BlockSpec((tb, width), row),
            pl.BlockSpec((tb, 1), row),
            pl.BlockSpec(rate2.shape, whole),
        ],
        out_specs=[
            pl.BlockSpec((tb, width), row),
            pl.BlockSpec((1, n_state, (tb + 1) * SUB, LANES), lambda i: (i, 0, 0, 0)),
        ],
        out_shape=[
            jax.ShapeDtypeStruct((slots, width), F32),
            jax.ShapeDtypeStruct((nb, n_state, (tb + 1) * SUB, LANES), F32),
        ],
        scratch_shapes=[pltpu.VMEM(rate2.shape, F32)] + [pltpu.VMEM((tb * SUB, LANES), F32)] * 3,
        compiler_params=pltpu.CompilerParams(vmem_limit_bytes=61 << 20),
        cost_estimate=small_cost(1 << 20),
        name="scan_forward",
    )(bc, rank, small, act, valid, rate2)


def backward_kernel(
    at_small, bc, rank, small, act, valid, rate2, gs, states,
    packed_out, gu_out, dtw_out, vec_out, rate_grad,
    part_s, rate_out, g_ref, dt_s, dtu_s, gs_s, gdt_s, ab_s, both_s, sums,
):
    tb, width = act.shape
    n_state = rate2.shape[0] // SUB
    part = 4

    @pl.when(pl.program_id(0) == 0)
    def _():
        g_ref[...] = jnp.zeros_like(g_ref)
        rate_out[...] = jnp.zeros_like(rate_out)
        vec_out[...] = jnp.zeros_like(vec_out)
        dtw_out[...] = jnp.zeros_like(dtw_out)
        if width < SUB * LANES:
            for ref in (dt_s, dtu_s, gs_s):
                ref[...] = jnp.zeros_like(ref)

    u = act[...].astype(F32)
    ok = valid[...]
    dt_b, skip = at_small.vector(small, at_small.taps + 1), at_small.vector(small, at_small.taps + 2)
    pre = jnp.dot(rank[...], small[at_small.dt_w, :], preferred_element_type=F32) + dt_b
    dt = softplus(pre) * ok
    gs_v = gs[...]
    scatter_lanes(dt_s, dt, tb)
    scatter_lanes(dtu_s, dt * u, tb)
    scatter_lanes(gs_s, gs_v, tb)

    row = lax.broadcasted_iota(jnp.int32, (SUB, 2 * LANES), 0)
    lane = lax.broadcasted_iota(jnp.int32, (SUB, 2 * LANES), 1)
    pick = (lane // LANES == row).astype(F32).astype(BF)
    run = SUB
    span = run * SUB

    def add_lanes(group, i):
        rows = pl.ds(pl.multiple_of(i * span, span), span)
        pairs = jnp.concatenate([both_s[group % 2, j, rows, :] for j in range(part)], axis=0)
        sums[group, pl.ds(pl.multiple_of(i * SUB, SUB), SUB), :] = contract_cols(pick, pairs)

    for group in range(n_state // part):
        index = range(group * part, (group + 1) * part)
        rates = [rate2[n * SUB : (n + 1) * SUB, :] for n in index]

        def token(t, carry, after):
            g, acc = carry
            at = pl.multiple_of(t * SUB, SUB)
            dt_t, dtu_t, gs_t = [ref[pl.ds(at, SUB), :] for ref in (dt_s, dtu_s, gs_s)]
            dtd = dt_t + bc[t, 2 * n_state]
            new_g, new_acc, before, sources, reads = [], [], [], [], []
            gdt = ab = None
            for j, n in enumerate(index):
                lam = gs_t * bc[t, n_state + n] + g[j]
                sources.append(lam * dtu_t)
                reads.append(after[j] * gs_t)
                back = jnp.exp2(dtd * rates[j]) * lam
                before.append(states[0, n, pl.ds(at, SUB), :])
                thr = back * before[j]
                gdt = thr * rates[j] if gdt is None else gdt + thr * rates[j]
                ab = lam * bc[t, n] if ab is None else ab + lam * bc[t, n]
                new_g.append(back)
                new_acc.append(acc[j] + thr * dt_t)
            if group == 0:
                gdt_s[pl.ds(at, SUB), :] = gdt
                ab_s[pl.ds(at, SUB), :] = ab
            else:
                gdt_s[pl.ds(at, SUB), :] += gdt
                ab_s[pl.ds(at, SUB), :] += ab
            return (tuple(new_g), tuple(new_acc)), before, sources, reads

        def some_tokens(i, carry):
            i = tb // run - 1 - i
            if group:
                add_lanes(group - 1, i)
            late = pl.multiple_of((i + 1) * span, SUB)
            after = [states[0, n, pl.ds(late, SUB), :] for n in index]
            for k in range(run - 1, 0, -2):
                t = i * run + k
                carry, after, sources1, reads1 = token(t, carry, after)
                carry, after, sources0, reads0 = token(t - 1, carry, after)
                rows = pl.ds(pl.multiple_of((t - 1) * SUB, 2 * SUB), 2 * SUB)
                for j in range(part):
                    both_s[group % 2, j, rows, 0:LANES] = jnp.concatenate([sources0[j], sources1[j]], axis=0).astype(BF)
                    both_s[group % 2, j, rows, LANES:] = jnp.concatenate([reads0[j], reads1[j]], axis=0).astype(BF)
            return carry

        start = (
            tuple(g_ref[n * SUB : (n + 1) * SUB, :] for n in index),
            tuple(rate_out[n * SUB : (n + 1) * SUB, :] for n in index),
        )
        g, acc = lax.fori_loop(0, tb // run, some_tokens, start, unroll=tb // run)
        for j, n in enumerate(index):
            g_ref[n * SUB : (n + 1) * SUB, :] = g[j]
            rate_out[n * SUB : (n + 1) * SUB, :] = acc[j]
    for i in range(tb // run):
        add_lanes(n_state // part - 1, i)

    ab = gather_lanes(ab_s, width, tb)
    gdt = gather_lanes(gdt_s, width, tb)
    gu_out[...] = (gs_v * skip + dt * ab).astype(BF)
    grad_pre = ok * (gdt * LN2 + u * ab) * jax.nn.sigmoid(pre)
    vec_out[0:1, :] += jnp.sum(grad_pre, axis=0, keepdims=True)
    vec_out[1:2, :] += jnp.sum(gs_v * u, axis=0, keepdims=True)
    low = grad_pre.astype(BF)
    dtw_out[...] += lax.dot_general(rank[...], low, (((0,), (0,)), ((), ())), preferred_element_type=F32)
    rank_w = rank.shape[1]
    rows = pl.ds(pl.multiple_of((pl.num_programs(0) - 1 - pl.program_id(0)) * tb, tb), tb)
    part_s[rows, 0:rank_w] = contract_cols(low, small[at_small.dt_w, :]).astype(BF)

    take_row = lax.broadcasted_iota(jnp.int32, (2 * tb, tb // run * SUB), 0)
    take_lane = lax.broadcasted_iota(jnp.int32, (2 * tb, tb // run * SUB), 1)
    take = (take_lane == take_row % tb // run * SUB + take_row // tb).astype(F32).astype(BF)
    keep_row = lax.broadcasted_iota(jnp.int32, (2 * tb, part * span), 0)
    keep_lane = lax.broadcasted_iota(jnp.int32, (2 * tb, part * span), 1)
    keep = keep_lane // SUB % run == keep_row % run
    from_lane = lax.broadcasted_iota(jnp.int32, (part * span, LANES), 0)
    to_lane = lax.broadcasted_iota(jnp.int32, (part * span, LANES), 1)
    tail = jnp.zeros((2 * tb, LANES), F32)
    for group in range(n_state // part):
        chosen = jnp.dot(take, sums[group].astype(BF), preferred_element_type=F32)
        chosen = jnp.where(keep, chosen, 0.0).astype(BF)
        fold = (to_lane == group * part + from_lane // span).astype(F32).astype(BF)
        tail = tail + jnp.dot(chosen, fold, preferred_element_type=F32)
    part_s[rows, rank_w : rank_w + n_state] = tail[0:tb, 0:n_state].astype(BF)
    part_s[rows, rank_w + n_state :] = tail[tb:, 0:n_state].astype(BF)

    @pl.when(pl.program_id(0) == pl.num_programs(0) - 1)
    def _():
        proj = part_s.shape[1]
        across = lax.broadcasted_iota(jnp.int32, (proj, proj), 0) == lax.broadcasted_iota(jnp.int32, (proj, proj), 1)
        one = across.astype(F32).astype(BF)
        for b in range(part_s.shape[0] // LANES):
            packed_out[b * proj : (b + 1) * proj, :] = contract_cols(
                one, part_s[b * LANES : (b + 1) * LANES, :]
            ).astype(BF)
        for k in range(width // LANES):
            rows = pl.ds(k, n_state, stride=SUB)
            rate_grad[:, k * LANES : (k + 1) * LANES] = rate_out[rows, :] * rate2[rows, :] * LN2


def scan_backward(at, bc, rank, small, act, valid, rate2, gs, states, tb):
    slots, width = act.shape
    n_state = rate2.shape[0] // SUB
    nb = slots // tb
    whole = lambda i: (0, 0)
    row = lambda i: (nb - 1 - i, 0)
    rank_w = rank.shape[1]
    proj = rank_w + 2 * n_state
    return pl.pallas_call(
        functools.partial(backward_kernel, at),
        grid=(nb,),
        in_specs=[
            pl.BlockSpec((tb, bc.shape[1]), row, memory_space=pltpu.SMEM),
            pl.BlockSpec((tb, rank_w), row),
            pl.BlockSpec(small.shape, whole),
            pl.BlockSpec((tb, width), row),
            pl.BlockSpec((tb, 1), row),
            pl.BlockSpec(rate2.shape, whole),
            pl.BlockSpec((tb, width), row),
            pl.BlockSpec((1, n_state, (tb + 1) * SUB, LANES), lambda i: (nb - 1 - i, 0, 0, 0)),
        ],
        out_specs=[
            pl.BlockSpec((proj * slots // LANES, LANES), whole),
            pl.BlockSpec((tb, width), row),
            pl.BlockSpec((rank_w, width), whole),
            pl.BlockSpec((2, width), whole),
            pl.BlockSpec((n_state, width), whole),
        ],
        out_shape=[
            jax.ShapeDtypeStruct((proj * slots // LANES, LANES), BF),
            jax.ShapeDtypeStruct((slots, width), BF),
            jax.ShapeDtypeStruct((rank_w, width), F32),
            jax.ShapeDtypeStruct((2, width), F32),
            jax.ShapeDtypeStruct((n_state, width), F32),
        ],
        scratch_shapes=[pltpu.VMEM((slots, proj), BF)] + [pltpu.VMEM(rate2.shape, F32)] * 2
        + [pltpu.VMEM((tb * SUB, LANES), F32)] * 5
        + [pltpu.VMEM((2, 4, tb * SUB, 2 * LANES), BF), pltpu.VMEM((n_state // 4, tb, 4 * SUB * SUB), F32)],
        compiler_params=pltpu.CompilerParams(vmem_limit_bytes=61 << 20),
        cost_estimate=small_cost(1 << 20),
        name="scan_backward",
    )(bc, rank, small, act, valid, rate2, gs, states)


def silu_grad(value, sig):
    return sig * (1.0 + value * (1.0 - sig))


def place_blocks(ref, own, other, index):
    chips = own.shape[0]
    rows = ref.shape[0] // (2 * chips)
    core = lax.rem(index, 2)
    for q in range(chips):
        ref[pl.ds(pl.multiple_of((2 * q + core) * rows, rows), rows), :] = own[q, 0:rows, :]
        ref[pl.ds(pl.multiple_of((2 * q + 1 - core) * rows, rows), rows), :] = other[q, 0:rows, :]


def block_copies(ref, own, other, index, sems, first):
    chips = own.shape[0]
    rows = ref.shape[0] // (2 * chips)
    core = lax.rem(index, 2)
    found = []
    for q in range(chips):
        for blocks, d in ((own, 2 * q + core), (other, 2 * q + 1 - core)):
            at = pl.ds(pl.multiple_of(d * rows, rows), rows)
            found.append(
                pltpu.make_async_copy(blocks.at[q, pl.ds(0, rows)], ref.at[at], sems.at[first + len(found)])
            )
    return found


def read_row(ref, row, cols):
    tile = SUB if ref.dtype == F32 else 2 * SUB
    base = pl.multiple_of(row // tile * tile, tile)
    rows = ref[pl.ds(base, tile), cols].astype(F32)
    mine = lax.broadcasted_iota(jnp.int32, rows.shape, 0) == row - base
    return jnp.sum(jnp.where(mine, rows, 0.0), axis=0, keepdims=True)


def add_row(ref, row, value):
    base = pl.multiple_of(row // SUB * SUB, SUB)
    rows = ref[pl.ds(base, SUB), :]
    mine = lax.broadcasted_iota(jnp.int32, rows.shape, 0) == row - base
    ref[pl.ds(base, SUB), :] = rows + jnp.where(mine, value, 0.0)


def split_kernel(n_dp, in_w, gain, out):
    rows = in_w.shape[0]
    n_line, full, width = out.shape
    owned = width // n_dp
    top = jnp.broadcast_to(gain[...].astype(F32), (full - 2 * rows, rows)).astype(in_w.dtype)
    for to in range(n_line):
        for half in range(2):
            for d in range(n_dp):
                at = ((half * n_dp + d) * n_line + to) * owned
                out[to, half * rows : (half + 1) * rows, d * owned : (d + 1) * owned] = in_w[:, at : at + owned]
        out[to, 2 * rows :, :] = jnp.zeros((full - 2 * rows, width), in_w.dtype)
        out[to, 2 * rows :, 0:rows] = top


def split_columns(in_w, gain, n_dp, n_line):
    rows, both = in_w.shape
    width = both // (2 * n_line)
    if width // n_dp % LANES:
        blocks = in_w.reshape(rows, 2, n_dp, n_line, width // n_dp).transpose(3, 1, 0, 2, 4)
        top = jnp.broadcast_to(jnp.pad(gain, (0, width - rows)), (n_line, 16, width))
        return jnp.concatenate([blocks.reshape(n_line, 2 * rows, width), top], axis=1)
    vmem = pl.BlockSpec(memory_space=pltpu.VMEM)
    return pl.pallas_call(
        functools.partial(split_kernel, n_dp),
        in_specs=[vmem] * 2,
        out_specs=vmem,
        out_shape=jax.ShapeDtypeStruct((n_line, 2 * rows + 16, width), in_w.dtype),
        cost_estimate=small_cost(1 << 10),
        name="split_columns",
    )(in_w, gain[None])


def join_kernel(n_dp, place, *refs):
    *inner, gate, in_w, gain, out, gain_out = refs
    n_line, rows, width = gate.shape
    owned = width // n_dp
    total = jnp.zeros((rows, LANES), F32)
    for s in range(n_line):
        for half in range(2):
            line = from_place(place[0], s, n_line) if half == 0 else s
            for d in range(n_dp):
                cols = slice(d * owned, (d + 1) * owned)
                block = (inner[s][:, cols] if half == 0 else gate[s, :, cols]).astype(F32)
                at = ((half * n_dp + d) * n_line + line) * owned
                at = pl.ds(pl.multiple_of(at, owned), owned) if half == 0 else slice(at, at + owned)
                out[:, at] = block
                term = block * in_w[:, at].astype(F32)
                for low in range(0, owned, LANES):
                    total = total + term[:, low : low + LANES]
    ones = jnp.ones((SUB, LANES), F32)
    sums = lax.dot_general(
        ones, total, (((1,), (1,)), ((), ())), precision=lax.Precision.HIGHEST, preferred_element_type=F32
    )
    gain_out[...] = sums[0:1, :] / gain[...].astype(F32)


def join_columns(place, inner, gate, in_w, gain, n_dp):
    rows, both = in_w.shape
    n_line, _, width = gate.shape
    if width // n_dp % LANES:
        blocks = jnp.stack([in_order(inner, "fsdp"), gate]).astype(F32).reshape(2, n_line, rows, n_dp, -1)
        full = blocks.transpose(2, 0, 3, 1, 4).reshape(rows, both)
        return full, jnp.sum(full * in_w.astype(F32), axis=1) / gain.astype(F32)
    vmem = pl.BlockSpec(memory_space=pltpu.VMEM)
    full, gain_grad = pl.pallas_call(
        functools.partial(join_kernel, n_dp),
        in_specs=[pl.BlockSpec(memory_space=pltpu.SMEM)] + [vmem] * (n_line + 3),
        out_specs=[vmem] * 2,
        out_shape=[jax.ShapeDtypeStruct((rows, both), F32), jax.ShapeDtypeStruct((1, rows), F32)],
        cost_estimate=small_cost(1 << 10),
        name="join_columns",
    )(place[None], *inner, gate, in_w, gain[None])
    return full, gain_grad[0]


def column_block(width, slots):
    return 256 if width % 256 == 0 and slots <= 1024 else LANES


def from_place(place, steps, n_line):
    return lax.rem(place - steps + n_line, n_line)


def outer(lefts, right, outs):
    rows = min(256, lefts[0].shape[1])

    @pl.loop(0, lefts[0].shape[1] // rows)
    def _(r):
        at = pl.ds(pl.multiple_of(r * rows, rows), rows)
        for left, out in zip(lefts, outs):
            found = lax.dot_general(left[:, at], right[...], (((0,), (0,)), ((), ())), preferred_element_type=F32)
            out[at, :] = found.astype(out.dtype)


def outer_kernel(kept, sent, right, kept_out, sent_out):
    outer((kept, sent), right, (kept_out, sent_out))


def outer_product(kept, sent, right):
    shape = (kept.shape[1], right.shape[1])
    vmem = pl.BlockSpec(memory_space=pltpu.VMEM)
    return pl.pallas_call(
        outer_kernel,
        in_specs=[vmem] * 3,
        out_specs=[vmem] * 2,
        out_shape=[jax.ShapeDtypeStruct(shape, BF)] * 2,
        compiler_params=pltpu.CompilerParams(vmem_limit_bytes=61 << 20),
        cost_estimate=small_cost(1 << 20),
        name="outer_product",
    )(kept, sent, right)


def to_shifts(source, outs, place):
    rows = outs[0].shape[0]
    for s, out in enumerate(outs):
        at = pl.multiple_of(lax.rem(place + s, len(outs)) * rows, rows)
        out[...] = source[pl.ds(at, rows), :]


def split_cores(ref, kept, sent, index, n_dp):
    size = ref.shape[1] // n_dp
    core = lax.rem(index, 2)
    for q in range(kept.shape[1] // size):
        cols = slice(q * size, (q + 1) * size)
        kept[:, cols] = ref[:, pl.ds(pl.multiple_of((2 * q + core) * size, size), size)]
        sent[:, cols] = ref[:, pl.ds(pl.multiple_of((2 * q + 1 - core) * size, size), size)]


def project_kernel(n_line, n_dp, at, info, *refs):
    toks, refs = refs[:n_line], refs[n_line:]
    own, other, small, allowed, gain, normed, kept, sent, inner, conv_out, activ, part, w_nat, inner_s, ext = refs
    held, model = toks[0].shape
    slots = held * n_line
    width = w_nat.shape[1]
    taps = at.taps
    rim = taps - 1
    rows_dp = model // n_dp
    core = lax.rem(info[0], 2)
    for q in range(n_dp // 2):
        for blocks, d in ((own, 2 * q + core), (other, 2 * q + 1 - core)):
            found = blocks[q, rows_dp:, 0:rows_dp].astype(F32)[0:1, :]
            gain[:, pl.ds(pl.multiple_of(d * rows_dp, rows_dp), rows_dp)] = found
    step = 32
    for s, tok in enumerate(toks):
        base = from_place(info[1], s, n_line) * held

        @pl.loop(0, held // step)
        def _(i):
            x = tok[pl.ds(pl.multiple_of(i * step, step), step), :].astype(F32)
            scale = lax.rsqrt(jnp.mean(x * x, axis=1, keepdims=True) + EPS)
            normed[pl.ds(pl.multiple_of(base + i * step, step), step), :] = (x * scale * gain[...]).astype(BF)

    split_cores(normed, kept, sent, info[0], n_dp)
    place_blocks(w_nat, own, other, info[0])
    cb = column_block(width, slots)

    @pl.loop(0, width // cb)
    def _(c):
        cols = pl.ds(pl.multiple_of(c * cb, cb), cb)
        inner_s[...] = jnp.dot(normed[...], w_nat[:, cols], preferred_element_type=F32)
        inner[:, cols] = inner_s[...].astype(BF)
        vectors = small[at.rest, cols].astype(F32)
        for f in range(n_line):
            rows = slice(f * held, (f + 1) * held)
            ext[SUB : SUB + held, :] = inner_s[rows, :]
            for k in range(1, rim + 1):
                if f == 0:
                    ext[SUB - k : SUB - k + 1, :] = jnp.zeros((1, cb), F32)
                else:
                    ext[SUB - k : SUB - k + 1, :] = read_row(inner_s, (f - 1) * held + info[1 + f] - k, slice(None))
            total = vectors[taps : taps + 1, :]
            for lag in range(taps):
                tapped = ext[SUB - lag : SUB - lag + held, :]
                total = total + vectors[rim - lag : rim - lag + 1, :] * tapped * allowed[rows, lag : lag + 1]
            conv_out[rows, cols] = total.astype(BF)
            activ[rows, cols] = (total * jax.nn.sigmoid(total)).astype(BF)

    proj = part.shape[0] * LANES // slots
    for b in range(slots // LANES):
        found = contract_cols(small[at.x_t, :], activ[b * LANES : (b + 1) * LANES, :])
        part[b * proj : (b + 1) * proj, :] = found.astype(BF)


def project(info, n_line, n_dp, toks, own, other, at, small, allowed):
    held, model = toks[0].shape
    slots = held * n_line
    width, proj = small.shape[1], at.x_t.stop - at.x_t.start
    vmem = pl.BlockSpec(memory_space=pltpu.VMEM)
    shapes = [
        ((1, model), F32), ((slots, model), BF), ((slots, model // 2), BF), ((slots, model // 2), BF),
        ((slots, width), BF), ((slots, width), BF), ((slots, width), BF), ((proj * slots // LANES, LANES), BF),
    ]
    return pl.pallas_call(
        functools.partial(project_kernel, n_line, n_dp, at),
        in_specs=[pl.BlockSpec(memory_space=pltpu.SMEM)] + [vmem] * (4 + len(toks)),
        out_specs=[vmem] * len(shapes),
        out_shape=[jax.ShapeDtypeStruct(s, t) for s, t in shapes],
        scratch_shapes=[
            pltpu.VMEM((model, width), BF),
            pltpu.VMEM((slots, column_block(width, slots)), F32),
            pltpu.VMEM((SUB + slots // n_line, column_block(width, slots)), F32),
        ],
        compiler_params=pltpu.CompilerParams(vmem_limit_bytes=61 << 20),
        cost_estimate=small_cost(1 << 20),
        name="project",
    )(info, *toks, own, other, small, allowed)


def gate_kernel(n_line, n_dp, at, info, own, other, normed, y, act, small, *refs):
    out_own, out_other, refs = refs[: n_dp // 2], refs[n_dp // 2 : n_dp], refs[n_dp:]
    branches, refs = refs[:n_line], refs[n_line:]
    gate, gated, o_nat, *halves, branch, w_nat = refs
    slots, width = y.shape
    model = normed.shape[1]
    place_blocks(w_nat, own, other, info[0])
    rows = width // n_dp
    core, chip = lax.rem(info[0], 2), lax.div(info[0], 2)
    for u in range(n_dp // 2):
        first = 2 * jnp.bitwise_xor(chip, u)
        o_nat[pl.ds(pl.multiple_of((first + core) * rows, rows), rows), :] = out_own[u][0:rows, :]
        o_nat[pl.ds(pl.multiple_of((first + 1 - core) * rows, rows), rows), :] = out_other[u][0:rows, :]
    cb = column_block(width, slots)

    @pl.loop(0, width // cb)
    def _(c):
        cols = pl.ds(pl.multiple_of(c * cb, cb), cb)
        value = jnp.dot(normed[...], w_nat[:, cols], preferred_element_type=F32)
        gate[:, cols] = value
        skip = small[at.rest, cols].astype(F32)[at.taps + 2 : at.taps + 3, :]
        scan_out = y[:, cols] + skip * act[:, cols].astype(F32)
        gated[:, cols] = (scan_out * value * jax.nn.sigmoid(value)).astype(BF)

    mb = column_block(model, slots)

    @pl.loop(0, model // mb)
    def _(c):
        cols = pl.ds(pl.multiple_of(c * mb, mb), mb)
        branch[:, cols] = jnp.dot(gated[...], o_nat[:, cols], preferred_element_type=F32).astype(BF)

    to_shifts(branch, branches, info[1])
    if halves:
        split_cores(gated, *halves, info[0], n_dp)


def gate_block(info, n_line, n_dp, own, other, out_own, out_other, normed, y, act, at, small):
    slots, width = y.shape
    model = normed.shape[1]
    vmem = pl.BlockSpec(memory_space=pltpu.VMEM)
    shapes = [((slots // n_line, model), BF)] * n_line
    shapes += [((slots, width), F32), ((slots, width), BF), ((width, model), BF)]
    if width // n_dp % LANES == 0:
        shapes += [((slots, width // 2), BF)] * 2
    outs = pl.pallas_call(
        functools.partial(gate_kernel, n_line, n_dp, at),
        in_specs=[pl.BlockSpec(memory_space=pltpu.SMEM)] + [vmem] * (6 + n_dp),
        out_specs=[vmem] * len(shapes),
        out_shape=[jax.ShapeDtypeStruct(s, t) for s, t in shapes],
        scratch_shapes=[pltpu.VMEM((slots, model), BF), pltpu.VMEM((model, width), BF)],
        compiler_params=pltpu.CompilerParams(vmem_limit_bytes=61 << 20),
        cost_estimate=small_cost(1 << 20),
        name="gate_block",
    )(info, own, other, normed, y, act, small, *out_own, *out_other)
    branches, (gate, gated, o_nat), halves = list(outs[:n_line]), outs[n_line : n_line + 3], outs[n_line + 3 :]
    return branches, gate, o_nat, *(halves or cores(gated, 1))


def gate_back_kernel(n_line, at, info, *refs):
    cots, refs = refs[:n_line], refs[n_line:]
    o_nat, gate, y, act, small, valid, normed, gs, grad_gate, dout, product = refs
    slots, width = y.shape
    held, model = cots[0].shape
    for s, cot in enumerate(cots):
        rows = pl.ds(pl.multiple_of(from_place(info[1], s, n_line) * held, held), held)
        dout[rows, :] = (cot[...].astype(F32) * valid[rows, :]).astype(BF)

    cb = column_block(width, slots)

    @pl.loop(0, width // cb)
    def _(c):
        cols = pl.ds(pl.multiple_of(c * cb, cb), cb)
        grad = lax.dot_general(dout[...], o_nat[cols, :], (((1,), (1,)), ((), ())), preferred_element_type=F32)
        value = gate[:, cols]
        sig = jax.nn.sigmoid(value)
        skip = small[at.rest, cols].astype(F32)[at.taps + 2 : at.taps + 3, :]
        scan_out = y[:, cols] + skip * act[:, cols].astype(F32)
        gs[:, cols] = grad * value * sig
        grad_gate[:, cols] = (grad * scan_out * silu_grad(value, sig)).astype(BF)

    outer((normed,), grad_gate, (product,))


def gate_back(info, n_line, cots, o_nat, gate, y, act, at, small, valid, normed):
    slots, width = y.shape
    model = o_nat.shape[1]
    vmem = pl.BlockSpec(memory_space=pltpu.VMEM)
    shapes = [((slots, width), F32), ((slots, width), BF), ((slots, model), BF)]
    shapes += [((model, width), BF)]
    return pl.pallas_call(
        functools.partial(gate_back_kernel, n_line, at),
        in_specs=[pl.BlockSpec(memory_space=pltpu.SMEM)] + [vmem] * (7 + len(cots)),
        out_specs=[vmem] * len(shapes),
        out_shape=[jax.ShapeDtypeStruct(s, t) for s, t in shapes],
        compiler_params=pltpu.CompilerParams(vmem_limit_bytes=61 << 20),
        cost_estimate=small_cost(1 << 20),
        name="gate_back",
    )(info, *cots, o_nat, gate, y, act, small, valid, normed)


def together(slots):
    return slots <= 1024


def conv_back_kernel(n_line, n_dp, at, info, gp_part, gp_got, gu, small, act, conv_out, inner, allowed, dtw, rate_grad, scan_vec,
                     grad_gate, *refs):
    slots, width = gu.shape
    inner_own, inner_other, gate_own, gate_other, *refs = refs
    halves_far, refs = (refs[:2], refs[2:]) if together(slots) else ((), refs)
    normed_far, *refs = refs
    products_far, refs = (refs[:2], refs[2:]) if together(slots) else ((), refs)
    gi_low, refs = (None, refs) if together(slots) else (refs[0], refs[1:])
    kept, sent, x_grad, vec, ext, gi, tail, grad_normed, column, gp, arrived, left, w_nat, gate_nat, *refs = refs
    halves = ()
    copies = block_copies(w_nat, inner_own, inner_other, info[0], arrived, 0)
    copies += block_copies(gate_nat, gate_own, gate_other, info[0], arrived, n_dp)
    if together(slots):
        gi_low, *refs = refs
        halves, products = refs[:2], refs[2:]
        for i, (src, dst) in enumerate(zip(halves_far, halves)):
            copies.append(pltpu.make_async_copy(src, dst, arrived.at[2 * n_dp + i]))
    for copy in copies:
        copy.start()
    leaving = []

    def leave(src, dst):
        copy = pltpu.make_async_copy(src, dst, left.at[len(leaving)])
        copy.start()
        leaving.append(copy)

    gp[...] = (gp_part[...] + gp_got[...].astype(F32)).astype(BF)
    held = slots // n_line
    taps = at.taps
    rim = taps - 1
    cb = column_block(width, slots)
    proj = x_grad.shape[0]
    x_grad[...] = sum(
        jnp.dot(gp[b * proj : (b + 1) * proj, :], act[b * LANES : (b + 1) * LANES, :], preferred_element_type=F32)
        for b in range(slots // LANES)
    )
    vec[...] = jnp.zeros_like(vec)
    for lag in range(taps):
        tail[lag, held : held + SUB, :] = jnp.zeros((SUB, cb), F32)

    @pl.loop(0, width // cb)
    def _(c):
        cols = pl.ds(pl.multiple_of(c * cb, cb), cb)
        vectors = small[at.rest, cols].astype(F32)
        for f in range(n_line - 1, -1, -1):
            rows = slice(f * held, (f + 1) * held)
            ext[SUB : SUB + held, :] = inner[rows, cols].astype(F32)
            for k in range(1, rim + 1):
                if f == 0:
                    ext[SUB - k : SUB - k + 1, :] = jnp.zeros((1, cb), F32)
                else:
                    ext[SUB - k : SUB - k + 1, :] = read_row(inner, (f - 1) * held + info[1 + f] - k, cols)
            back = [
                lax.dot_general(
                    gp[b * proj : (b + 1) * proj, :], small[at.x_t, cols], (((0,), (0,)), ((), ())),
                    preferred_element_type=F32,
                )
                for b in range(f * held // LANES, (f + 1) * held // LANES)
            ]
            grad = gu[rows, cols].astype(F32) + jnp.concatenate(back, axis=0)
            co = conv_out[rows, cols].astype(F32)
            grad = grad * silu_grad(co, jax.nn.sigmoid(co))
            vec[taps : taps + 1, cols] += jnp.sum(grad, axis=0, keepdims=True)
            for lag in range(taps):
                weighted = grad * allowed[rows, lag : lag + 1]
                vec[rim - lag : rim - lag + 1, cols] += jnp.sum(
                    weighted * ext[SUB - lag : SUB - lag + held, :], axis=0, keepdims=True
                )
                tail[lag, 0:held, :] = weighted * vectors[rim - lag : rim - lag + 1, :]
            total = tail[0, 0:held, :]
            for lag in range(1, taps):
                total = total + tail[lag, lag : lag + held, :]
            gi[rows, :] = total
            if f + 1 < n_line:
                for k in range(1, rim + 1):
                    add_row(gi, f * held + info[2 + f] - k, gi[slots + k : slots + k + 1, :])
            for k in range(1, rim + 1):
                row = tail[k, 0:1, :]
                for lag in range(k + 1, taps):
                    row = row + tail[lag, lag - k : lag - k + 1, :]
                gi[slots + k : slots + k + 1, :] = row
        gi_low[:, cols] = gi[0:slots, :].astype(BF)

    for copy in copies:
        copy.wait()
    model = w_nat.shape[0]
    mb = column_block(model, slots)

    @pl.loop(0, model // mb)
    def _(c):
        cols = pl.ds(pl.multiple_of(c * mb, mb), mb)
        found = contract_cols(gi_low[...], w_nat[cols, :]) + contract_cols(grad_gate[...], gate_nat[cols, :])
        grad_normed[:, cols] = found.astype(BF)

    leave(grad_normed, normed_far)
    if halves:
        step = model // 2 // 4
        for r in range(4):
            rows = slice(r * step, (r + 1) * step)
            for half, product, out in zip(halves, products, products_far):
                product[rows, :] = lax.dot_general(
                    half[:, rows], gi_low[...], (((0,), (0,)), ((), ())), preferred_element_type=F32
                ).astype(BF)
                leave(product.at[pl.ds(r * step, step)], out.at[pl.ds(r * step, step)])
    vec[taps + 1 : taps + 3, :] = scan_vec[...]
    owned = width // n_dp
    if kept.shape[0] == 1:
        kept[0, at.dt_w, :], kept[0, at.x_t, :], kept[0, at.a_t, :], kept[0, at.rest, :] = (
            dtw[...], x_grad[...], rate_grad[...], vec[...]
        )
        for copy in leaving:
            copy.wait()
        return
    core = lax.rem(info[0], 2)
    fold = kept.shape[1]
    for q in range(n_dp // 2):
        for ref, d in ((kept, 2 * q + core), (sent, 2 * q + 1 - core)):
            cols = pl.ds(pl.multiple_of(d * owned, owned), owned)
            for rows, source in ((at.dt_w, dtw), (at.x_t, x_grad), (at.a_t, rate_grad), (at.rest, vec)):
                column[rows, :] = source[:, cols]
            for b in range(width // owned):
                ref[q, :, b * owned : (b + 1) * owned] = column[b * fold : (b + 1) * fold, :].astype(ref.dtype)
    for copy in leaving:
        copy.wait()


def conv_back(info, n_line, n_dp, gp_part, gp_got, gu, at, small, act, conv_out, inner, allowed, dtw, rate_grad, scan_vec, grad_gate,
              inner_blocks, gate_blocks, normed_k, normed_s):
    slots, width = gu.shape
    held, model = slots // n_line, 2 * normed_k.shape[1]
    cb = column_block(width, slots)
    owned = width // n_dp
    tiles, one = owned % LANES == 0, together(slots)
    vmem, away = pl.BlockSpec(memory_space=pltpu.VMEM), pl.BlockSpec(memory_space=pl.ANY)
    fold = at.fold(n_dp)
    shape = (n_dp // 2, fold, width) if tiles else (1, at.rows, width)
    later = [*inner_blocks, *gate_blocks] + ([normed_k, normed_s] if one else [])
    low, half = jax.ShapeDtypeStruct((slots, width), BF), jax.ShapeDtypeStruct((model // 2, width), BF)
    outs = pl.pallas_call(
        functools.partial(conv_back_kernel, n_line, n_dp, at),
        in_specs=[pl.BlockSpec(memory_space=pltpu.SMEM)] + [vmem] * 12 + [away] * len(later),
        out_specs=[away] + ([away] * 2 if one else [vmem]) + [vmem] * 2,
        out_shape=[jax.ShapeDtypeStruct((slots, model), BF)]
        + ([half] * 2 if one else [low])
        + [
            jax.ShapeDtypeStruct(shape, F32),
            jax.ShapeDtypeStruct(shape if tiles else (SUB, LANES), BF if tiles else F32),
        ],
        scratch_shapes=[
            pltpu.VMEM((at.x_t.stop - at.x_t.start, width), F32),
            pltpu.VMEM((16, width), F32),
            pltpu.VMEM((SUB + held, cb), F32),
            pltpu.VMEM((slots + SUB, cb), F32),
            pltpu.VMEM((at.taps, held + SUB, cb), F32),
            pltpu.VMEM((slots, model), BF),
            pltpu.VMEM((n_dp * fold, owned), F32),
            pltpu.VMEM(gp_got.shape, BF),
            pltpu.SemaphoreType.DMA((2 * n_dp + 2,)),
            pltpu.SemaphoreType.DMA((9,)),
        ]
        + [pltpu.VMEM((model, width), BF)] * 2
        + ([pltpu.VMEM((slots, width), BF)] + [pltpu.VMEM((slots, model // 2), BF)] * 2 if one else [])
        + ([pltpu.VMEM((model // 2, width), BF)] * 2 if one else []),
        compiler_params=pltpu.CompilerParams(vmem_limit_bytes=61 << 20),
        cost_estimate=small_cost(1 << 20),
        name="conv_back",
    )(info, gp_part, gp_got, gu, small, act, conv_out, inner, allowed, dtw, rate_grad, scan_vec, grad_gate, *later)
    grad_normed, *products, kept, sent = outs
    if not one:
        products = outer_product(normed_k, normed_s, products[0])
    if not tiles:
        kept, sent = [
            part.reshape(at.rows, n_dp // 2, owned).transpose(1, 0, 2) for part in cores(kept[0], 1)
        ]
    return grad_normed, *products, kept, sent.astype(BF)


def swap(value, axis, mask):
    count = lax.axis_size(axis)
    return lax.ppermute(value, axis, [(i, i ^ mask) for i in range(count)])


def shift(value, axis, steps):
    count = lax.axis_size(axis)
    return lax.ppermute(value, axis, [(i, (i + steps) % count) for i in range(count)])


def chips_of(axis):
    return [list(range(core, lax.axis_size(axis), 2)) for core in range(2)]


def to_line(blocks):
    return lax.all_to_all(blocks, "fsdp", 0, 0)


def to_chips(blocks):
    return lax.all_to_all(blocks, "dp", 0, 0, axis_index_groups=chips_of("dp"))


def repeated(value, count):
    return jnp.broadcast_to(value[None], (count,) + value.shape)


def in_order(parts, axis):
    count, me = lax.axis_size(axis), lax.axis_index(axis)
    up = jnp.stack([parts[-k % count] for k in range(count)] * 2)
    return lax.dynamic_slice_in_dim(up, lax.rem(count - me, count), count, 0)


def by_chip(parts):
    chip, count = lax.div(lax.axis_index("dp"), 2), len(parts)
    bits = count.bit_length() - 1
    cube = jnp.stack(parts).reshape((2,) * bits + parts[0].shape)
    for place in range(bits):
        mine = lax.rem(chip >> (bits - 1 - place), 2) == 1
        cube = jnp.where(mine, jnp.flip(cube, place), cube)
    return cube.reshape((count,) + parts[0].shape)


def by_device(own, other):
    core = lax.rem(lax.axis_index("dp"), 2) == 1
    both = jnp.where(core, jnp.stack([other, own], axis=1), jnp.stack([own, other], axis=1))
    return lax.optimization_barrier(both.reshape((-1,) + own.shape[1:]))


def last_line(value, reach):
    while True:
        got = swap(value.astype(BF), "fsdp", reach)
        reach *= 2
        if reach >= lax.axis_size("fsdp"):
            return value, got
        value = value + got.astype(F32)


def fence(*values):
    flat, shape = jax.tree.flatten(values)
    return jax.tree.unflatten(shape, lax.optimization_barrier(tuple(flat)))


def cores(value, axis):
    cut = value.shape[:axis] + (lax.axis_size("dp") // 2, 2, -1) + value.shape[axis + 1 :]
    cube = value.reshape(cut)
    core = lax.rem(lax.axis_index("dp"), 2)
    found = [lax.dynamic_index_in_dim(cube, at, axis + 1, keepdims=False) for at in (core, 1 - core)]
    flat = value.shape[:axis] + (value.shape[axis] // 2,) + value.shape[axis + 1 :]
    return [part.reshape(flat) for part in found]


def add_core_kernel(chip, kept, got, small_kept, small_got, *outs):
    rows = kept.shape[0] // len(outs)
    for u, out in enumerate(outs):
        q = jnp.bitwise_xor(chip[0], u)
        at = pl.ds(pl.multiple_of(q * rows, rows), rows)
        out[0:rows, :] = (kept[at, :].astype(F32) + got[at, :].astype(F32)).astype(BF)
        out[rows:, :] = (small_kept[q] + small_got[q].astype(F32)).astype(BF)


def add_core(kept, got, small_kept, small_got):
    chips, width = lax.axis_size("dp") // 2, kept.shape[1]
    rows = kept.shape[0] // chips + small_kept.shape[1]
    vmem = pl.BlockSpec(memory_space=pltpu.VMEM)
    return pl.pallas_call(
        add_core_kernel,
        in_specs=[pl.BlockSpec(memory_space=pltpu.SMEM)] + [vmem] * 4,
        out_specs=[vmem] * chips,
        out_shape=[jax.ShapeDtypeStruct((rows, width), BF)] * chips,
        compiler_params=pltpu.CompilerParams(vmem_limit_bytes=61 << 20),
        cost_estimate=small_cost(1 << 10),
        name="add_core",
    )(lax.div(lax.axis_index("dp"), 2)[None], kept, got, small_kept, small_got)


def add_chips_near(blocks):
    count, chip = lax.axis_size("dp") // 2, lax.div(lax.axis_index("dp"), 2)
    total = lax.dynamic_index_in_dim(blocks, chip, 0, keepdims=False)
    for u in range(1, count):
        total = total + far(blocks, u).astype(F32)
    return total


def sum_chips_kernel(count, n_line, at, place, *refs):
    blocks, outs, (dt_g, x_g, a_g, conv_g, *vectors, column) = (
        refs[:count], refs[count : count + n_line], refs[count + n_line :]
    )
    rows = outs[0].shape[0]
    for s, out in enumerate(outs):
        mine = pl.ds(pl.multiple_of(lax.rem(place[0] + s, n_line) * rows, rows), rows)
        out[...] = sum(block[mine, :].astype(F32) for block in blocks).astype(BF)
    first, owned = rows * n_line, column.shape[1]
    small = sum(block[first:, :].astype(F32) for block in blocks)
    fold = small.shape[0]
    for b in range(small.shape[1] // owned):
        column[b * fold : (b + 1) * fold, :] = small[:, b * owned : (b + 1) * owned]
    dt_g[...], x_g[...], a_g[...] = column[at.dt_w, :], column[at.x_t, :], column[at.a_t, :]
    rest = column[at.rest, :]
    conv_g[...] = rest[: at.taps, :]
    for i, out in enumerate(vectors):
        out[...] = rest[at.taps + i : at.taps + i + 1, :]


def sum_chips(place, blocks, n_line, rows, at, owned):
    full, width = blocks[0].shape
    vmem = pl.BlockSpec(memory_space=pltpu.VMEM)
    small = [(part.stop - part.start, owned) for part in (at.dt_w, at.x_t, at.a_t)]
    small += [(at.taps, owned)] + [(1, owned)] * 3
    outs = pl.pallas_call(
        functools.partial(sum_chips_kernel, len(blocks), n_line, at),
        in_specs=[pl.BlockSpec(memory_space=pltpu.SMEM)] + [vmem] * len(blocks),
        out_specs=[vmem] * (n_line + len(small)),
        out_shape=[jax.ShapeDtypeStruct((rows, width), BF)] * n_line
        + [jax.ShapeDtypeStruct(shape, F32) for shape in small],
        scratch_shapes=[pltpu.VMEM(((full - n_line * rows) * (width // owned), owned), F32)],
        compiler_params=pltpu.CompilerParams(vmem_limit_bytes=61 << 20),
        cost_estimate=small_cost(1 << 10),
        name="sum_chips",
    )(place[None], *blocks)
    return list(outs[:n_line]), list(outs[n_line:])


def sent_far(kept, got, u):
    rows = kept.shape[0] // (lax.axis_size("dp") // 2)
    at = jnp.bitwise_xor(lax.div(lax.axis_index("dp"), 2), u) * rows
    return sum(lax.dynamic_slice_in_dim(part, at, rows, 0).astype(F32) for part in (kept, got)).astype(BF)


def far(blocks, u):
    block = lax.dynamic_index_in_dim(blocks, jnp.bitwise_xor(lax.div(lax.axis_index("dp"), 2), u), 0, keepdims=False)
    return swap(block.astype(BF), "dp", 2 * u)


def halves_kernel(chip, kept, got, first, second, *held):
    rows, half = held[0].shape
    outs = {
        (0, 0): held[0], (2, 0): held[1], (0, 1): held[2], (1, 1): held[3],
        (1, 0): first.at[0:rows], (3, 0): first.at[rows : 2 * rows],
        (2, 1): second.at[0:rows], (3, 1): second.at[rows : 2 * rows],
    }
    for (u, side), out in outs.items():
        at = pl.ds(pl.multiple_of(jnp.bitwise_xor(chip[0], u) * rows, rows), rows)
        cols = slice(side * half, (side + 1) * half)
        out[...] = (kept[at, cols].astype(F32) + got[at, cols].astype(F32)).astype(BF)


def chip_sum(kept, got):
    chips, (rows, width) = lax.axis_size("dp") // 2, kept.shape
    if chips != 4 or rows // chips % LANES:
        return ChipSum([sent_far(kept, got, u) for u in range(chips)])
    rows, half = rows // chips, width // 2
    vmem = pl.BlockSpec(memory_space=pltpu.VMEM)
    first, second, *held = pl.pallas_call(
        halves_kernel,
        in_specs=[pl.BlockSpec(memory_space=pltpu.SMEM)] + [vmem] * 2,
        out_specs=[vmem] * 6,
        out_shape=[jax.ShapeDtypeStruct((2 * rows, half), BF)] * 2 + [jax.ShapeDtypeStruct((rows, half), BF)] * 4,
        compiler_params=pltpu.CompilerParams(vmem_limit_bytes=61 << 20),
        cost_estimate=small_cost(1 << 10),
        name="chip_halves",
    )(lax.div(lax.axis_index("dp"), 2)[None], kept, got)
    return ChipSum(held, [first, second])


def total_kernel(left, right, left_got, right_got, out):
    half = left.shape[1]
    out[:, 0:half] = left[...] + left_got[...].astype(F32)
    out[:, half:] = right[...] + right_got[...].astype(F32)


class ChipSum:
    def __init__(self, held, sends=None):
        self.direct = sends is None
        self.held, self.sends, self.got = held, sends or held[1:], []

    def fenced(self, *others):
        (self.held, self.sends, self.got), *others = fence((self.held, self.sends, self.got), *others)
        return others

    def first(self):
        self.got = [swap(send, "dp", 2 * u) for u, send in enumerate(self.sends, 1)]
        self.sends = []

    def add(self):
        if self.direct:
            return
        rows = self.held[0].shape[0]
        own = [h.astype(F32) + got[:rows].astype(F32) for h, got in zip(self.held[::2], self.got)]
        self.sends = [(h.astype(F32) + got[rows:].astype(F32)).astype(BF) for h, got in zip(self.held[1::2], self.got)]
        self.held, self.got = own, []

    def second(self):
        if not self.direct:
            self.got = [swap(send, "dp", 2 * u) for u, send in zip((2, 1), self.sends)]

    def total(self):
        if self.direct:
            return sum(part.astype(F32) for part in (self.held[0], *self.got))
        rows, half = self.held[0].shape
        vmem = pl.BlockSpec(memory_space=pltpu.VMEM)
        return pl.pallas_call(
            total_kernel,
            in_specs=[vmem] * 4,
            out_specs=vmem,
            out_shape=jax.ShapeDtypeStruct((rows, 2 * half), F32),
            compiler_params=pltpu.CompilerParams(vmem_limit_bytes=61 << 20),
            cost_estimate=small_cost(1 << 10),
            name="chip_total",
        )(*self.held, *self.got)


def per_device(
    tokens, counts, lengths, gain, in_weight, conv_weight, conv_bias, x_weight,
    dt_weight, dt_bias, a_log, skip, out_weight, cotangent,
):
    n_dp, n_line = lax.axis_size("dp"), lax.axis_size("fsdp")
    group, place = lax.axis_index("dp"), lax.axis_index("fsdp")
    held_slots, model = tokens.shape
    slots = held_slots * n_line
    owned = skip.shape[0]
    width = owned * n_dp
    in_rows = in_weight.shape[0]
    taps, rank_w, n_state = conv_weight.shape[0], dt_weight.shape[0], a_log.shape[1]
    proj = x_weight.shape[1]
    tb = 64 if slots % 64 == 0 else slots

    count_row = lax.dynamic_index_in_dim(counts, group, 0, keepdims=False)
    length_row = lax.dynamic_index_in_dim(lengths, group, 0, keepdims=False)
    info = jnp.concatenate([jnp.stack([group, place]).astype(jnp.int32), count_row])
    offsets = jnp.cumsum(count_row) - count_row
    within = lax.broadcasted_iota(jnp.int32, (n_line, held_slots), 1)
    present = within < count_row[:, None]
    position = offsets[:, None] + within
    second, third = length_row[0], length_row[0] + length_row[1]
    begin = jnp.where(position >= third, third, jnp.where(position >= second, second, 0))
    marks = jnp.stack(
        [position - lag >= begin for lag in range(taps)] + [present, present & (position == begin)]
    ).astype(F32).reshape(taps + 2, slots).T
    allowed, valid, opens = marks[:, :taps], marks[:, taps : taps + 1], marks[:, taps + 1 :] * FAR

    own_tokens, own_cot = tokens, cotangent
    steps = range(1, n_line)
    chips = range(1, n_dp // 2)
    at = Small(rank_w, proj, n_state, taps)

    parts = split_columns(in_weight, gain, n_dp, n_line)
    rest = jnp.concatenate([conv_weight, conv_bias[None], dt_bias[None], skip[None]], axis=0)
    rest = jnp.pad(rest, ((0, 16 - rest.shape[0]), (0, 0)))
    small = jnp.concatenate([dt_weight, x_weight.T, a_log.T, rest], axis=0)
    small_rows = -(-at.rows * owned // model)
    small_rows += -small_rows % 16
    small = jnp.pad(small, ((0, small_rows * model // owned - at.rows), (0, 0))).reshape(small_rows, model)
    packed = jnp.concatenate([out_weight, small], axis=0)
    parts, tokens = fence(parts, tokens)
    parts = to_line(parts)
    toks = {0: tokens, 1: shift(tokens, "fsdp", 1)}
    near = [packed] + [swap(packed, "dp", 2 * u) for u in chips]
    own_valid = lax.dynamic_slice_in_dim(valid, place * held_slots, held_slots, 0)
    parts, toks, near, info, allowed, valid, opens, own_valid = fence(
        parts, toks, near, info, allowed, valid, opens, own_valid
    )

    gain_rows = jnp.pad(parts[:, 2 * in_rows, :in_rows].reshape(1, -1), ((0, 15), (0, width - n_line * in_rows)))
    inner_block = jnp.concatenate([parts[:, :in_rows].reshape(-1, width), gain_rows], axis=0)
    gate_in = parts[:, in_rows : 2 * in_rows].reshape(-1, width)
    inner_rep, gate_in, toks = fence(repeated(inner_block, n_dp // 2), gate_in, toks)
    inner_own = to_chips(inner_rep)
    for s in steps[1:]:
        toks[s] = shift(toks[0], "fsdp", s)
    gate_rep = repeated(gate_in, n_dp // 2)
    small = by_chip([block[owned:].reshape(-1, owned)[: at.rows] for block in near])
    small_other = swap(small, "dp", 1)
    inner_own, toks, near, gate_rep, cotangent, small, small_other = fence(
        inner_own, toks, near, gate_rep, cotangent, small, small_other
    )

    inner_other = swap(inner_own, "dp", 1)
    small = by_device(small, small_other).transpose(1, 0, 2).reshape(-1, width)
    inner_own, inner_other, toks, cotangent, near, small = fence(inner_own, inner_other, toks, cotangent, near, small)
    rates = -jnp.exp(small[at.a_t].astype(F32))
    chunks = width // LANES
    rate2 = jnp.pad(
        (rates * (1.0 / LN2)).reshape(n_state, chunks, LANES), ((0, 0), (0, SUB - chunks), (0, 0))
    ).reshape(n_state * SUB, LANES)

    gate_own = to_chips(gate_rep)
    cots = {0: cotangent, 1: shift(cotangent, "fsdp", 1)}
    out_other = [swap(block, "dp", 1) for block in near[: len(near) // 2]]
    full_gain, normed, normed_kept, normed_sent, inner, conv_out, activ, low = project(
        info, n_line, n_dp, [toks[s] for s in range(n_line)], inner_own, inner_other, at, small, allowed
    )
    low, rate2, cots, near, out_other = fence(low, rate2, cots, near, out_other)

    part = low.astype(F32) + swap(low, "fsdp", 1).astype(F32)
    part, gate_own, near, out_other = fence(part, gate_own, near, out_other)
    part, got = last_line(part, 2)
    out_near, out_other = near, out_other + [swap(block, "dp", 1) for block in near[len(near) // 2 :]]
    part, got, cots, out_near, out_other = fence(part, got, cots, out_near, out_other)
    projected = part + got.astype(F32)

    gate_other = swap(gate_own, "dp", 1)
    for s in steps[1:]:
        cots[s] = shift(cots[0], "fsdp", s)
    projected = projected.reshape(-1, proj, LANES).transpose(0, 2, 1).reshape(slots, proj)
    rank_low = projected[:, :rank_w].astype(BF)
    bc = jnp.concatenate([projected[:, rank_w:], opens], axis=1)
    scanned, states = scan_forward(at, bc, rank_low, small, activ, valid, rate2, tb)
    scanned, gate_own, gate_other, cots[n_line - 1] = fence(scanned, gate_own, gate_other, cots[n_line - 1])

    branches, gate, out_nat, *gated = gate_block(
        info, n_line, n_dp, gate_own, gate_other, out_near, out_other, normed, scanned, activ, at, small
    )
    branches, gate, gated, out_nat, cots = fence(branches, gate, gated, out_nat, cots)

    branches[1] = shift(branches[1], "fsdp", 1)
    grad_scan, grad_gate, dout, gate_grad = gate_back(
        info, n_line, [cots[s] for s in range(n_line)], out_nat, gate, scanned, activ, at, small, valid, normed
    )
    branches, grad_scan, grad_gate, dout, gated, gate_grad = fence(
        branches, grad_scan, grad_gate, dout, gated, gate_grad
    )

    gate_sums = lax.all_to_all(gate_grad.reshape(n_dp, -1, width), "dp", 0, 0)
    for s in steps[1:]:
        branches[s] = shift(branches[s], "fsdp", s)
    low, grad_u, dt_w_grad, vectors, rate_grad = scan_backward(
        at, bc, rank_low, small, activ, valid, rate2, grad_scan, states, tb
    )
    low, branches, gated, dout, grad_gate = fence(low, branches, gated, dout, grad_gate)

    out_kept, out_sent = outer_product(*gated, dout)
    part = low.astype(F32) + swap(low, "fsdp", 1).astype(F32)
    part, out_kept, out_sent, grad_gate = fence(part, out_kept, out_sent, grad_gate)
    out_got = swap(out_sent, "dp", 1)
    gate_rows = jnp.sum(gate_sums.astype(F32), axis=0).astype(BF)
    out_kept, out_got, gate_rows = fence(out_kept, out_got, gate_rows)
    out_sum = chip_sum(out_kept, out_got)
    part, got = last_line(part, 2)
    part, got, out_sum.held, out_sum.sends, gate_rows = fence(part, got, out_sum.held, out_sum.sends, gate_rows)

    gate_got = to_line(gate_rows.reshape(n_line, in_rows, width))
    out_sum.first()
    grad_normed, inner_kept, inner_sent, small_kept, small_sent = conv_back(
        info, n_line, n_dp, part, got, grad_u, at, small, activ, conv_out, inner, allowed,
        dt_w_grad, rate_grad, vectors, grad_gate, (inner_own, inner_other), (gate_own, gate_other),
        normed_kept, normed_sent,
    )
    grad_normed, gate_got, inner_kept, inner_sent, small_kept, small_sent, branches = out_sum.fenced(
        grad_normed, gate_got, inner_kept, inner_sent, small_kept, small_sent, branches
    )

    grad_normed = to_line(grad_normed.reshape(n_line, held_slots, model))
    folded = owned % LANES == 0
    inner_got, small_got = swap(inner_sent, "dp", 1), swap(small_sent, "dp", 1)
    if folded:
        blocks = add_core(inner_kept, inner_got, small_kept, small_got)
    else:
        blocks = [sent_far(inner_kept, inner_got, u) for u in range(n_dp // 2)]
    blocks, small_kept, small_got, branches = out_sum.fenced(blocks, small_kept, small_got, branches)

    blocks = [swap(block, "dp", 2 * u) if u else block for u, block in enumerate(blocks)]
    out_sum.add()
    if folded:
        inner_sent, small_sum = sum_chips(place, blocks, n_line, in_rows, at, owned)
    else:
        rows = sum(block.astype(F32) for block in blocks).astype(BF).reshape(n_line, in_rows, width)
        inner_sent = [
            lax.dynamic_index_in_dim(rows, lax.rem(place + s, n_line), 0, keepdims=False) for s in range(n_line)
        ]
        small_sum = add_chips_near(small_kept + small_got.astype(F32))
        tail_g = small_sum[at.rest]
        small_sum = [small_sum[at.dt_w], small_sum[at.x_t], small_sum[at.a_t], tail_g[:taps]] + [
            tail_g[taps + i : taps + i + 1] for i in range(3)
        ]
    inner_sent, small_sum, branches = out_sum.fenced(inner_sent, small_sum, branches)

    inner_got = [shift(block, "fsdp", s) if s else block for s, block in enumerate(inner_sent)]
    out_sum.second()
    grad_normed = jnp.sum(grad_normed.astype(F32), axis=0)
    out_weight_grad = out_sum.total()
    dt_g, x_g, a_g, conv_g, *vectors = small_sum
    conv_b_g, dt_b_g, skip_g = [value[0] for value in vectors]
    small_out = [conv_g, conv_b_g, x_g.T, dt_g, dt_b_g, a_g.T, skip_g]
    own_f = own_tokens.astype(F32)
    output = (own_f + own_valid * sum(p.astype(F32) for p in branches)).astype(BF)
    own_scale = lax.rsqrt(jnp.mean(own_f * own_f, axis=1, keepdims=True) + EPS)
    unit = own_f * own_scale
    grad_unit = grad_normed * full_gain
    token_grad = own_cot.astype(F32) + own_scale * (
        grad_unit - unit * jnp.mean(grad_unit * unit, axis=1, keepdims=True)
    )
    inner_got, token_grad, output, out_weight_grad = fence(inner_got, token_grad, output, out_weight_grad)
    in_weight_grad, gain_grad = join_columns(place, inner_got, gate_got, in_weight, gain, n_dp)
    return output, token_grad, gain_grad, in_weight_grad, *small_out, out_weight_grad


def solution(mesh):
    both = ("dp", "fsdp")
    rows, cols, vec = P(both, None), P(None, both), P(both)
    return jax.shard_map(
        per_device,
        mesh=mesh,
        in_specs=(rows, P(), P(), vec, rows, cols, vec, rows, cols, vec, rows, vec, rows, rows),
        out_specs=(rows, rows, vec, rows, cols, vec, rows, cols, vec, rows, vec, rows),
        check_vma=False,
    )
```

```python
import functools

import jax
import jax.numpy as jnp
from jax import lax
from jax.experimental import pallas as pl
from jax.experimental.pallas import tpu as pltpu
from jax.sharding import PartitionSpec as P

BF, F32 = jnp.bfloat16, jnp.float32
LANES, SUB = 128, 8
LN2 = 0.6931471805599453
FAR = 1.0e5
EPS = 1e-5


def small_cost(flops):
    return pl.CostEstimate(flops=flops, bytes_accessed=1 << 16, transcendentals=0)


class Small:
    def __init__(self, rank, proj, state, taps):
        self.dt_w = slice(0, rank)
        self.x_t = slice(rank, rank + proj)
        self.a_t = slice(rank + proj, rank + proj + state)
        self.rest = slice(rank + proj + state, rank + proj + state + 16)
        self.taps, self.rows = taps, rank + proj + state + 16

    def fold(self, parts):
        rows = -(-self.rows // parts)
        return rows + -rows % 16

    def vector(self, ref, at):
        return ref[self.rest, :].astype(F32)[at : at + 1, :]


def contract_cols(left, right):
    return lax.dot_general(left, right, (((1,), (1,)), ((), ())), preferred_element_type=F32)


def scatter_lanes(ref, value, rows):
    for k in range(value.shape[1] // LANES):
        ref[pl.ds(k, rows, stride=SUB), :] = value[:, k * LANES : (k + 1) * LANES]


def gather_lanes(ref, width, rows):
    return jnp.concatenate(
        [ref[pl.ds(k, rows, stride=SUB), :] for k in range(width // LANES)], axis=1
    )


def softplus(v):
    return jnp.maximum(v, 0.0) + jnp.log1p(jnp.exp(-jnp.abs(v)))


def forward_kernel(at, bc, rank, small, act, valid, rate2, y_out, states, h_ref, dt_s, dtu_s, y_s):
    tb, width = act.shape
    n_state = rate2.shape[0] // SUB

    @pl.when(pl.program_id(0) == 0)
    def _():
        h_ref[...] = jnp.zeros_like(h_ref)
        if width < SUB * LANES:
            dt_s[...] = jnp.zeros_like(dt_s)
            dtu_s[...] = jnp.zeros_like(dtu_s)

    dt_b = at.vector(small, at.taps + 1)
    pre = jnp.dot(rank[...], small[at.dt_w, :], preferred_element_type=F32) + dt_b
    dt = softplus(pre) * valid[...]
    scatter_lanes(dt_s, dt, tb)
    scatter_lanes(dtu_s, dt * act[...].astype(F32), tb)
    rates = [rate2[n * SUB : (n + 1) * SUB, :] for n in range(n_state)]
    first = [h_ref[n * SUB : (n + 1) * SUB, :] for n in range(n_state)]
    for n in range(n_state):
        states[0, n, 0:SUB, :] = first[n]

    def token(t, h):
        at = pl.multiple_of(t * SUB, SUB)
        dt_t = dt_s[pl.ds(at, SUB), :] + bc[t, 2 * n_state]
        dtu_t = dtu_s[pl.ds(at, SUB), :]
        new, parts = [], [None, None]
        for n in range(n_state):
            hn = jnp.exp2(dt_t * rates[n]) * h[n] + dtu_t * bc[t, n]
            states[0, n, pl.ds(at + SUB, SUB), :] = hn
            term = hn * bc[t, n_state + n]
            parts[n % 2] = term if parts[n % 2] is None else parts[n % 2] + term
            new.append(hn)
        y_s[pl.ds(at, SUB), :] = parts[0] + parts[1]
        return tuple(new)

    last = lax.fori_loop(0, tb, token, tuple(first), unroll=8)
    for n in range(n_state):
        h_ref[n * SUB : (n + 1) * SUB, :] = last[n]
    y_out[...] = gather_lanes(y_s, width, tb)


def scan_forward(at, bc, rank, small, act, valid, rate2, tb):
    slots, width = act.shape
    n_state = rate2.shape[0] // SUB
    nb = slots // tb
    whole = lambda i: (0, 0)
    row = lambda i: (i, 0)
    return pl.pallas_call(
        functools.partial(forward_kernel, at),
        grid=(nb,),
        in_specs=[
            pl.BlockSpec((tb, bc.shape[1]), row, memory_space=pltpu.SMEM),
            pl.BlockSpec((tb, rank.shape[1]), row),
            pl.BlockSpec(small.shape, whole),
            pl.BlockSpec((tb, width), row),
            pl.BlockSpec((tb, 1), row),
            pl.BlockSpec(rate2.shape, whole),
        ],
        out_specs=[
            pl.BlockSpec((tb, width), row),
            pl.BlockSpec((1, n_state, (tb + 1) * SUB, LANES), lambda i: (i, 0, 0, 0)),
        ],
        out_shape=[
            jax.ShapeDtypeStruct((slots, width), F32),
            jax.ShapeDtypeStruct((nb, n_state, (tb + 1) * SUB, LANES), F32),
        ],
        scratch_shapes=[pltpu.VMEM(rate2.shape, F32)] + [pltpu.VMEM((tb * SUB, LANES), F32)] * 3,
        compiler_params=pltpu.CompilerParams(vmem_limit_bytes=61 << 20),
        cost_estimate=small_cost(1 << 20),
        name="scan_forward",
    )(bc, rank, small, act, valid, rate2)


def backward_kernel(
    at_small, bc, rank, small, act, valid, rate2, gs, states,
    packed_out, gu_out, dtw_out, vec_out, rate_grad,
    part_s, rate_out, g_ref, dt_s, dtu_s, gs_s, gdt_s, ab_s, both_s, sums,
):
    tb, width = act.shape
    n_state = rate2.shape[0] // SUB
    part = 4

    @pl.when(pl.program_id(0) == 0)
    def _():
        g_ref[...] = jnp.zeros_like(g_ref)
        rate_out[...] = jnp.zeros_like(rate_out)
        vec_out[...] = jnp.zeros_like(vec_out)
        dtw_out[...] = jnp.zeros_like(dtw_out)
        if width < SUB * LANES:
            for ref in (dt_s, dtu_s, gs_s):
                ref[...] = jnp.zeros_like(ref)

    u = act[...].astype(F32)
    ok = valid[...]
    dt_b, skip = at_small.vector(small, at_small.taps + 1), at_small.vector(small, at_small.taps + 2)
    pre = jnp.dot(rank[...], small[at_small.dt_w, :], preferred_element_type=F32) + dt_b
    dt = softplus(pre) * ok
    gs_v = gs[...]
    scatter_lanes(dt_s, dt, tb)
    scatter_lanes(dtu_s, dt * u, tb)
    scatter_lanes(gs_s, gs_v, tb)

    row = lax.broadcasted_iota(jnp.int32, (SUB, 2 * LANES), 0)
    lane = lax.broadcasted_iota(jnp.int32, (SUB, 2 * LANES), 1)
    pick = (lane // LANES == row).astype(F32).astype(BF)
    run = SUB
    span = run * SUB

    def add_lanes(group, i):
        rows = pl.ds(pl.multiple_of(i * span, span), span)
        pairs = jnp.concatenate([both_s[group % 2, j, rows, :] for j in range(part)], axis=0)
        sums[group, pl.ds(pl.multiple_of(i * SUB, SUB), SUB), :] = contract_cols(pick, pairs)

    for group in range(n_state // part):
        index = range(group * part, (group + 1) * part)
        rates = [rate2[n * SUB : (n + 1) * SUB, :] for n in index]

        def token(t, carry, after):
            g, acc = carry
            at = pl.multiple_of(t * SUB, SUB)
            dt_t, dtu_t, gs_t = [ref[pl.ds(at, SUB), :] for ref in (dt_s, dtu_s, gs_s)]
            dtd = dt_t + bc[t, 2 * n_state]
            new_g, new_acc, before, sources, reads = [], [], [], [], []
            gdt = ab = None
            for j, n in enumerate(index):
                lam = gs_t * bc[t, n_state + n] + g[j]
                sources.append(lam * dtu_t)
                reads.append(after[j] * gs_t)
                back = jnp.exp2(dtd * rates[j]) * lam
                before.append(states[0, n, pl.ds(at, SUB), :])
                thr = back * before[j]
                gdt = thr * rates[j] if gdt is None else gdt + thr * rates[j]
                ab = lam * bc[t, n] if ab is None else ab + lam * bc[t, n]
                new_g.append(back)
                new_acc.append(acc[j] + thr * dt_t)
            if group == 0:
                gdt_s[pl.ds(at, SUB), :] = gdt
                ab_s[pl.ds(at, SUB), :] = ab
            else:
                gdt_s[pl.ds(at, SUB), :] += gdt
                ab_s[pl.ds(at, SUB), :] += ab
            return (tuple(new_g), tuple(new_acc)), before, sources, reads

        def some_tokens(i, carry):
            i = tb // run - 1 - i
            if group:
                add_lanes(group - 1, i)
            late = pl.multiple_of((i + 1) * span, SUB)
            after = [states[0, n, pl.ds(late, SUB), :] for n in index]
            for k in range(run - 1, 0, -2):
                t = i * run + k
                carry, after, sources1, reads1 = token(t, carry, after)
                carry, after, sources0, reads0 = token(t - 1, carry, after)
                rows = pl.ds(pl.multiple_of((t - 1) * SUB, 2 * SUB), 2 * SUB)
                for j in range(part):
                    both_s[group % 2, j, rows, 0:LANES] = jnp.concatenate([sources0[j], sources1[j]], axis=0).astype(BF)
                    both_s[group % 2, j, rows, LANES:] = jnp.concatenate([reads0[j], reads1[j]], axis=0).astype(BF)
            return carry

        start = (
            tuple(g_ref[n * SUB : (n + 1) * SUB, :] for n in index),
            tuple(rate_out[n * SUB : (n + 1) * SUB, :] for n in index),
        )
        g, acc = lax.fori_loop(0, tb // run, some_tokens, start, unroll=tb // run)
        for j, n in enumerate(index):
            g_ref[n * SUB : (n + 1) * SUB, :] = g[j]
            rate_out[n * SUB : (n + 1) * SUB, :] = acc[j]
    for i in range(tb // run):
        add_lanes(n_state // part - 1, i)

    ab = gather_lanes(ab_s, width, tb)
    gdt = gather_lanes(gdt_s, width, tb)
    gu_out[...] = (gs_v * skip + dt * ab).astype(BF)
    grad_pre = ok * (gdt * LN2 + u * ab) * jax.nn.sigmoid(pre)
    vec_out[0:1, :] += jnp.sum(grad_pre, axis=0, keepdims=True)
    vec_out[1:2, :] += jnp.sum(gs_v * u, axis=0, keepdims=True)
    low = grad_pre.astype(BF)
    dtw_out[...] += lax.dot_general(rank[...], low, (((0,), (0,)), ((), ())), preferred_element_type=F32)
    rank_w = rank.shape[1]
    rows = pl.ds(pl.multiple_of((pl.num_programs(0) - 1 - pl.program_id(0)) * tb, tb), tb)
    part_s[rows, 0:rank_w] = contract_cols(low, small[at_small.dt_w, :]).astype(BF)

    take_row = lax.broadcasted_iota(jnp.int32, (2 * tb, tb // run * SUB), 0)
    take_lane = lax.broadcasted_iota(jnp.int32, (2 * tb, tb // run * SUB), 1)
    take = (take_lane == take_row % tb // run * SUB + take_row // tb).astype(F32).astype(BF)
    keep_row = lax.broadcasted_iota(jnp.int32, (2 * tb, part * span), 0)
    keep_lane = lax.broadcasted_iota(jnp.int32, (2 * tb, part * span), 1)
    keep = keep_lane // SUB % run == keep_row % run
    from_lane = lax.broadcasted_iota(jnp.int32, (part * span, LANES), 0)
    to_lane = lax.broadcasted_iota(jnp.int32, (part * span, LANES), 1)
    tail = jnp.zeros((2 * tb, LANES), F32)
    for group in range(n_state // part):
        chosen = jnp.dot(take, sums[group].astype(BF), preferred_element_type=F32)
        chosen = jnp.where(keep, chosen, 0.0).astype(BF)
        fold = (to_lane == group * part + from_lane // span).astype(F32).astype(BF)
        tail = tail + jnp.dot(chosen, fold, preferred_element_type=F32)
    part_s[rows, rank_w : rank_w + n_state] = tail[0:tb, 0:n_state].astype(BF)
    part_s[rows, rank_w + n_state :] = tail[tb:, 0:n_state].astype(BF)

    @pl.when(pl.program_id(0) == pl.num_programs(0) - 1)
    def _():
        proj = part_s.shape[1]
        across = lax.broadcasted_iota(jnp.int32, (proj, proj), 0) == lax.broadcasted_iota(jnp.int32, (proj, proj), 1)
        one = across.astype(F32).astype(BF)
        for b in range(part_s.shape[0] // LANES):
            packed_out[b * proj : (b + 1) * proj, :] = contract_cols(
                one, part_s[b * LANES : (b + 1) * LANES, :]
            ).astype(BF)
        for k in range(width // LANES):
            rows = pl.ds(k, n_state, stride=SUB)
            rate_grad[:, k * LANES : (k + 1) * LANES] = rate_out[rows, :] * rate2[rows, :] * LN2


def scan_backward(at, bc, rank, small, act, valid, rate2, gs, states, tb):
    slots, width = act.shape
    n_state = rate2.shape[0] // SUB
    nb = slots // tb
    whole = lambda i: (0, 0)
    row = lambda i: (nb - 1 - i, 0)
    rank_w = rank.shape[1]
    proj = rank_w + 2 * n_state
    return pl.pallas_call(
        functools.partial(backward_kernel, at),
        grid=(nb,),
        in_specs=[
            pl.BlockSpec((tb, bc.shape[1]), row, memory_space=pltpu.SMEM),
            pl.BlockSpec((tb, rank_w), row),
            pl.BlockSpec(small.shape, whole),
            pl.BlockSpec((tb, width), row),
            pl.BlockSpec((tb, 1), row),
            pl.BlockSpec(rate2.shape, whole),
            pl.BlockSpec((tb, width), row),
            pl.BlockSpec((1, n_state, (tb + 1) * SUB, LANES), lambda i: (nb - 1 - i, 0, 0, 0)),
        ],
        out_specs=[
            pl.BlockSpec((proj * slots // LANES, LANES), whole),
            pl.BlockSpec((tb, width), row),
            pl.BlockSpec((rank_w, width), whole),
            pl.BlockSpec((2, width), whole),
            pl.BlockSpec((n_state, width), whole),
        ],
        out_shape=[
            jax.ShapeDtypeStruct((proj * slots // LANES, LANES), BF),
            jax.ShapeDtypeStruct((slots, width), BF),
            jax.ShapeDtypeStruct((rank_w, width), F32),
            jax.ShapeDtypeStruct((2, width), F32),
            jax.ShapeDtypeStruct((n_state, width), F32),
        ],
        scratch_shapes=[pltpu.VMEM((slots, proj), BF)] + [pltpu.VMEM(rate2.shape, F32)] * 2
        + [pltpu.VMEM((tb * SUB, LANES), F32)] * 5
        + [pltpu.VMEM((2, 4, tb * SUB, 2 * LANES), BF), pltpu.VMEM((n_state // 4, tb, 4 * SUB * SUB), F32)],
        compiler_params=pltpu.CompilerParams(vmem_limit_bytes=61 << 20),
        cost_estimate=small_cost(1 << 20),
        name="scan_backward",
    )(bc, rank, small, act, valid, rate2, gs, states)


def silu_grad(value, sig):
    return sig * (1.0 + value * (1.0 - sig))


def place_blocks(ref, own, other, index):
    chips = own.shape[0]
    rows = ref.shape[0] // (2 * chips)
    core = lax.rem(index, 2)
    for q in range(chips):
        ref[pl.ds(pl.multiple_of((2 * q + core) * rows, rows), rows), :] = own[q, 0:rows, :]
        ref[pl.ds(pl.multiple_of((2 * q + 1 - core) * rows, rows), rows), :] = other[q, 0:rows, :]


def block_copies(ref, own, other, index, sems, first):
    chips = own.shape[0]
    rows = ref.shape[0] // (2 * chips)
    core = lax.rem(index, 2)
    found = []
    for q in range(chips):
        for blocks, d in ((own, 2 * q + core), (other, 2 * q + 1 - core)):
            at = pl.ds(pl.multiple_of(d * rows, rows), rows)
            found.append(
                pltpu.make_async_copy(blocks.at[q, pl.ds(0, rows)], ref.at[at], sems.at[first + len(found)])
            )
    return found


def read_row(ref, row, cols):
    tile = SUB if ref.dtype == F32 else 2 * SUB
    base = pl.multiple_of(row // tile * tile, tile)
    rows = ref[pl.ds(base, tile), cols].astype(F32)
    mine = lax.broadcasted_iota(jnp.int32, rows.shape, 0) == row - base
    return jnp.sum(jnp.where(mine, rows, 0.0), axis=0, keepdims=True)


def add_row(ref, row, value):
    base = pl.multiple_of(row // SUB * SUB, SUB)
    rows = ref[pl.ds(base, SUB), :]
    mine = lax.broadcasted_iota(jnp.int32, rows.shape, 0) == row - base
    ref[pl.ds(base, SUB), :] = rows + jnp.where(mine, value, 0.0)


def split_kernel(n_dp, in_w, gain, out):
    rows = in_w.shape[0]
    n_line, full, width = out.shape
    owned = width // n_dp
    top = jnp.broadcast_to(gain[...].astype(F32), (full - 2 * rows, rows)).astype(in_w.dtype)
    for to in range(n_line):
        for half in range(2):
            for d in range(n_dp):
                at = ((half * n_dp + d) * n_line + to) * owned
                out[to, half * rows : (half + 1) * rows, d * owned : (d + 1) * owned] = in_w[:, at : at + owned]
        out[to, 2 * rows :, :] = jnp.zeros((full - 2 * rows, width), in_w.dtype)
        out[to, 2 * rows :, 0:rows] = top


def split_columns(in_w, gain, n_dp, n_line):
    rows, both = in_w.shape
    width = both // (2 * n_line)
    if width // n_dp % LANES:
        blocks = in_w.reshape(rows, 2, n_dp, n_line, width // n_dp).transpose(3, 1, 0, 2, 4)
        top = jnp.broadcast_to(jnp.pad(gain, (0, width - rows)), (n_line, 16, width))
        return jnp.concatenate([blocks.reshape(n_line, 2 * rows, width), top], axis=1)
    vmem = pl.BlockSpec(memory_space=pltpu.VMEM)
    return pl.pallas_call(
        functools.partial(split_kernel, n_dp),
        in_specs=[vmem] * 2,
        out_specs=vmem,
        out_shape=jax.ShapeDtypeStruct((n_line, 2 * rows + 16, width), in_w.dtype),
        cost_estimate=small_cost(1 << 10),
        name="split_columns",
    )(in_w, gain[None])


def join_kernel(n_dp, place, *refs):
    *inner, gate, in_w, gain, out, gain_out = refs
    n_line, rows, width = gate.shape
    owned = width // n_dp
    total = jnp.zeros((rows, LANES), F32)
    for s in range(n_line):
        for half in range(2):
            line = from_place(place[0], s, n_line) if half == 0 else s
            for d in range(n_dp):
                cols = slice(d * owned, (d + 1) * owned)
                block = (inner[s][:, cols] if half == 0 else gate[s, :, cols]).astype(F32)
                at = ((half * n_dp + d) * n_line + line) * owned
                at = pl.ds(pl.multiple_of(at, owned), owned) if half == 0 else slice(at, at + owned)
                out[:, at] = block
                term = block * in_w[:, at].astype(F32)
                for low in range(0, owned, LANES):
                    total = total + term[:, low : low + LANES]
    ones = jnp.ones((SUB, LANES), F32)
    sums = lax.dot_general(
        ones, total, (((1,), (1,)), ((), ())), precision=lax.Precision.HIGHEST, preferred_element_type=F32
    )
    gain_out[...] = sums[0:1, :] / gain[...].astype(F32)


def join_columns(place, inner, gate, in_w, gain, n_dp):
    rows, both = in_w.shape
    n_line, _, width = gate.shape
    if width // n_dp % LANES:
        blocks = jnp.stack([in_order(inner, "fsdp"), gate]).astype(F32).reshape(2, n_line, rows, n_dp, -1)
        full = blocks.transpose(2, 0, 3, 1, 4).reshape(rows, both)
        return full, jnp.sum(full * in_w.astype(F32), axis=1) / gain.astype(F32)
    vmem = pl.BlockSpec(memory_space=pltpu.VMEM)
    full, gain_grad = pl.pallas_call(
        functools.partial(join_kernel, n_dp),
        in_specs=[pl.BlockSpec(memory_space=pltpu.SMEM)] + [vmem] * (n_line + 3),
        out_specs=[vmem] * 2,
        out_shape=[jax.ShapeDtypeStruct((rows, both), F32), jax.ShapeDtypeStruct((1, rows), F32)],
        cost_estimate=small_cost(1 << 10),
        name="join_columns",
    )(place[None], *inner, gate, in_w, gain[None])
    return full, gain_grad[0]


def column_block(width, slots):
    return 256 if width % 256 == 0 and slots <= 1024 else LANES


def from_place(place, steps, n_line):
    return lax.rem(place - steps + n_line, n_line)


def outer(lefts, right, outs):
    rows = min(256, lefts[0].shape[1])

    @pl.loop(0, lefts[0].shape[1] // rows)
    def _(r):
        at = pl.ds(pl.multiple_of(r * rows, rows), rows)
        for left, out in zip(lefts, outs):
            found = lax.dot_general(left[:, at], right[...], (((0,), (0,)), ((), ())), preferred_element_type=F32)
            out[at, :] = found.astype(out.dtype)


def outer_kernel(kept, sent, right, kept_out, sent_out):
    outer((kept, sent), right, (kept_out, sent_out))


def outer_product(kept, sent, right):
    shape = (kept.shape[1], right.shape[1])
    vmem = pl.BlockSpec(memory_space=pltpu.VMEM)
    return pl.pallas_call(
        outer_kernel,
        in_specs=[vmem] * 3,
        out_specs=[vmem] * 2,
        out_shape=[jax.ShapeDtypeStruct(shape, BF)] * 2,
        compiler_params=pltpu.CompilerParams(vmem_limit_bytes=61 << 20),
        cost_estimate=small_cost(1 << 20),
        name="outer_product",
    )(kept, sent, right)


def to_shifts(source, outs, place):
    rows = outs[0].shape[0]
    for s, out in enumerate(outs):
        at = pl.multiple_of(lax.rem(place + s, len(outs)) * rows, rows)
        out[...] = source[pl.ds(at, rows), :]


def split_cores(ref, kept, sent, index, n_dp):
    size = ref.shape[1] // n_dp
    core = lax.rem(index, 2)
    for q in range(kept.shape[1] // size):
        cols = slice(q * size, (q + 1) * size)
        kept[:, cols] = ref[:, pl.ds(pl.multiple_of((2 * q + core) * size, size), size)]
        sent[:, cols] = ref[:, pl.ds(pl.multiple_of((2 * q + 1 - core) * size, size), size)]


def project_kernel(n_line, n_dp, at, info, *refs):
    toks, refs = refs[:n_line], refs[n_line:]
    own, other, small, allowed, gain, normed, kept, sent, inner, conv_out, activ, part, w_nat, inner_s, ext = refs
    held, model = toks[0].shape
    slots = held * n_line
    width = w_nat.shape[1]
    taps = at.taps
    rim = taps - 1
    rows_dp = model // n_dp
    core = lax.rem(info[0], 2)
    for q in range(n_dp // 2):
        for blocks, d in ((own, 2 * q + core), (other, 2 * q + 1 - core)):
            found = blocks[q, rows_dp:, 0:rows_dp].astype(F32)[0:1, :]
            gain[:, pl.ds(pl.multiple_of(d * rows_dp, rows_dp), rows_dp)] = found
    step = 32
    for s, tok in enumerate(toks):
        base = from_place(info[1], s, n_line) * held

        @pl.loop(0, held // step)
        def _(i):
            x = tok[pl.ds(pl.multiple_of(i * step, step), step), :].astype(F32)
            scale = lax.rsqrt(jnp.mean(x * x, axis=1, keepdims=True) + EPS)
            normed[pl.ds(pl.multiple_of(base + i * step, step), step), :] = (x * scale * gain[...]).astype(BF)

    split_cores(normed, kept, sent, info[0], n_dp)
    place_blocks(w_nat, own, other, info[0])
    cb = column_block(width, slots)

    @pl.loop(0, width // cb)
    def _(c):
        cols = pl.ds(pl.multiple_of(c * cb, cb), cb)
        inner_s[...] = jnp.dot(normed[...], w_nat[:, cols], preferred_element_type=F32)
        inner[:, cols] = inner_s[...].astype(BF)
        vectors = small[at.rest, cols].astype(F32)
        for f in range(n_line):
            rows = slice(f * held, (f + 1) * held)
            ext[SUB : SUB + held, :] = inner_s[rows, :]
            for k in range(1, rim + 1):
                if f == 0:
                    ext[SUB - k : SUB - k + 1, :] = jnp.zeros((1, cb), F32)
                else:
                    ext[SUB - k : SUB - k + 1, :] = read_row(inner_s, (f - 1) * held + info[1 + f] - k, slice(None))
            total = vectors[taps : taps + 1, :]
            for lag in range(taps):
                tapped = ext[SUB - lag : SUB - lag + held, :]
                total = total + vectors[rim - lag : rim - lag + 1, :] * tapped * allowed[rows, lag : lag + 1]
            conv_out[rows, cols] = total.astype(BF)
            activ[rows, cols] = (total * jax.nn.sigmoid(total)).astype(BF)

    proj = part.shape[0] * LANES // slots
    for b in range(slots // LANES):
        found = contract_cols(small[at.x_t, :], activ[b * LANES : (b + 1) * LANES, :])
        part[b * proj : (b + 1) * proj, :] = found.astype(BF)


def project(info, n_line, n_dp, toks, own, other, at, small, allowed):
    held, model = toks[0].shape
    slots = held * n_line
    width, proj = small.shape[1], at.x_t.stop - at.x_t.start
    vmem = pl.BlockSpec(memory_space=pltpu.VMEM)
    shapes = [
        ((1, model), F32), ((slots, model), BF), ((slots, model // 2), BF), ((slots, model // 2), BF),
        ((slots, width), BF), ((slots, width), BF), ((slots, width), BF), ((proj * slots // LANES, LANES), BF),
    ]
    return pl.pallas_call(
        functools.partial(project_kernel, n_line, n_dp, at),
        in_specs=[pl.BlockSpec(memory_space=pltpu.SMEM)] + [vmem] * (4 + len(toks)),
        out_specs=[vmem] * len(shapes),
        out_shape=[jax.ShapeDtypeStruct(s, t) for s, t in shapes],
        scratch_shapes=[
            pltpu.VMEM((model, width), BF),
            pltpu.VMEM((slots, column_block(width, slots)), F32),
            pltpu.VMEM((SUB + slots // n_line, column_block(width, slots)), F32),
        ],
        compiler_params=pltpu.CompilerParams(vmem_limit_bytes=61 << 20),
        cost_estimate=small_cost(1 << 20),
        name="project",
    )(info, *toks, own, other, small, allowed)


def gate_kernel(n_line, n_dp, at, info, own, other, normed, y, act, small, *refs):
    out_own, out_other, refs = refs[: n_dp // 2], refs[n_dp // 2 : n_dp], refs[n_dp:]
    branches, refs = refs[:n_line], refs[n_line:]
    gate, gated, o_nat, *halves, branch, w_nat = refs
    slots, width = y.shape
    model = normed.shape[1]
    place_blocks(w_nat, own, other, info[0])
    rows = width // n_dp
    core, chip = lax.rem(info[0], 2), lax.div(info[0], 2)
    for u in range(n_dp // 2):
        first = 2 * jnp.bitwise_xor(chip, u)
        o_nat[pl.ds(pl.multiple_of((first + core) * rows, rows), rows), :] = out_own[u][0:rows, :]
        o_nat[pl.ds(pl.multiple_of((first + 1 - core) * rows, rows), rows), :] = out_other[u][0:rows, :]
    cb = column_block(width, slots)

    @pl.loop(0, width // cb)
    def _(c):
        cols = pl.ds(pl.multiple_of(c * cb, cb), cb)
        value = jnp.dot(normed[...], w_nat[:, cols], preferred_element_type=F32)
        gate[:, cols] = value
        skip = small[at.rest, cols].astype(F32)[at.taps + 2 : at.taps + 3, :]
        scan_out = y[:, cols] + skip * act[:, cols].astype(F32)
        gated[:, cols] = (scan_out * value * jax.nn.sigmoid(value)).astype(BF)

    mb = column_block(model, slots)

    @pl.loop(0, model // mb)
    def _(c):
        cols = pl.ds(pl.multiple_of(c * mb, mb), mb)
        branch[:, cols] = jnp.dot(gated[...], o_nat[:, cols], preferred_element_type=F32).astype(BF)

    to_shifts(branch, branches, info[1])
    if halves:
        split_cores(gated, *halves, info[0], n_dp)


def gate_block(info, n_line, n_dp, own, other, out_own, out_other, normed, y, act, at, small):
    slots, width = y.shape
    model = normed.shape[1]
    vmem = pl.BlockSpec(memory_space=pltpu.VMEM)
    shapes = [((slots // n_line, model), BF)] * n_line
    shapes += [((slots, width), F32), ((slots, width), BF), ((width, model), BF)]
    if width // n_dp % LANES == 0:
        shapes += [((slots, width // 2), BF)] * 2
    outs = pl.pallas_call(
        functools.partial(gate_kernel, n_line, n_dp, at),
        in_specs=[pl.BlockSpec(memory_space=pltpu.SMEM)] + [vmem] * (6 + n_dp),
        out_specs=[vmem] * len(shapes),
        out_shape=[jax.ShapeDtypeStruct(s, t) for s, t in shapes],
        scratch_shapes=[pltpu.VMEM((slots, model), BF), pltpu.VMEM((model, width), BF)],
        compiler_params=pltpu.CompilerParams(vmem_limit_bytes=61 << 20),
        cost_estimate=small_cost(1 << 20),
        name="gate_block",
    )(info, own, other, normed, y, act, small, *out_own, *out_other)
    branches, (gate, gated, o_nat), halves = list(outs[:n_line]), outs[n_line : n_line + 3], outs[n_line + 3 :]
    return branches, gate, o_nat, *(halves or cores(gated, 1))


def gate_back_kernel(n_line, at, info, *refs):
    cots, refs = refs[:n_line], refs[n_line:]
    o_nat, gate, y, act, small, valid, normed, gs, grad_gate, dout, product = refs
    slots, width = y.shape
    held, model = cots[0].shape
    for s, cot in enumerate(cots):
        rows = pl.ds(pl.multiple_of(from_place(info[1], s, n_line) * held, held), held)
        dout[rows, :] = (cot[...].astype(F32) * valid[rows, :]).astype(BF)

    cb = column_block(width, slots)

    @pl.loop(0, width // cb)
    def _(c):
        cols = pl.ds(pl.multiple_of(c * cb, cb), cb)
        grad = lax.dot_general(dout[...], o_nat[cols, :], (((1,), (1,)), ((), ())), preferred_element_type=F32)
        value = gate[:, cols]
        sig = jax.nn.sigmoid(value)
        skip = small[at.rest, cols].astype(F32)[at.taps + 2 : at.taps + 3, :]
        scan_out = y[:, cols] + skip * act[:, cols].astype(F32)
        gs[:, cols] = grad * value * sig
        grad_gate[:, cols] = (grad * scan_out * silu_grad(value, sig)).astype(BF)

    outer((normed,), grad_gate, (product,))


def gate_back(info, n_line, cots, o_nat, gate, y, act, at, small, valid, normed):
    slots, width = y.shape
    model = o_nat.shape[1]
    vmem = pl.BlockSpec(memory_space=pltpu.VMEM)
    shapes = [((slots, width), F32), ((slots, width), BF), ((slots, model), BF)]
    shapes += [((model, width), BF)]
    return pl.pallas_call(
        functools.partial(gate_back_kernel, n_line, at),
        in_specs=[pl.BlockSpec(memory_space=pltpu.SMEM)] + [vmem] * (7 + len(cots)),
        out_specs=[vmem] * len(shapes),
        out_shape=[jax.ShapeDtypeStruct(s, t) for s, t in shapes],
        compiler_params=pltpu.CompilerParams(vmem_limit_bytes=61 << 20),
        cost_estimate=small_cost(1 << 20),
        name="gate_back",
    )(info, *cots, o_nat, gate, y, act, small, valid, normed)


def combined(slots, owned):
    return together(slots) and owned % LANES == 0


def together(slots):
    return slots <= 1024


def conv_back_kernel(n_line, n_dp, at, info, gp_part, gp_got, gu, small, act, conv_out, inner, allowed, dtw, rate_grad, scan_vec,
                     grad_gate, *refs):
    slots, width = gu.shape
    inner_own, inner_other, gate_own, gate_other, *refs = refs
    halves_far, refs = (refs[:2], refs[2:]) if together(slots) else ((), refs)
    normed_far, *refs = refs
    products_far, refs = (refs[:2], refs[2:]) if together(slots) else ((), refs)
    gi_low, refs = (None, refs) if together(slots) else (refs[0], refs[1:])
    kept, sent, x_grad, vec, ext, gi, tail, grad_normed, column, gp, arrived, left, w_nat, gate_nat, *refs = refs
    below = combined(slots, width // n_dp)
    halves = ()
    copies = block_copies(w_nat, inner_own, inner_other, info[0], arrived, 0)
    copies += block_copies(gate_nat, gate_own, gate_other, info[0], arrived, n_dp)
    if together(slots):
        gi_low, *refs = refs
        halves, products = refs[:2], refs[2:]
        for i, (src, dst) in enumerate(zip(halves_far, halves)):
            copies.append(pltpu.make_async_copy(src, dst, arrived.at[2 * n_dp + i]))
    for copy in copies:
        copy.start()
    leaving = []

    def leave(src, dst):
        copy = pltpu.make_async_copy(src, dst, left.at[len(leaving)])
        copy.start()
        leaving.append(copy)

    gp[...] = (gp_part[...] + gp_got[...].astype(F32)).astype(BF)
    held = slots // n_line
    taps = at.taps
    rim = taps - 1
    cb = column_block(width, slots)
    proj = x_grad.shape[0]
    x_grad[...] = sum(
        jnp.dot(gp[b * proj : (b + 1) * proj, :], act[b * LANES : (b + 1) * LANES, :], preferred_element_type=F32)
        for b in range(slots // LANES)
    )
    vec[...] = jnp.zeros_like(vec)
    for lag in range(taps):
        tail[lag, held : held + SUB, :] = jnp.zeros((SUB, cb), F32)

    @pl.loop(0, width // cb)
    def _(c):
        cols = pl.ds(pl.multiple_of(c * cb, cb), cb)
        vectors = small[at.rest, cols].astype(F32)
        for f in range(n_line - 1, -1, -1):
            rows = slice(f * held, (f + 1) * held)
            ext[SUB : SUB + held, :] = inner[rows, cols].astype(F32)
            for k in range(1, rim + 1):
                if f == 0:
                    ext[SUB - k : SUB - k + 1, :] = jnp.zeros((1, cb), F32)
                else:
                    ext[SUB - k : SUB - k + 1, :] = read_row(inner, (f - 1) * held + info[1 + f] - k, cols)
            back = [
                lax.dot_general(
                    gp[b * proj : (b + 1) * proj, :], small[at.x_t, cols], (((0,), (0,)), ((), ())),
                    preferred_element_type=F32,
                )
                for b in range(f * held // LANES, (f + 1) * held // LANES)
            ]
            grad = gu[rows, cols].astype(F32) + jnp.concatenate(back, axis=0)
            co = conv_out[rows, cols].astype(F32)
            grad = grad * silu_grad(co, jax.nn.sigmoid(co))
            vec[taps : taps + 1, cols] += jnp.sum(grad, axis=0, keepdims=True)
            for lag in range(taps):
                weighted = grad * allowed[rows, lag : lag + 1]
                vec[rim - lag : rim - lag + 1, cols] += jnp.sum(
                    weighted * ext[SUB - lag : SUB - lag + held, :], axis=0, keepdims=True
                )
                tail[lag, 0:held, :] = weighted * vectors[rim - lag : rim - lag + 1, :]
            total = tail[0, 0:held, :]
            for lag in range(1, taps):
                total = total + tail[lag, lag : lag + held, :]
            gi[rows, :] = total
            if f + 1 < n_line:
                for k in range(1, rim + 1):
                    add_row(gi, f * held + info[2 + f] - k, gi[slots + k : slots + k + 1, :])
            for k in range(1, rim + 1):
                row = tail[k, 0:1, :]
                for lag in range(k + 1, taps):
                    row = row + tail[lag, lag - k : lag - k + 1, :]
                gi[slots + k : slots + k + 1, :] = row
        gi_low[:, cols] = gi[0:slots, :].astype(BF)

    for copy in copies:
        copy.wait()
    model = w_nat.shape[0]
    mb = column_block(model, slots)

    @pl.loop(0, model // mb)
    def _(c):
        cols = pl.ds(pl.multiple_of(c * mb, mb), mb)
        found = contract_cols(gi_low[...], w_nat[cols, :]) + contract_cols(grad_gate[...], gate_nat[cols, :])
        grad_normed[:, cols] = found.astype(BF)

    leave(grad_normed, normed_far)
    if halves:
        step = model // 2 // 4
        for r in range(4):
            rows = slice(r * step, (r + 1) * step)
            for half, product, out in zip(halves, products, products_far):
                product[rows, :] = lax.dot_general(
                    half[:, rows], gi_low[...], (((0,), (0,)), ((), ())), preferred_element_type=F32
                ).astype(BF)
                leave(product.at[pl.ds(r * step, step)], out.at[pl.ds(r * step, step)])
    vec[taps + 1 : taps + 3, :] = scan_vec[...]
    owned = width // n_dp
    if kept.shape[0] == 1:
        kept[0, at.dt_w, :], kept[0, at.x_t, :], kept[0, at.a_t, :], kept[0, at.rest, :] = (
            dtw[...], x_grad[...], rate_grad[...], vec[...]
        )
        for copy in leaving:
            copy.wait()
        return
    core = lax.rem(info[0], 2)
    fold = kept.shape[1]
    for q in range(n_dp // 2):
        for ref, d in ((kept, 2 * q + core), (sent, 2 * q + 1 - core)):
            cols = pl.ds(pl.multiple_of(d * owned, owned), owned)
            for rows, source in ((at.dt_w, dtw), (at.x_t, x_grad), (at.a_t, rate_grad), (at.rest, vec)):
                column[rows, :] = source[:, cols]
            for b in range(width // owned):
                cols = slice(b * owned, (b + 1) * owned)
                value = column[b * fold : (b + 1) * fold, :].astype(ref.dtype)
                if ref is sent and below:
                    sent[q * fold : (q + 1) * fold, cols] = value
                else:
                    ref[q, :, cols] = value
    if below:
        leave(sent, products_far[1].at[pl.ds(model // 2, sent.shape[0])])
    for copy in leaving:
        copy.wait()


def conv_back(info, n_line, n_dp, gp_part, gp_got, gu, at, small, act, conv_out, inner, allowed, dtw, rate_grad, scan_vec, grad_gate,
              inner_blocks, gate_blocks, normed_k, normed_s):
    slots, width = gu.shape
    held, model = slots // n_line, 2 * normed_k.shape[1]
    cb = column_block(width, slots)
    owned = width // n_dp
    one, below = together(slots), combined(slots, owned)
    tiles = below
    vmem, away = pl.BlockSpec(memory_space=pltpu.VMEM), pl.BlockSpec(memory_space=pl.ANY)
    fold = at.fold(n_dp)
    shape = (n_dp // 2, fold, width) if tiles else (1, at.rows, width)
    later = [*inner_blocks, *gate_blocks] + ([normed_k, normed_s] if one else [])
    low, half = jax.ShapeDtypeStruct((slots, width), BF), jax.ShapeDtypeStruct((model // 2, width), BF)
    more = n_dp // 2 * fold if below else 0
    longer = jax.ShapeDtypeStruct((model // 2 + more, width), BF)
    outs = pl.pallas_call(
        functools.partial(conv_back_kernel, n_line, n_dp, at),
        in_specs=[pl.BlockSpec(memory_space=pltpu.SMEM)] + [vmem] * 12 + [away] * len(later),
        out_specs=[away] + ([away] * 2 if one else [vmem]) + [vmem] * (1 if below else 2),
        out_shape=[jax.ShapeDtypeStruct((slots, model), BF)]
        + ([half, longer] if one else [low])
        + [jax.ShapeDtypeStruct(shape, F32)]
        + ([] if below else [jax.ShapeDtypeStruct(shape if tiles else (SUB, LANES), BF if tiles else F32)]),
        scratch_shapes=([pltpu.VMEM((more, width), BF)] if below else [])
        + [
            pltpu.VMEM((at.x_t.stop - at.x_t.start, width), F32),
            pltpu.VMEM((16, width), F32),
            pltpu.VMEM((SUB + held, cb), F32),
            pltpu.VMEM((slots + SUB, cb), F32),
            pltpu.VMEM((at.taps, held + SUB, cb), F32),
            pltpu.VMEM((slots, model), BF),
            pltpu.VMEM((n_dp * fold, owned), F32),
            pltpu.VMEM(gp_got.shape, BF),
            pltpu.SemaphoreType.DMA((2 * n_dp + 2,)),
            pltpu.SemaphoreType.DMA((10,)),
        ]
        + [pltpu.VMEM((model, width), BF)] * 2
        + ([pltpu.VMEM((slots, width), BF)] + [pltpu.VMEM((slots, model // 2), BF)] * 2 if one else [])
        + ([pltpu.VMEM((model // 2, width), BF)] * 2 if one else []),
        compiler_params=pltpu.CompilerParams(vmem_limit_bytes=61 << 20),
        cost_estimate=small_cost(1 << 20),
        name="conv_back",
    )(info, gp_part, gp_got, gu, small, act, conv_out, inner, allowed, dtw, rate_grad, scan_vec, grad_gate, *later)
    grad_normed, *products, kept, sent = (*outs, None) if below else outs
    if not one:
        products = outer_product(normed_k, normed_s, products[0])
    if not tiles:
        kept, sent = [
            part.reshape(at.rows, n_dp // 2, owned).transpose(1, 0, 2) for part in cores(kept[0], 1)
        ]
    return grad_normed, *products, kept, sent if below else sent.astype(BF)


def swap(value, axis, mask):
    count = lax.axis_size(axis)
    return lax.ppermute(value, axis, [(i, i ^ mask) for i in range(count)])


def shift(value, axis, steps):
    count = lax.axis_size(axis)
    return lax.ppermute(value, axis, [(i, (i + steps) % count) for i in range(count)])


def chips_of(axis):
    return [list(range(core, lax.axis_size(axis), 2)) for core in range(2)]


def to_line(blocks):
    return lax.all_to_all(blocks, "fsdp", 0, 0)


def to_chips(blocks):
    return lax.all_to_all(blocks, "dp", 0, 0, axis_index_groups=chips_of("dp"))


def repeated(value, count):
    return jnp.broadcast_to(value[None], (count,) + value.shape)


def in_order(parts, axis):
    count, me = lax.axis_size(axis), lax.axis_index(axis)
    up = jnp.stack([parts[-k % count] for k in range(count)] * 2)
    return lax.dynamic_slice_in_dim(up, lax.rem(count - me, count), count, 0)


def by_chip(parts):
    chip, count = lax.div(lax.axis_index("dp"), 2), len(parts)
    bits = count.bit_length() - 1
    cube = jnp.stack(parts).reshape((2,) * bits + parts[0].shape)
    for place in range(bits):
        mine = lax.rem(chip >> (bits - 1 - place), 2) == 1
        cube = jnp.where(mine, jnp.flip(cube, place), cube)
    return cube.reshape((count,) + parts[0].shape)


def by_device(own, other):
    core = lax.rem(lax.axis_index("dp"), 2) == 1
    both = jnp.where(core, jnp.stack([other, own], axis=1), jnp.stack([own, other], axis=1))
    return lax.optimization_barrier(both.reshape((-1,) + own.shape[1:]))


def last_line(value, reach):
    while True:
        got = swap(value.astype(BF), "fsdp", reach)
        reach *= 2
        if reach >= lax.axis_size("fsdp"):
            return value, got
        value = value + got.astype(F32)


def fence(*values):
    flat, shape = jax.tree.flatten(values)
    return jax.tree.unflatten(shape, lax.optimization_barrier(tuple(flat)))


def cores(value, axis):
    cut = value.shape[:axis] + (lax.axis_size("dp") // 2, 2, -1) + value.shape[axis + 1 :]
    cube = value.reshape(cut)
    core = lax.rem(lax.axis_index("dp"), 2)
    found = [lax.dynamic_index_in_dim(cube, at, axis + 1, keepdims=False) for at in (core, 1 - core)]
    flat = value.shape[:axis] + (value.shape[axis] // 2,) + value.shape[axis + 1 :]
    return [part.reshape(flat) for part in found]


def add_core_kernel(chip, kept, got, small_kept, *outs):
    rows, fold = kept.shape[0] // len(outs), small_kept.shape[1]
    for u, out in enumerate(outs):
        q = jnp.bitwise_xor(chip[0], u)
        at = pl.ds(pl.multiple_of(q * rows, rows), rows)
        out[0:rows, :] = (kept[at, :].astype(F32) + got[at, :].astype(F32)).astype(BF)
        below = pl.ds(pl.multiple_of(kept.shape[0] + q * fold, fold), fold)
        out[rows:, :] = (small_kept[q] + got[below, :].astype(F32)).astype(BF)


def add_core(kept, got, small_kept):
    chips, width = lax.axis_size("dp") // 2, kept.shape[1]
    rows = kept.shape[0] // chips + small_kept.shape[1]
    vmem = pl.BlockSpec(memory_space=pltpu.VMEM)
    return pl.pallas_call(
        add_core_kernel,
        in_specs=[pl.BlockSpec(memory_space=pltpu.SMEM)] + [vmem] * 3,
        out_specs=[vmem] * chips,
        out_shape=[jax.ShapeDtypeStruct((rows, width), BF)] * chips,
        compiler_params=pltpu.CompilerParams(vmem_limit_bytes=61 << 20),
        cost_estimate=small_cost(1 << 10),
        name="add_core",
    )(lax.div(lax.axis_index("dp"), 2)[None], kept, got, small_kept)


def add_chips_near(blocks):
    count, chip = lax.axis_size("dp") // 2, lax.div(lax.axis_index("dp"), 2)
    total = lax.dynamic_index_in_dim(blocks, chip, 0, keepdims=False)
    for u in range(1, count):
        total = total + far(blocks, u).astype(F32)
    return total


def sum_chips_kernel(count, n_line, at, place, *refs):
    blocks, outs, (dt_g, x_g, a_g, conv_g, *vectors, column) = (
        refs[:count], refs[count : count + n_line], refs[count + n_line :]
    )
    rows = outs[0].shape[0]
    for s, out in enumerate(outs):
        mine = pl.ds(pl.multiple_of(lax.rem(place[0] + s, n_line) * rows, rows), rows)
        out[...] = sum(block[mine, :].astype(F32) for block in blocks).astype(BF)
    first, owned = rows * n_line, column.shape[1]
    small = sum(block[first:, :].astype(F32) for block in blocks)
    fold = small.shape[0]
    for b in range(small.shape[1] // owned):
        column[b * fold : (b + 1) * fold, :] = small[:, b * owned : (b + 1) * owned]
    dt_g[...], x_g[...], a_g[...] = column[at.dt_w, :], column[at.x_t, :], column[at.a_t, :]
    rest = column[at.rest, :]
    conv_g[...] = rest[: at.taps, :]
    for i, out in enumerate(vectors):
        out[...] = rest[at.taps + i : at.taps + i + 1, :]


def sum_chips(place, blocks, n_line, rows, at, owned):
    full, width = blocks[0].shape
    vmem = pl.BlockSpec(memory_space=pltpu.VMEM)
    small = [(part.stop - part.start, owned) for part in (at.dt_w, at.x_t, at.a_t)]
    small += [(at.taps, owned)] + [(1, owned)] * 3
    outs = pl.pallas_call(
        functools.partial(sum_chips_kernel, len(blocks), n_line, at),
        in_specs=[pl.BlockSpec(memory_space=pltpu.SMEM)] + [vmem] * len(blocks),
        out_specs=[vmem] * (n_line + len(small)),
        out_shape=[jax.ShapeDtypeStruct((rows, width), BF)] * n_line
        + [jax.ShapeDtypeStruct(shape, F32) for shape in small],
        scratch_shapes=[pltpu.VMEM(((full - n_line * rows) * (width // owned), owned), F32)],
        compiler_params=pltpu.CompilerParams(vmem_limit_bytes=61 << 20),
        cost_estimate=small_cost(1 << 10),
        name="sum_chips",
    )(place[None], *blocks)
    return list(outs[:n_line]), list(outs[n_line:])


def sent_far(kept, got, u):
    rows = kept.shape[0] // (lax.axis_size("dp") // 2)
    at = jnp.bitwise_xor(lax.div(lax.axis_index("dp"), 2), u) * rows
    return sum(lax.dynamic_slice_in_dim(part, at, rows, 0).astype(F32) for part in (kept, got)).astype(BF)


def far(blocks, u):
    block = lax.dynamic_index_in_dim(blocks, jnp.bitwise_xor(lax.div(lax.axis_index("dp"), 2), u), 0, keepdims=False)
    return swap(block.astype(BF), "dp", 2 * u)


def halves_kernel(chip, kept, got, first, second, *held):
    rows, half = held[0].shape
    outs = {
        (0, 0): held[0], (2, 0): held[1], (0, 1): held[2], (1, 1): held[3],
        (1, 0): first.at[0:rows], (3, 0): first.at[rows : 2 * rows],
        (2, 1): second.at[0:rows], (3, 1): second.at[rows : 2 * rows],
    }
    for (u, side), out in outs.items():
        at = pl.ds(pl.multiple_of(jnp.bitwise_xor(chip[0], u) * rows, rows), rows)
        cols = slice(side * half, (side + 1) * half)
        out[...] = (kept[at, cols].astype(F32) + got[at, cols].astype(F32)).astype(BF)


def chip_sum(kept, got):
    chips, (rows, width) = lax.axis_size("dp") // 2, kept.shape
    if chips != 4 or rows // chips % LANES:
        return ChipSum([sent_far(kept, got, u) for u in range(chips)])
    rows, half = rows // chips, width // 2
    vmem = pl.BlockSpec(memory_space=pltpu.VMEM)
    first, second, *held = pl.pallas_call(
        halves_kernel,
        in_specs=[pl.BlockSpec(memory_space=pltpu.SMEM)] + [vmem] * 2,
        out_specs=[vmem] * 6,
        out_shape=[jax.ShapeDtypeStruct((2 * rows, half), BF)] * 2 + [jax.ShapeDtypeStruct((rows, half), BF)] * 4,
        compiler_params=pltpu.CompilerParams(vmem_limit_bytes=61 << 20),
        cost_estimate=small_cost(1 << 10),
        name="chip_halves",
    )(lax.div(lax.axis_index("dp"), 2)[None], kept, got)
    return ChipSum(held, [first, second])


def total_kernel(left, right, left_got, right_got, out):
    half = left.shape[1]
    out[:, 0:half] = left[...] + left_got[...].astype(F32)
    out[:, half:] = right[...] + right_got[...].astype(F32)


class ChipSum:
    def __init__(self, held, sends=None):
        self.direct = sends is None
        self.held, self.sends, self.got = held, sends or held[1:], []

    def fenced(self, *others):
        (self.held, self.sends, self.got), *others = fence((self.held, self.sends, self.got), *others)
        return others

    def first(self):
        self.got = [swap(send, "dp", 2 * u) for u, send in enumerate(self.sends, 1)]
        self.sends = []

    def add(self):
        if self.direct:
            return
        rows = self.held[0].shape[0]
        own = [h.astype(F32) + got[:rows].astype(F32) for h, got in zip(self.held[::2], self.got)]
        self.sends = [(h.astype(F32) + got[rows:].astype(F32)).astype(BF) for h, got in zip(self.held[1::2], self.got)]
        self.held, self.got = own, []

    def second(self):
        if not self.direct:
            self.got = [swap(send, "dp", 2 * u) for u, send in zip((2, 1), self.sends)]

    def total(self):
        if self.direct:
            return sum(part.astype(F32) for part in (self.held[0], *self.got))
        rows, half = self.held[0].shape
        vmem = pl.BlockSpec(memory_space=pltpu.VMEM)
        return pl.pallas_call(
            total_kernel,
            in_specs=[vmem] * 4,
            out_specs=vmem,
            out_shape=jax.ShapeDtypeStruct((rows, 2 * half), F32),
            compiler_params=pltpu.CompilerParams(vmem_limit_bytes=61 << 20),
            cost_estimate=small_cost(1 << 10),
            name="chip_total",
        )(*self.held, *self.got)


def per_device(
    tokens, counts, lengths, gain, in_weight, conv_weight, conv_bias, x_weight,
    dt_weight, dt_bias, a_log, skip, out_weight, cotangent,
):
    n_dp, n_line = lax.axis_size("dp"), lax.axis_size("fsdp")
    group, place = lax.axis_index("dp"), lax.axis_index("fsdp")
    held_slots, model = tokens.shape
    slots = held_slots * n_line
    owned = skip.shape[0]
    width = owned * n_dp
    in_rows = in_weight.shape[0]
    taps, rank_w, n_state = conv_weight.shape[0], dt_weight.shape[0], a_log.shape[1]
    proj = x_weight.shape[1]
    tb = 64 if slots % 64 == 0 else slots

    count_row = lax.dynamic_index_in_dim(counts, group, 0, keepdims=False)
    length_row = lax.dynamic_index_in_dim(lengths, group, 0, keepdims=False)
    info = jnp.concatenate([jnp.stack([group, place]).astype(jnp.int32), count_row])
    offsets = jnp.cumsum(count_row) - count_row
    within = lax.broadcasted_iota(jnp.int32, (n_line, held_slots), 1)
    present = within < count_row[:, None]
    position = offsets[:, None] + within
    second, third = length_row[0], length_row[0] + length_row[1]
    begin = jnp.where(position >= third, third, jnp.where(position >= second, second, 0))
    marks = jnp.stack(
        [position - lag >= begin for lag in range(taps)] + [present, present & (position == begin)]
    ).astype(F32).reshape(taps + 2, slots).T
    allowed, valid, opens = marks[:, :taps], marks[:, taps : taps + 1], marks[:, taps + 1 :] * FAR

    own_tokens, own_cot = tokens, cotangent
    steps = range(1, n_line)
    chips = range(1, n_dp // 2)
    at = Small(rank_w, proj, n_state, taps)

    parts = split_columns(in_weight, gain, n_dp, n_line)
    rest = jnp.concatenate([conv_weight, conv_bias[None], dt_bias[None], skip[None]], axis=0)
    rest = jnp.pad(rest, ((0, 16 - rest.shape[0]), (0, 0)))
    small = jnp.concatenate([dt_weight, x_weight.T, a_log.T, rest], axis=0)
    small_rows = -(-at.rows * owned // model)
    small_rows += -small_rows % 16
    small = jnp.pad(small, ((0, small_rows * model // owned - at.rows), (0, 0))).reshape(small_rows, model)
    packed = jnp.concatenate([out_weight, small], axis=0)
    parts, tokens = fence(parts, tokens)
    parts = to_line(parts)
    toks = {0: tokens, 1: shift(tokens, "fsdp", 1)}
    near = [packed] + [swap(packed, "dp", 2 * u) for u in chips]
    own_valid = lax.dynamic_slice_in_dim(valid, place * held_slots, held_slots, 0)
    parts, toks, near, info, allowed, valid, opens, own_valid = fence(
        parts, toks, near, info, allowed, valid, opens, own_valid
    )

    gain_rows = jnp.pad(parts[:, 2 * in_rows, :in_rows].reshape(1, -1), ((0, 15), (0, width - n_line * in_rows)))
    inner_block = jnp.concatenate([parts[:, :in_rows].reshape(-1, width), gain_rows], axis=0)
    gate_in = parts[:, in_rows : 2 * in_rows].reshape(-1, width)
    inner_rep, gate_in, toks = fence(repeated(inner_block, n_dp // 2), gate_in, toks)
    inner_own = to_chips(inner_rep)
    for s in steps[1:]:
        toks[s] = shift(toks[0], "fsdp", s)
    gate_rep = repeated(gate_in, n_dp // 2)
    small = by_chip([block[owned:].reshape(-1, owned)[: at.rows] for block in near])
    small_other = swap(small, "dp", 1)
    inner_own, toks, near, gate_rep, cotangent, small, small_other = fence(
        inner_own, toks, near, gate_rep, cotangent, small, small_other
    )

    inner_other = swap(inner_own, "dp", 1)
    small = by_device(small, small_other).transpose(1, 0, 2).reshape(-1, width)
    inner_own, inner_other, toks, cotangent, near, small = fence(inner_own, inner_other, toks, cotangent, near, small)
    rates = -jnp.exp(small[at.a_t].astype(F32))
    chunks = width // LANES
    rate2 = jnp.pad(
        (rates * (1.0 / LN2)).reshape(n_state, chunks, LANES), ((0, 0), (0, SUB - chunks), (0, 0))
    ).reshape(n_state * SUB, LANES)

    gate_own = to_chips(gate_rep)
    cots = {0: cotangent, 1: shift(cotangent, "fsdp", 1)}
    out_other = [swap(block, "dp", 1) for block in near[: len(near) // 2]]
    full_gain, normed, normed_kept, normed_sent, inner, conv_out, activ, low = project(
        info, n_line, n_dp, [toks[s] for s in range(n_line)], inner_own, inner_other, at, small, allowed
    )
    low, rate2, cots, near, out_other = fence(low, rate2, cots, near, out_other)

    part = low.astype(F32) + swap(low, "fsdp", 1).astype(F32)
    part, gate_own, near, out_other = fence(part, gate_own, near, out_other)
    part, got = last_line(part, 2)
    out_near, out_other = near, out_other + [swap(block, "dp", 1) for block in near[len(near) // 2 :]]
    part, got, cots, out_near, out_other = fence(part, got, cots, out_near, out_other)
    projected = part + got.astype(F32)

    gate_other = swap(gate_own, "dp", 1)
    for s in steps[1:]:
        cots[s] = shift(cots[0], "fsdp", s)
    projected = projected.reshape(-1, proj, LANES).transpose(0, 2, 1).reshape(slots, proj)
    rank_low = projected[:, :rank_w].astype(BF)
    bc = jnp.concatenate([projected[:, rank_w:], opens], axis=1)
    scanned, states = scan_forward(at, bc, rank_low, small, activ, valid, rate2, tb)
    scanned, gate_own, gate_other, cots[n_line - 1] = fence(scanned, gate_own, gate_other, cots[n_line - 1])

    branches, gate, out_nat, *gated = gate_block(
        info, n_line, n_dp, gate_own, gate_other, out_near, out_other, normed, scanned, activ, at, small
    )
    branches, gate, gated, out_nat, cots = fence(branches, gate, gated, out_nat, cots)

    branches[1] = shift(branches[1], "fsdp", 1)
    grad_scan, grad_gate, dout, gate_grad = gate_back(
        info, n_line, [cots[s] for s in range(n_line)], out_nat, gate, scanned, activ, at, small, valid, normed
    )
    branches, grad_scan, grad_gate, dout, gated, gate_grad = fence(
        branches, grad_scan, grad_gate, dout, gated, gate_grad
    )

    gate_sums = lax.all_to_all(gate_grad.reshape(n_dp, -1, width), "dp", 0, 0)
    for s in steps[1:]:
        branches[s] = shift(branches[s], "fsdp", s)
    low, grad_u, dt_w_grad, vectors, rate_grad = scan_backward(
        at, bc, rank_low, small, activ, valid, rate2, grad_scan, states, tb
    )
    low, branches, gated, dout, grad_gate = fence(low, branches, gated, dout, grad_gate)

    out_kept, out_sent = outer_product(*gated, dout)
    part = low.astype(F32) + swap(low, "fsdp", 1).astype(F32)
    part, out_kept, out_sent, grad_gate = fence(part, out_kept, out_sent, grad_gate)
    out_got = swap(out_sent, "dp", 1)
    gate_rows = jnp.sum(gate_sums.astype(F32), axis=0).astype(BF)
    out_kept, out_got, gate_rows = fence(out_kept, out_got, gate_rows)
    out_sum = chip_sum(out_kept, out_got)
    part, got = last_line(part, 2)
    part, got, out_sum.held, out_sum.sends, gate_rows = fence(part, got, out_sum.held, out_sum.sends, gate_rows)

    gate_got = to_line(gate_rows.reshape(n_line, in_rows, width))
    out_sum.first()
    grad_normed, inner_kept, inner_sent, small_kept, small_sent = conv_back(
        info, n_line, n_dp, part, got, grad_u, at, small, activ, conv_out, inner, allowed,
        dt_w_grad, rate_grad, vectors, grad_gate, (inner_own, inner_other), (gate_own, gate_other),
        normed_kept, normed_sent,
    )
    grad_normed, gate_got, inner_kept, inner_sent, small_kept, small_sent, branches = out_sum.fenced(
        grad_normed, gate_got, inner_kept, inner_sent, small_kept, small_sent, branches
    )

    grad_normed = to_line(grad_normed.reshape(n_line, held_slots, model))
    folded = combined(slots, owned)
    out_sum.add()
    out_sum.second()
    inner_got, small_got = swap(inner_sent, "dp", 1), None
    if folded:
        blocks = add_core(inner_kept, inner_got, small_kept)
    else:
        small_got = swap(small_sent, "dp", 1)
        blocks = [sent_far(inner_kept, inner_got, u) for u in range(n_dp // 2)]
    blocks, small_kept, small_got, branches = out_sum.fenced(blocks, small_kept, small_got, branches)

    blocks = [swap(block, "dp", 2 * u) if u else block for u, block in enumerate(blocks)]
    out_weight_grad = out_sum.total()
    if folded:
        inner_sent, small_sum = sum_chips(place, blocks, n_line, in_rows, at, owned)
    else:
        rows = sum(block.astype(F32) for block in blocks).astype(BF).reshape(n_line, in_rows, width)
        inner_sent = [
            lax.dynamic_index_in_dim(rows, lax.rem(place + s, n_line), 0, keepdims=False) for s in range(n_line)
        ]
        small_sum = add_chips_near(small_kept + small_got.astype(F32))
        tail_g = small_sum[at.rest]
        small_sum = [small_sum[at.dt_w], small_sum[at.x_t], small_sum[at.a_t], tail_g[:taps]] + [
            tail_g[taps + i : taps + i + 1] for i in range(3)
        ]
    inner_sent, small_sum, branches, out_weight_grad = fence(inner_sent, small_sum, branches, out_weight_grad)

    inner_got = [shift(block, "fsdp", s) if s else block for s, block in enumerate(inner_sent)]
    grad_normed = jnp.sum(grad_normed.astype(F32), axis=0)
    dt_g, x_g, a_g, conv_g, *vectors = small_sum
    conv_b_g, dt_b_g, skip_g = [value[0] for value in vectors]
    small_out = [conv_g, conv_b_g, x_g.T, dt_g, dt_b_g, a_g.T, skip_g]
    own_f = own_tokens.astype(F32)
    output = (own_f + own_valid * sum(p.astype(F32) for p in branches)).astype(BF)
    own_scale = lax.rsqrt(jnp.mean(own_f * own_f, axis=1, keepdims=True) + EPS)
    unit = own_f * own_scale
    grad_unit = grad_normed * full_gain
    token_grad = own_cot.astype(F32) + own_scale * (
        grad_unit - unit * jnp.mean(grad_unit * unit, axis=1, keepdims=True)
    )
    inner_got, token_grad, output = fence(inner_got, token_grad, output)
    in_weight_grad, gain_grad = join_columns(place, inner_got, gate_got, in_weight, gain, n_dp)
    return output, token_grad, gain_grad, in_weight_grad, *small_out, out_weight_grad


def solution(mesh):
    both = ("dp", "fsdp")
    rows, cols, vec = P(both, None), P(None, both), P(both)
    return jax.shard_map(
        per_device,
        mesh=mesh,
        in_specs=(rows, P(), P(), vec, rows, cols, vec, rows, cols, vec, rows, vec, rows, rows),
        out_specs=(rows, rows, vec, rows, cols, vec, rows, cols, vec, rows, vec, rows),
        check_vma=False,
    )
```
